128 devices in a mesh: dp: 16 (over y_hi, x, core), tensor: 8 (over z, y_lo).
Axes of the slice: x: 4, y: 4 (y_hi: 2, y_lo: 2; y = y_hi * 2 + y_lo), z: 4, core: 2. Of those that a mesh axis runs over, the one named last changes fastest.
Arguments:
- kv_pool: bfloat16 [8192, 8, 16, 256], P('dp', 'tensor'), may hold values from -6 to 6
- page_loc: int32 [8, 128, 64], replicated, may hold values from 0 to 8191, as said below
- lengths: int32 [128], replicated, may hold values from 256 to 1024
- placement: int32 [128], replicated, may hold values from 0 to 127, as said below
- queries: bfloat16 [2, 128, 64, 128], P(None, 'dp', 'tensor'), may hold values from -27 to 27
- new_kv: bfloat16 [2, 128, 8, 256], P(None, 'dp', 'tensor'), may hold values from -6 to 6
- resid_in: bfloat16 [2, 128, 8192], P(None, None, 'dp'), may hold values from -1.5 to 1.5
- w_out: bfloat16 [8192, 8192], P('tensor', 'dp'), may hold values from -0.0625 to 0.0625
- ffn_gain: float32 [8192], replicated, may hold values from 0.1 to 1.9
- w_gate: bfloat16 [8192, 28672], P(None, ('dp', 'tensor')), may hold values from -0.0625 to 0.0625
- w_up: bfloat16 [8192, 28672], P(None, ('dp', 'tensor')), may hold values from -0.0625 to 0.0625
- w_down: bfloat16 [28672, 8192], P(('dp', 'tensor')), may hold values from -0.125 to 0.125
Outputs:
- block_out: bfloat16 [2, 128, 8192], P(None, 'dp', 'tensor')
- kv_cache: bfloat16 [8, 128, 1040, 256], P('tensor', 'dp')
The draws below stay inside these ranges and needn't reach their ends.
Inputs may be any that keep to these rules, and one draw needn't show every extreme that they name: `placement`: A permutation: every decoding slot holds one request; slots d * 8 to (d + 1) * 8 - 1 belong to dp index d. The requests of one dp index, drawn from the seed, all have 1024 tokens. For p < ceil(lengths[r] / 16), page_loc[h, r, p] = device * 512 + row names the pool row holding tokens 16 * p onward of request r for key-value head h; two pages of one head never share a row; of the pages of one head of the requests of one dp index, at most 32 lie on any one dp index of the pool, and this is reached in every draw; entries past a request's pages are 0.
All inputs are finite; a program needn't handle non-finite values.
Results may differ from the reference program's by a relative error of at most 0.034.
Values may be sent and summed in bfloat16 or wider, within the bound.
No kernel may reach another device: no remote copies, remote signals or barrier semaphores. Data moves between devices by JAX's collectives and lax.ppermute only.
A program may use at most 128 MiB of HBM per device.

```python
import math
import jax
import jax.numpy as jnp
from jax import lax

D = 8192
H = 64
KVH = 8
HD = 128
FF = 28672
REQ_DEV = 8
MAXLEN = 1024
PAGE = 16
STEPS = 2
GROUP = 8
REQUESTS = 128
MAXPG = 64
CACHE_TOK = 1040
CAP = 32
PSLOTS = 512
N_DP = 16


def page_layout(key):
    keys = jax.random.split(key, 5)
    placement = jax.random.permutation(keys[0], REQUESTS).astype(jnp.int32)
    raw_len = jax.random.randint(keys[1], (REQUESTS,), MAXLEN // 4, MAXLEN + 1).astype(jnp.int32)
    full_dev = jax.random.randint(keys[2], (), 0, N_DP).astype(jnp.int32)
    lengths = jnp.where(placement // REQ_DEV == full_dev, MAXLEN, raw_len).astype(jnp.int32)
    slot_order = jnp.zeros((REQUESTS,), jnp.int32).at[placement].set(jnp.arange(REQUESTS, dtype=jnp.int32))
    pages_slot = (lengths[slot_order] + PAGE - 1) // PAGE
    pages_dev = pages_slot.reshape(N_DP, REQ_DEV)
    starts = (jnp.cumsum(pages_dev, axis=1) - pages_dev).reshape(REQUESTS)
    page_idx = jnp.arange(MAXPG, dtype=jnp.int32)
    order_idx = starts[:, None] + page_idx[None, :]
    dest_dev = jnp.arange(REQUESTS, dtype=jnp.int32) // REQ_DEV
    offsets = jax.random.randint(keys[3], (N_DP, KVH), 0, N_DP).astype(jnp.int32)
    source = (order_idx[None, :, :] + jnp.transpose(offsets[dest_dev])[:, :, None]) % N_DP
    region = dest_dev[None, :, None] * CAP + order_idx[None, :, :] // N_DP
    region = jnp.minimum(region, PSLOTS - 1)
    perm_keys = jax.random.split(keys[4], N_DP * KVH)
    perms = jax.vmap(lambda one_key: jax.random.permutation(one_key, PSLOTS).astype(jnp.int32))(perm_keys).reshape(N_DP, KVH, PSLOTS)
    head_grid = jnp.arange(KVH, dtype=jnp.int32)[:, None, None]
    pool_row = perms[source, head_grid, region]
    live_page = page_idx[None, None, :] < pages_slot[None, :, None]
    loc_slot = jnp.where(live_page, source * PSLOTS + pool_row, 0).astype(jnp.int32)
    page_loc = loc_slot[:, placement, :]
    return (placement, lengths, page_loc)


def draw_placement(key, part):
    return page_layout(key)[0]


def draw_lengths(key, part):
    return page_layout(key)[1]


def draw_page_loc(key, part):
    return page_layout(key)[2]


def draw_kv_pool(key, part):
    key = jax.random.fold_in(key, 11)
    shape = (N_DP * PSLOTS, KVH, PAGE, 2 * HD)
    pool = jnp.clip(jax.random.normal(key, shape, jnp.float32), -6.0, 6.0)
    return pool.astype(jnp.bfloat16)


def draw_new_kv(key, part):
    key = jax.random.fold_in(key, 12)
    shape = (STEPS, REQUESTS, KVH, 2 * HD)
    values = jnp.clip(jax.random.normal(key, shape, jnp.float32), -6.0, 6.0)
    return values.astype(jnp.bfloat16)


def draw_queries(key, part):
    key = jax.random.fold_in(key, 13)
    shape = (STEPS, REQUESTS, H, HD)
    values = jnp.clip(2.5 * jax.random.normal(key, shape, jnp.float32), -10.0, 10.0)
    return values.astype(jnp.bfloat16)


def with_spikes(result, own_key, source, target, blocks, factor):
    def block_of(axis_at):
        return (jnp.arange(result.shape[axis_at]) // (result.shape[axis_at] // blocks)).reshape((-1,) + (1,) * (result.ndim - 1 - axis_at))

    one_side = jax.random.permutation(own_key, blocks)[block_of(target)]
    far = (block_of(target) + blocks // 2) % blocks
    return jnp.where((block_of(source) == one_side) | (block_of(source) == far), factor * result, result)


def block_levels(rng, shape, pieces, low, largest):
    loudness = 1.0
    for axis_at, shards_of in pieces:
        draws = jax.random.uniform(jax.random.fold_in(jax.random.fold_in(rng, 6), axis_at), (shards_of,), jnp.float32, low / len(pieces), largest / len(pieces))
        loudness = loudness * jnp.repeat(jnp.exp(draws), shape[axis_at] // shards_of).reshape((-1,) + (1,) * (len(shape) - 1 - axis_at))
    return loudness


def centred(rng, dims, deviation, most, cuts=(), kind=jnp.bfloat16):
    factor_of = block_levels(rng, dims, cuts, -0.22, 0.18) if cuts else 1.0
    result = jax.random.normal(rng, dims, jnp.float32) * deviation * factor_of
    return jnp.minimum(jnp.maximum(result, -most), most).astype(kind)


def bell_draw_with(own_key, shape, width, bound, cuts, heavy, kind=jnp.bfloat16):
    array = width * jax.random.normal(own_key, shape, jnp.float32)
    if cuts:
        array = array * block_levels(own_key, shape, cuts, -0.22, 0.18)
    return jnp.clip(with_spikes(array, jax.random.fold_in(own_key, 3), *heavy), -bound, bound).astype(kind)


def setup_inputs(seed: int = 0) -> dict:
    streams_of = jax.random.split(jax.random.key(seed), 13)
    return {
        "kv_pool": draw_kv_pool(jax.random.fold_in(streams_of[12], 71), 0),
        "page_loc": draw_page_loc(jax.random.fold_in(streams_of[12], 71), 0),
        "lengths": draw_lengths(jax.random.fold_in(streams_of[12], 71), 0),
        "placement": draw_placement(jax.random.fold_in(streams_of[12], 71), 0),
        "queries": draw_queries(jax.random.fold_in(streams_of[12], 71), 0),
        "new_kv": draw_new_kv(jax.random.fold_in(streams_of[12], 71), 0),
        "resid_in": centred(streams_of[6], (STEPS, REQUESTS, D), 0.25, 1.5, ((2, 16),)),
        "w_out": centred(streams_of[7], (H * HD, D), (H * HD) ** -0.5, 0.0625, ((0, 8), (1, 16))),
        "ffn_gain": jnp.clip(1.0 + 0.18 * jax.random.normal(streams_of[8], (D,), jnp.float32), 0.1, 1.9),
        "w_gate": centred(streams_of[9], (D, FF), D ** -0.5, 0.0625, ((1, 128),)),
        "w_up": centred(streams_of[10], (D, FF), D ** -0.5, 0.0625, ((1, 128),)),
        "w_down": bell_draw_with(streams_of[11], (FF, D), FF ** -0.5, 0.125, ((0, 128),), (0, 1, 128, 5.5)),
    }


def reference(kv_pool, page_loc, lengths, placement, queries, new_kv, resid_in, w_out, ffn_gain, w_gate, w_up, w_down):
    slot_order = jnp.zeros((REQUESTS,), jnp.int32).at[placement].set(jnp.arange(REQUESTS, dtype=jnp.int32))
    len_slot = lengths[slot_order]
    loc_slot = page_loc[:, slot_order, :]
    positions = jnp.arange(CACHE_TOK, dtype=jnp.int32)
    fresh_all = jnp.transpose(new_kv, (2, 0, 1, 3))

    def build_head(packed):
        kv_head, locs, fresh = packed
        pages = kv_pool[locs, kv_head]
        tokens = pages.reshape(REQUESTS, MAXLEN, 2 * HD)
        padded = jnp.concatenate([tokens, jnp.zeros((REQUESTS, PAGE, 2 * HD), tokens.dtype)], axis=1)
        cache = jnp.where(positions[None, :, None] < len_slot[:, None, None], padded, jnp.zeros((), padded.dtype))
        for step_idx in range(STEPS):
            cache = jnp.where(positions[None, :, None] == (len_slot + step_idx)[:, None, None], fresh[step_idx][:, None, :], cache)
        return cache
    kv_cache = lax.map(build_head, (jnp.arange(KVH, dtype=jnp.int32), loc_slot, fresh_all))
    outputs = []
    for step_idx in range(STEPS):
        query_heads = jnp.transpose(queries[step_idx].reshape(REQUESTS, KVH, GROUP, HD), (1, 0, 2, 3))

        def attend(packed, step_idx=step_idx):
            query, cache = packed
            scores = jnp.einsum('rgd,rtd->rgt', query.astype(jnp.float32), cache[:, :, :HD].astype(jnp.float32)) * (1.0 / math.sqrt(HD))
            visible = positions[None, None, :] < (len_slot + step_idx + 1)[:, None, None]
            scores = jnp.where(visible, scores, -jnp.inf)
            peak = lax.optimization_barrier(jnp.max(scores, axis=-1, keepdims=True))
            expo = jnp.exp(scores - peak)
            probs = (expo / lax.optimization_barrier(jnp.sum(expo, axis=-1, keepdims=True))).astype(jnp.bfloat16)
            return jnp.einsum('rgt,rtd->rgd', probs.astype(jnp.float32), cache[:, :, HD:].astype(jnp.float32)).astype(jnp.bfloat16)
        mixed = lax.map(attend, (query_heads, kv_cache))
        mixed = jnp.transpose(mixed, (1, 0, 2, 3)).reshape(REQUESTS, H * HD)
        projected = jnp.dot(mixed, w_out, preferred_element_type=jnp.float32)
        hidden = (resid_in[step_idx].astype(jnp.float32) + projected).astype(jnp.bfloat16)
        hid_wide = hidden.astype(jnp.float32)
        inverse = lax.rsqrt(lax.optimization_barrier(jnp.mean(hid_wide * hid_wide, axis=-1, keepdims=True)) + 1e-05)
        normed = (hid_wide * inverse * ffn_gain).astype(jnp.bfloat16)
        gate = jnp.dot(normed, w_gate, preferred_element_type=jnp.float32)
        upper = jnp.dot(normed, w_up, preferred_element_type=jnp.float32)
        act = (jax.nn.silu(gate) * upper).astype(jnp.bfloat16)
        down = jnp.dot(act, w_down, preferred_element_type=jnp.float32)
        outputs.append((hid_wide + down).astype(jnp.bfloat16))
    return (jnp.stack(outputs), kv_cache)
```

```python
import math

import jax
import jax.numpy as jnp
from jax import lax
from jax.sharding import Mesh, PartitionSpec as P

DP = ("yh", "x", "c")
CDP = ("c", "yh", "x")
TENSOR = ("z", "yl")
CHIPS = ("yh", "x", "z", "yl")


def to_all(block, axes, count):
    copies = lax.optimization_barrier(jnp.broadcast_to(block[None], (count,) + block.shape))
    return lax.all_to_all(copies, axes, 0, 0, tiled=True)


def page_plan(page_loc, lengths, placement, dev_dp, dev_tensor, n_dp, pslots, page_size):
    n_req = lengths.shape[0]
    max_pages = page_loc.shape[2]
    req_dev = n_req // n_dp
    entries = req_dev * max_pages
    capacity = pslots // n_dp
    loc_head = lax.dynamic_index_in_dim(page_loc, dev_tensor, 0, keepdims=False)
    slot_hot = placement[None, :] == jnp.arange(n_req, dtype=jnp.int32)[:, None]
    len_slot = jnp.sum(jnp.where(slot_hot, lengths[None, :], 0), axis=1)
    loc_slot = jnp.dot(
        slot_hot.astype(jnp.float32), loc_head.astype(jnp.float32), precision=lax.Precision.HIGHEST
    ).astype(jnp.int32)
    pages_slot = (len_slot + page_size - 1) // page_size
    live = jnp.arange(max_pages, dtype=jnp.int32)[None, :] < pages_slot[:, None]
    source = jnp.where(live, loc_slot // pslots, n_dp).reshape(n_dp, entries)
    row = (loc_slot % pslots).reshape(n_dp, entries)
    before = (
        jnp.arange(entries, dtype=jnp.int32)[:, None] < jnp.arange(entries, dtype=jnp.int32)[None, :]
    ).astype(jnp.bfloat16)
    mine_out = source == dev_dp
    rank_out = jnp.dot(
        mine_out.astype(jnp.bfloat16), before, preferred_element_type=jnp.float32
    ).astype(jnp.int32)
    rank_out = jnp.where(mine_out, rank_out, capacity)
    hit = rank_out[:, None, :] == jnp.arange(capacity, dtype=jnp.int32)[None, :, None]
    send_rows = jnp.sum(jnp.where(hit, row[:, None, :], 0), axis=2)
    my_source = lax.dynamic_index_in_dim(source, dev_dp, 0, keepdims=False)
    source_hot = my_source[None, :] == jnp.arange(n_dp, dtype=jnp.int32)[:, None]
    rank_in = jnp.dot(
        source_hot.astype(jnp.bfloat16), before, preferred_element_type=jnp.float32
    ).astype(jnp.int32)
    my_rank = jnp.sum(jnp.where(source_hot, rank_in, 0), axis=0)
    pick = jnp.where(my_source < n_dp, my_source * capacity + my_rank, 0)
    my_len = lax.dynamic_slice_in_dim(len_slot, dev_dp * req_dev, req_dev)
    return send_rows, pick, my_len


def per_device(
    kv_pool,
    page_loc,
    lengths,
    placement,
    queries,
    new_kv,
    resid_in,
    w_out,
    ffn_gain,
    w_gate,
    w_up,
    w_down,
):
    n_dp = lax.axis_size(DP)
    n_tensor = lax.axis_size(TENSOR)
    dev_dp = lax.axis_index(DP)
    dev_cdp = lax.axis_index(CDP)
    dev_tensor = lax.axis_index(TENSOR)
    core = lax.axis_index("c")
    pslots, _, page_size, width_two = kv_pool.shape
    head_dim = width_two // 2
    n_req = lengths.shape[0]
    req_dev = n_req // n_dp
    max_pages = page_loc.shape[2]
    max_len = max_pages * page_size
    cache_len = max_len + page_size
    n_steps = queries.shape[0]
    hq_dev = queries.shape[2]
    width = ffn_gain.shape[0]
    rows_dev = n_steps * req_dev
    rows_all = n_steps * n_req
    capacity = pslots // n_dp

    send_rows, pick, my_len = page_plan(
        page_loc, lengths, placement, dev_dp, dev_tensor, n_dp, pslots, page_size
    )
    outgoing = kv_pool[send_rows.reshape(-1), 0].reshape(n_dp, capacity, page_size, width_two)
    received = lax.all_to_all(outgoing, DP, 0, 0, tiled=True)
    arrived = received.reshape(pslots, page_size, width_two)[pick]
    tokens = arrived.reshape(req_dev, max_len, width_two)
    padded = jnp.pad(tokens, ((0, 0), (0, page_size), (0, 0)))
    positions = jnp.arange(cache_len, dtype=jnp.int32)
    cache = jnp.where(
        positions[None, :, None] < my_len[:, None, None], padded, jnp.zeros((), padded.dtype)
    )
    for step_idx in range(n_steps):
        cache = jnp.where(
            positions[None, :, None] == (my_len + step_idx)[:, None, None],
            new_kv[step_idx],
            cache,
        )
    query = jnp.transpose(queries, (1, 0, 2, 3)).reshape(req_dev, n_steps * hq_dev, head_dim)
    scores = jnp.einsum(
        "rqd,rtd->rqt", query, cache[..., :head_dim], preferred_element_type=jnp.float32
    ) * (1.0 / math.sqrt(head_dim))
    step_of = jnp.arange(n_steps * hq_dev, dtype=jnp.int32) // hq_dev
    visible = positions[None, None, :] <= my_len[:, None, None] + step_of[None, :, None]
    scores = jnp.where(visible, scores, -jnp.inf)
    peak = jnp.max(scores, axis=-1, keepdims=True)
    expo = jnp.exp(scores - peak)
    probs = (expo / jnp.sum(expo, axis=-1, keepdims=True)).astype(jnp.bfloat16)
    mixed = jnp.einsum(
        "rqt,rtd->rqd", probs, cache[..., head_dim:], preferred_element_type=jnp.float32
    ).astype(jnp.bfloat16)
    mixed = jnp.transpose(
        mixed.reshape(req_dev, n_steps, hq_dev * head_dim), (1, 0, 2)
    ).reshape(rows_dev, hq_dev * head_dim)

    mixed_all = to_all(mixed, CDP, n_dp).reshape(rows_all, hq_dev * head_dim)
    partial_out = jnp.dot(mixed_all, w_out, preferred_element_type=jnp.float32).astype(jnp.bfloat16)
    rows_blk = rows_all // n_tensor
    cols_blk = width // n_dp
    parts = lax.all_to_all(
        partial_out.reshape(n_tensor, rows_blk, cols_blk), TENSOR, 0, 0, tiled=True
    )
    resid_rows = jnp.transpose(
        resid_in.reshape(n_steps, n_dp // 2, 2, req_dev, cols_blk), (2, 1, 0, 3, 4)
    ).reshape(n_tensor, rows_blk, cols_blk)
    resid_blk = lax.dynamic_index_in_dim(resid_rows, dev_tensor, 0, keepdims=False)
    hidden_blk = (
        resid_blk.astype(jnp.float32) + jnp.sum(parts.astype(jnp.float32), axis=0)
    ).astype(jnp.bfloat16)
    chips_dp = n_dp // 2
    own_half = to_all(hidden_blk, CHIPS, chips_dp * n_tensor).reshape(chips_dp, rows_all, cols_blk)
    other_half = lax.ppermute(own_half, "c", [(0, 1), (1, 0)])
    halves = jnp.stack(
        [
            jnp.where(core == 0, own_half, other_half),
            jnp.where(core == 0, other_half, own_half),
        ],
        axis=1,
    )
    hidden = jnp.transpose(halves, (2, 0, 1, 3)).reshape(rows_all, width)
    hid_wide = hidden.astype(jnp.float32)
    inverse = lax.rsqrt(jnp.mean(hid_wide * hid_wide, axis=-1, keepdims=True) + 1e-05)
    normed = (hid_wide * inverse * ffn_gain).astype(jnp.bfloat16)
    gate = jnp.dot(normed, w_gate, preferred_element_type=jnp.float32)
    upper = jnp.dot(normed, w_up, preferred_element_type=jnp.float32)
    act = (jax.nn.silu(gate) * upper).astype(jnp.bfloat16)
    act_cores = act.reshape(2, rows_all // 2, act.shape[1])
    width_out = width // n_tensor

    def down(rows):
        return jnp.dot(rows, w_down, preferred_element_type=jnp.float32)

    theirs = down(lax.dynamic_index_in_dim(act_cores, 1 - core, 0, keepdims=False)).astype(
        jnp.bfloat16
    )
    from_core = lax.ppermute(theirs, "c", [(0, 1), (1, 0)])
    ours = down(lax.dynamic_index_in_dim(act_cores, core, 0, keepdims=False))
    chip_sum = (ours + from_core.astype(jnp.float32)).astype(jnp.bfloat16)
    chip_sum = jnp.transpose(
        chip_sum.reshape(chips_dp, rows_dev, n_tensor, width_out), (0, 2, 1, 3)
    ).reshape(chips_dp * n_tensor, rows_dev, width_out)
    pieces = lax.all_to_all(chip_sum, CHIPS, 0, 0, tiled=True)
    ffn_part = jnp.sum(pieces.astype(jnp.float32), axis=0)
    own_hidden = lax.dynamic_slice(
        hidden, (dev_cdp * rows_dev, dev_tensor * width_out), (rows_dev, width_out)
    )
    block_out = (own_hidden.astype(jnp.float32) + ffn_part).astype(jnp.bfloat16)
    return (block_out.reshape(n_steps, req_dev, width_out), cache[None])


def solution(mesh):
    fine = Mesh(mesh.devices.reshape(2, 4, 2, 4, 2), ("yh", "x", "c", "z", "yl"))
    placed = (
        P(DP, TENSOR, None, None),
        P(),
        P(),
        P(),
        P(None, DP, TENSOR, None),
        P(None, DP, TENSOR, None),
        P(None, None, DP),
        P(TENSOR, DP),
        P(),
        P(None, DP + TENSOR),
        P(None, DP + TENSOR),
        P(DP + TENSOR, None),
    )
    return jax.shard_map(
        per_device,
        mesh=fine,
        in_specs=placed,
        out_specs=(P(None, DP, TENSOR), P(TENSOR, DP, None, None)),
        check_vma=False,
    )
```

```python
import math

import jax
import jax.numpy as jnp
from jax import lax
from jax.experimental import pallas as pl
from jax.experimental.pallas import tpu as pltpu
from jax.sharding import Mesh, PartitionSpec as P

DP = ("yh", "x", "c")
CDP = ("c", "yh", "x")
TENSOR = ("z", "yl")
CHIPS = ("yh", "x", "z", "yl")


def to_all(block, axes, count):
    copies = lax.optimization_barrier(jnp.broadcast_to(block[None], (count,) + block.shape))
    return lax.all_to_all(copies, axes, 0, 0, tiled=True)

VMEM_LIMIT = 48 * 1024 * 1024


def intake(pick, lens, received, fresh, query, n_copies):
    req_dev, n_rows, head_dim = query.shape
    n_steps = fresh.shape[0]
    _, page_size, width_two = received.shape
    max_pages = pick.shape[0] // req_dev
    pages = max_pages + 1
    group = n_rows // n_steps
    scale = 1.0 / math.sqrt(head_dim)
    ahead = 2

    def kernel(pick_ref, len_ref, recv_ref, fresh_ref, q_ref, cache_ref, mixed_ref, buf, heads, in_sems, out_sems):
        def start(r):
            def body(p, carry):
                pltpu.make_async_copy(
                    recv_ref.at[pick_ref[r * max_pages + p]], buf.at[r, p], in_sems.at[r]
                ).start()
                return carry

            lax.fori_loop(0, max_pages, body, 0, unroll=8)

        def copy_out(r):
            return pltpu.make_async_copy(buf.at[r], cache_ref.at[r], out_sems.at[r])

        for r in range(ahead):
            start(r)
        row_at = lax.broadcasted_iota(jnp.int32, (page_size, width_two), 0)
        for r in range(req_dev):
            if r + ahead < req_dev:
                start(r + ahead)
            pltpu.make_async_copy(
                recv_ref.at[pl.ds(0, max_pages)], buf.at[r, pl.ds(0, max_pages)], in_sems.at[r]
            ).wait()
            length = len_ref[r]
            full = length // page_size

            def clear(p, carry):
                buf[r, p] = jnp.zeros((page_size, width_two), buf.dtype)
                return carry

            lax.fori_loop(full + 1, pages, clear, 0)
            edge = buf[r, full].astype(jnp.float32)
            buf[r, full] = jnp.where(row_at < length % page_size, edge, 0.0).astype(buf.dtype)
            for s in range(n_steps):
                at = length + s
                page = buf[r, at // page_size].astype(jnp.float32)
                token = fresh_ref[s, r : r + 1, :]
                buf[r, at // page_size] = jnp.where(
                    row_at == at % page_size, token, page
                ).astype(buf.dtype)
            copy_out(r).start()
            tokens = buf[r].reshape(pages * page_size, width_two)
            scores = scale * lax.dot_general(
                q_ref[r],
                tokens[:, :head_dim],
                (((1,), (1,)), ((), ())),
                preferred_element_type=jnp.float32,
            )
            last = length + lax.broadcasted_iota(jnp.int32, scores.shape, 0) // group
            scores = jnp.where(
                lax.broadcasted_iota(jnp.int32, scores.shape, 1) <= last, scores, -jnp.inf
            )
            expo = jnp.exp(scores - jnp.max(scores, axis=1, keepdims=True))
            total = jnp.sum(expo, axis=1, keepdims=True)
            probs = (expo / total).astype(jnp.bfloat16)
            head_out = jnp.dot(probs, tokens[:, head_dim:], preferred_element_type=jnp.float32)
            for i in range(n_rows):
                heads[i, r : r + 1, :] = head_out[i : i + 1, :]
        for g in range(group):
            block = jnp.concatenate([heads[s * group + g] for s in range(n_steps)], axis=0)
            block = block.astype(mixed_ref.dtype)
            for k in range(n_copies):
                mixed_ref[k, :, g * head_dim : (g + 1) * head_dim] = block
        for r in range(req_dev):
            copy_out(r).wait()

    smem = pl.BlockSpec(memory_space=pltpu.SMEM)
    vmem = pl.BlockSpec(memory_space=pltpu.VMEM)
    hbm = pl.BlockSpec(memory_space=pl.ANY)
    return pl.pallas_call(
        kernel,
        in_specs=[smem, smem, hbm, vmem, vmem],
        out_specs=[hbm, vmem],
        out_shape=[
            jax.ShapeDtypeStruct((req_dev, pages, page_size, width_two), received.dtype),
            jax.ShapeDtypeStruct(
                (n_copies, n_steps * req_dev, group * head_dim), received.dtype
            ),
        ],
        scratch_shapes=[
            pltpu.VMEM((req_dev, pages, page_size, width_two), received.dtype),
            pltpu.VMEM((n_rows, req_dev, head_dim), jnp.float32),
            pltpu.SemaphoreType.DMA((req_dev,)),
            pltpu.SemaphoreType.DMA((req_dev,)),
        ],
        compiler_params=pltpu.CompilerParams(vmem_limit_bytes=VMEM_LIMIT),
        name="intake",
    )(pick, lens, received, fresh, query)


def expand_step(x_ref, gate_ref, up_ref, gain_ref, gate_sum, up_sum, squares):
    wide = x_ref[0].astype(jnp.float32)
    lanes = squares.shape[1]
    square = wide * wide
    squares[...] += sum(
        square[:, k * lanes : (k + 1) * lanes] for k in range(square.shape[1] // lanes)
    )
    scaled = (wide * gain_ref[...]).astype(jnp.bfloat16)
    contract = (((1,), (1,)), ((), ()))
    gate_sum[...] += lax.dot_general(
        scaled, gate_ref[...], contract, preferred_element_type=jnp.float32
    )
    up_sum[...] += lax.dot_general(
        scaled, up_ref[...], contract, preferred_element_type=jnp.float32
    )


def expand_own(core_at, own_half, gate_rows, up_rows, gain_row):
    steps, rows, cols = own_half.shape
    units = gate_rows.shape[0]

    def kernel(core_ref, x_ref, gate_ref, up_ref, gain_ref, gate_sum, up_sum, squares):
        @pl.when(pl.program_id(0) == 0)
        def _():
            gate_sum[...] = jnp.zeros_like(gate_sum)
            up_sum[...] = jnp.zeros_like(up_sum)
            squares[...] = jnp.zeros_like(squares)

        expand_step(x_ref, gate_ref, up_ref, gain_ref, gate_sum, up_sum, squares)

    weight = pl.BlockSpec((units, cols), lambda i, core: (0, 2 * i + core[0]))
    return pl.pallas_call(
        kernel,
        grid_spec=pltpu.PrefetchScalarGridSpec(
            num_scalar_prefetch=1,
            grid=(steps,),
            in_specs=[
                pl.BlockSpec((1, rows, cols), lambda i, core: (i, 0, 0)),
                weight,
                weight,
                pl.BlockSpec((1, cols), lambda i, core: (0, 2 * i + core[0])),
            ],
            out_specs=[
                pl.BlockSpec((rows, units), lambda i, core: (0, 0)),
                pl.BlockSpec((rows, units), lambda i, core: (0, 0)),
                pl.BlockSpec((rows, 128), lambda i, core: (0, 0)),
            ],
        ),
        out_shape=[
            jax.ShapeDtypeStruct((rows, units), jnp.float32),
            jax.ShapeDtypeStruct((rows, units), jnp.float32),
            jax.ShapeDtypeStruct((rows, 128), jnp.float32),
        ],
        compiler_params=pltpu.CompilerParams(vmem_limit_bytes=VMEM_LIMIT),
        name="expand_own",
    )(core_at, own_half, gate_rows, up_rows, gain_row)


def expand_other(core_at, other_half, gate_rows, up_rows, gain_row, sums, w_down, n_tensor, rows_dev):
    steps, rows, cols = other_half.shape
    units, width = w_down.shape
    cols_out = width // n_tensor
    half_rows = rows // 2
    chips = half_rows // rows_dev

    def kernel(
        core_ref, x_ref, gate_ref, up_ref, gain_ref, gate_in, up_in, squares_in, down_ref,
        act_ref, theirs_ref, gate_sum, up_sum, squares,
    ):
        step = pl.program_id(0)

        @pl.when(step == 0)
        def _():
            gate_sum[...] = gate_in[...]
            up_sum[...] = up_in[...]
            squares[...] = squares_in[...]

        @pl.when(step < steps)
        def _():
            expand_step(x_ref, gate_ref, up_ref, gain_ref, gate_sum, up_sum, squares)

        @pl.when(step == steps - 1)
        def _():
            mean = jnp.sum(squares[...], axis=1, keepdims=True) * (1.0 / width)
            inverse = lax.rsqrt(mean + 1e-05)
            gate = gate_sum[...] * inverse
            act = gate / (1.0 + jnp.exp(-gate)) * (up_sum[...] * inverse)
            act_ref[...] = act.astype(act_ref.dtype).reshape(2, half_rows, units)

        @pl.when(step >= steps)
        def _():
            out = jnp.dot(
                act_ref[1 - core_ref[0]], down_ref[...], preferred_element_type=jnp.float32
            )
            theirs_ref[...] = out.astype(theirs_ref.dtype).reshape(chips, 1, rows_dev, cols_out)

    def into(i):
        return jnp.minimum(i, steps - 1)

    def out_of(i):
        return jnp.maximum(i - steps, 0)

    weight = pl.BlockSpec((units, cols), lambda i, core: (0, 2 * into(i) + 1 - core[0]))
    whole = pl.BlockSpec((rows, units), lambda i, core: (0, 0))
    return pl.pallas_call(
        kernel,
        grid_spec=pltpu.PrefetchScalarGridSpec(
            num_scalar_prefetch=1,
            grid=(steps + n_tensor,),
            in_specs=[
                pl.BlockSpec((1, rows, cols), lambda i, core: (into(i), 0, 0)),
                weight,
                weight,
                pl.BlockSpec((1, cols), lambda i, core: (0, 2 * into(i) + 1 - core[0])),
                whole,
                whole,
                pl.BlockSpec((rows, 128), lambda i, core: (0, 0)),
                pl.BlockSpec((units, cols_out), lambda i, core: (0, out_of(i))),
            ],
            out_specs=[
                pl.BlockSpec((2, half_rows, units), lambda i, core: (0, 0, 0)),
                pl.BlockSpec((chips, 1, rows_dev, cols_out), lambda i, core: (0, out_of(i), 0, 0)),
            ],
            scratch_shapes=[
                pltpu.VMEM((rows, units), jnp.float32),
                pltpu.VMEM((rows, units), jnp.float32),
                pltpu.VMEM((rows, 128), jnp.float32),
            ],
        ),
        out_shape=[
            jax.ShapeDtypeStruct((2, half_rows, units), jnp.bfloat16),
            jax.ShapeDtypeStruct((chips, n_tensor, rows_dev, cols_out), jnp.bfloat16),
        ],
        compiler_params=pltpu.CompilerParams(vmem_limit_bytes=VMEM_LIMIT),
        name="expand_other",
    )(core_at, other_half, gate_rows, up_rows, gain_row, *sums, w_down)


def shrink_own(core_at, act, w_down, n_tensor, rows_dev):
    _, half_rows, units = act.shape
    cols_out = w_down.shape[1] // n_tensor
    chips = half_rows // rows_dev

    def kernel(core_ref, act_ref, down_ref, ours_ref):
        out = jnp.dot(act_ref[0], down_ref[...], preferred_element_type=jnp.float32)
        ours_ref[...] = out.astype(ours_ref.dtype).reshape(chips, 1, rows_dev, cols_out)

    return pl.pallas_call(
        kernel,
        grid_spec=pltpu.PrefetchScalarGridSpec(
            num_scalar_prefetch=1,
            grid=(n_tensor,),
            in_specs=[
                pl.BlockSpec((1, half_rows, units), lambda i, core: (core[0], 0, 0)),
                pl.BlockSpec((units, cols_out), lambda i, core: (0, i)),
            ],
            out_specs=pl.BlockSpec((chips, 1, rows_dev, cols_out), lambda i, core: (0, i, 0, 0)),
        ),
        out_shape=jax.ShapeDtypeStruct((chips, n_tensor, rows_dev, cols_out), jnp.bfloat16),
        compiler_params=pltpu.CompilerParams(vmem_limit_bytes=VMEM_LIMIT),
        name="shrink_own",
    )(core_at, act, w_down)


def page_plan(page_loc, lengths, placement, dev_dp, dev_tensor, n_dp, pslots, page_size):
    n_req = lengths.shape[0]
    max_pages = page_loc.shape[2]
    req_dev = n_req // n_dp
    entries = req_dev * max_pages
    capacity = pslots // n_dp
    loc_head = lax.dynamic_index_in_dim(page_loc, dev_tensor, 0, keepdims=False)
    slot_hot = placement[None, :] == jnp.arange(n_req, dtype=jnp.int32)[:, None]
    len_slot = jnp.sum(jnp.where(slot_hot, lengths[None, :], 0), axis=1)
    loc_slot = jnp.dot(
        slot_hot.astype(jnp.float32), loc_head.astype(jnp.float32), precision=lax.Precision.HIGHEST
    ).astype(jnp.int32)
    pages_slot = (len_slot + page_size - 1) // page_size
    live = jnp.arange(max_pages, dtype=jnp.int32)[None, :] < pages_slot[:, None]
    source = jnp.where(live, loc_slot // pslots, n_dp).reshape(n_dp, entries)
    row = (loc_slot % pslots).reshape(n_dp, entries)
    before = (
        jnp.arange(entries, dtype=jnp.int32)[:, None] < jnp.arange(entries, dtype=jnp.int32)[None, :]
    ).astype(jnp.bfloat16)
    mine_out = source == dev_dp
    rank_out = jnp.dot(
        mine_out.astype(jnp.bfloat16), before, preferred_element_type=jnp.float32
    ).astype(jnp.int32)
    rank_out = jnp.where(mine_out, rank_out, capacity)
    hit = rank_out[:, None, :] == jnp.arange(capacity, dtype=jnp.int32)[None, :, None]
    send_rows = jnp.sum(jnp.where(hit, row[:, None, :], 0), axis=2)
    my_source = lax.dynamic_index_in_dim(source, dev_dp, 0, keepdims=False)
    source_hot = my_source[None, :] == jnp.arange(n_dp, dtype=jnp.int32)[:, None]
    rank_in = jnp.dot(
        source_hot.astype(jnp.bfloat16), before, preferred_element_type=jnp.float32
    ).astype(jnp.int32)
    my_rank = jnp.sum(jnp.where(source_hot, rank_in, 0), axis=0)
    pick = jnp.where(my_source < n_dp, my_source * capacity + my_rank, 0)
    my_len = lax.dynamic_slice_in_dim(len_slot, dev_dp * req_dev, req_dev)
    return send_rows, pick, my_len


def per_device(
    kv_pool,
    page_loc,
    lengths,
    placement,
    queries,
    new_kv,
    resid_in,
    w_out,
    ffn_gain,
    w_gate,
    w_up,
    w_down,
):
    n_dp = lax.axis_size(DP)
    n_tensor = lax.axis_size(TENSOR)
    dev_dp = lax.axis_index(DP)
    dev_cdp = lax.axis_index(CDP)
    dev_tensor = lax.axis_index(TENSOR)
    core = lax.axis_index("c")
    pslots, _, page_size, width_two = kv_pool.shape
    head_dim = width_two // 2
    n_req = lengths.shape[0]
    req_dev = n_req // n_dp
    max_pages = page_loc.shape[2]
    max_len = max_pages * page_size
    cache_len = max_len + page_size
    n_steps = queries.shape[0]
    hq_dev = queries.shape[2]
    width = ffn_gain.shape[0]
    rows_dev = n_steps * req_dev
    rows_all = n_steps * n_req
    capacity = pslots // n_dp

    send_rows, pick, my_len = page_plan(
        page_loc, lengths, placement, dev_dp, dev_tensor, n_dp, pslots, page_size
    )
    outgoing = kv_pool[send_rows.reshape(-1), 0].reshape(n_dp, capacity, page_size, width_two)
    received = lax.all_to_all(outgoing, DP, 0, 0, tiled=True)
    query = jnp.transpose(queries, (1, 0, 2, 3)).reshape(req_dev, n_steps * hq_dev, head_dim)
    cache, mixed_copies = intake(
        pick,
        my_len,
        received.reshape(pslots, page_size, width_two),
        new_kv.reshape(n_steps, req_dev, width_two).astype(jnp.float32),
        query,
        n_dp,
    )

    mixed_all = lax.all_to_all(mixed_copies, CDP, 0, 0, tiled=True).reshape(
        rows_all, hq_dev * head_dim
    )
    partial_out = jnp.dot(mixed_all, w_out, preferred_element_type=jnp.float32).astype(jnp.bfloat16)
    rows_blk = rows_all // n_tensor
    cols_blk = width // n_dp
    parts = lax.all_to_all(
        partial_out.reshape(n_tensor, rows_blk, cols_blk), TENSOR, 0, 0, tiled=True
    )
    resid_rows = jnp.transpose(
        resid_in.reshape(n_steps, n_dp // 2, 2, req_dev, cols_blk), (2, 1, 0, 3, 4)
    ).reshape(n_tensor, rows_blk, cols_blk)
    resid_blk = lax.dynamic_index_in_dim(resid_rows, dev_tensor, 0, keepdims=False)
    hidden_blk = (
        resid_blk.astype(jnp.float32) + jnp.sum(parts.astype(jnp.float32), axis=0)
    ).astype(jnp.bfloat16)
    chips_dp = n_dp // 2
    own_half = to_all(hidden_blk, CHIPS, chips_dp * n_tensor).reshape(chips_dp, rows_all, cols_blk)
    other_half = lax.ppermute(own_half, "c", [(0, 1), (1, 0)])
    core_at = core.reshape(1).astype(jnp.int32)
    gate_rows = jnp.swapaxes(w_gate, 0, 1)
    up_rows = jnp.swapaxes(w_up, 0, 1)
    gain_row = ffn_gain.reshape(1, width)
    width_out = width // n_tensor
    sums = expand_own(core_at, own_half, gate_rows, up_rows, gain_row)
    act, theirs = expand_other(
        core_at, other_half, gate_rows, up_rows, gain_row, sums, w_down, n_tensor, rows_dev
    )
    from_core = lax.ppermute(theirs, "c", [(0, 1), (1, 0)])
    ours = shrink_own(core_at, act, w_down, n_tensor, rows_dev)
    chip_sum = (
        (ours.astype(jnp.float32) + from_core.astype(jnp.float32))
        .astype(jnp.bfloat16)
        .reshape(chips_dp * n_tensor, rows_dev, width_out)
    )
    pieces = lax.all_to_all(chip_sum, CHIPS, 0, 0, tiled=True)
    ffn_part = jnp.sum(pieces.astype(jnp.float32), axis=0)

    def own_cols(half):
        return lax.dynamic_slice(
            half, (dev_tensor, dev_cdp * rows_dev, 0), (1, rows_dev, cols_blk)
        )[0]

    mine, partners = own_cols(own_half), own_cols(other_half)
    own_hidden = jnp.concatenate(
        [jnp.where(core == 0, mine, partners), jnp.where(core == 0, partners, mine)], axis=1
    )
    block_out = (own_hidden.astype(jnp.float32) + ffn_part).astype(jnp.bfloat16)
    return (block_out.reshape(n_steps, req_dev, width_out), cache.reshape(1, req_dev, cache_len, width_two))


def solution(mesh):
    fine = Mesh(mesh.devices.reshape(2, 4, 2, 4, 2), ("yh", "x", "c", "z", "yl"))
    placed = (
        P(DP, TENSOR, None, None),
        P(),
        P(),
        P(),
        P(None, DP, TENSOR, None),
        P(None, DP, TENSOR, None),
        P(None, None, DP),
        P(TENSOR, DP),
        P(),
        P(None, DP + TENSOR),
        P(None, DP + TENSOR),
        P(DP + TENSOR, None),
    )
    return jax.shard_map(
        per_device,
        mesh=fine,
        in_specs=placed,
        out_specs=(P(None, DP, TENSOR), P(TENSOR, DP, None, None)),
        check_vma=False,
    )
```

```python
import math

import jax
import jax.numpy as jnp
from jax import lax
from jax.experimental import pallas as pl
from jax.experimental.pallas import tpu as pltpu
from jax.sharding import Mesh, PartitionSpec as P

DP = ("yh", "x", "c")
CDP = ("c", "yh", "x")
TENSOR = ("z", "yl")
CHIPS = ("yh", "x", "z", "yl")


def to_all(block, axes, count):
    copies = lax.optimization_barrier(jnp.broadcast_to(block[None], (count,) + block.shape))
    return lax.all_to_all(copies, axes, 0, 0, tiled=True)

VMEM_LIMIT = 20 * 1024 * 1024
BLOCK = 512
SMEM = pl.BlockSpec(memory_space=pltpu.SMEM)
VMEM = pl.BlockSpec(memory_space=pltpu.VMEM)
HBM = pl.BlockSpec(memory_space=pltpu.HBM)


def intake(pick, lens, received, fresh, query, n_copies):
    req_dev, n_rows, head_dim = query.shape
    n_steps = fresh.shape[0]
    _, page_size, width_two = received.shape
    max_pages = pick.shape[0] // req_dev
    pages = max_pages + 1
    group = n_rows // n_steps
    scale = 1.0 / math.sqrt(head_dim)
    ahead = 2

    def kernel(pick_ref, len_ref, recv_ref, fresh_ref, q_ref, cache_ref, mixed_ref, buf, heads, in_sems, out_sems):
        def start(r):
            def body(p, carry):
                pltpu.make_async_copy(
                    recv_ref.at[pick_ref[r * max_pages + p]], buf.at[r, p], in_sems.at[r]
                ).start()
                return carry

            lax.fori_loop(0, max_pages, body, 0, unroll=8)

        def copy_out(r):
            return pltpu.make_async_copy(buf.at[r], cache_ref.at[r], out_sems.at[r])

        for r in range(ahead):
            start(r)
        row_at = lax.broadcasted_iota(jnp.int32, (page_size, width_two), 0)
        for r in range(req_dev):
            if r + ahead < req_dev:
                start(r + ahead)
            pltpu.make_async_copy(
                recv_ref.at[pl.ds(0, max_pages)], buf.at[r, pl.ds(0, max_pages)], in_sems.at[r]
            ).wait()
            length = len_ref[r]
            full = length // page_size

            def clear(p, carry):
                buf[r, p] = jnp.zeros((page_size, width_two), buf.dtype)
                return carry

            lax.fori_loop(full + 1, pages, clear, 0)
            edge = buf[r, full].astype(jnp.float32)
            buf[r, full] = jnp.where(row_at < length % page_size, edge, 0.0).astype(buf.dtype)
            for s in range(n_steps):
                at = length + s
                page = buf[r, at // page_size].astype(jnp.float32)
                token = fresh_ref[s, r : r + 1, :]
                buf[r, at // page_size] = jnp.where(
                    row_at == at % page_size, token, page
                ).astype(buf.dtype)
            copy_out(r).start()
            tokens = buf[r].reshape(pages * page_size, width_two)
            scores = scale * lax.dot_general(
                q_ref[r],
                tokens[:, :head_dim],
                (((1,), (1,)), ((), ())),
                preferred_element_type=jnp.float32,
            )
            last = length + lax.broadcasted_iota(jnp.int32, scores.shape, 0) // group
            scores = jnp.where(
                lax.broadcasted_iota(jnp.int32, scores.shape, 1) <= last, scores, -jnp.inf
            )
            expo = jnp.exp(scores - jnp.max(scores, axis=1, keepdims=True))
            total = jnp.sum(expo, axis=1, keepdims=True)
            probs = (expo / total).astype(jnp.bfloat16)
            head_out = jnp.dot(probs, tokens[:, head_dim:], preferred_element_type=jnp.float32)
            for i in range(n_rows):
                heads[i, r : r + 1, :] = head_out[i : i + 1, :]
        for g in range(group):
            block = jnp.concatenate([heads[s * group + g] for s in range(n_steps)], axis=0)
            block = block.astype(mixed_ref.dtype)
            for k in range(n_copies):
                mixed_ref[k, :, g * head_dim : (g + 1) * head_dim] = block
        for r in range(req_dev):
            copy_out(r).wait()

    return pl.pallas_call(
        kernel,
        in_specs=[SMEM, SMEM, HBM, VMEM, VMEM],
        out_specs=[HBM, VMEM],
        out_shape=[
            jax.ShapeDtypeStruct((req_dev, pages, page_size, width_two), received.dtype),
            jax.ShapeDtypeStruct(
                (n_copies, n_steps * req_dev, group * head_dim), received.dtype
            ),
        ],
        scratch_shapes=[
            pltpu.VMEM((req_dev, pages, page_size, width_two), received.dtype),
            pltpu.VMEM((n_rows, req_dev, head_dim), jnp.float32),
            pltpu.SemaphoreType.DMA((req_dev,)),
            pltpu.SemaphoreType.DMA((req_dev,)),
        ],
        compiler_params=pltpu.CompilerParams(vmem_limit_bytes=VMEM_LIMIT),
        name="intake",
    )(pick, lens, received, fresh, query)


def start_weights(side, sources, buffers, sems):
    for m, (source, buffer) in enumerate(zip(sources, buffers)):
        for i in range(buffer.shape[1] // BLOCK):
            weight_copy(side, source, buffer, sems.at[m, i], i).start()


def weight_copy(side, source, buffer, sem, i):
    at = pl.multiple_of((2 * i + side) * BLOCK, BLOCK)
    return pltpu.make_async_copy(
        source.at[:, pl.ds(at, BLOCK)], buffer.at[:, pl.ds(i * BLOCK, BLOCK)], sem
    )


def expand(side, x_ref, gain_ref, sources, buffers, sems, scaled, parts=2):
    steps = x_ref.shape[0]
    squares = 0.0
    for i in range(steps):
        at = pl.multiple_of((2 * i + side) * BLOCK, BLOCK)
        wide = x_ref[i].astype(jnp.float32)
        square = wide * wide
        squares += sum(square[:, k * 128 : (k + 1) * 128] for k in range(BLOCK // 128))
        scaled[:, i * BLOCK : (i + 1) * BLOCK] = (wide * gain_ref[:, pl.ds(at, BLOCK)]).astype(
            scaled.dtype
        )
    products = [0.0] * len(sources)
    for part in range(parts):
        span = steps // parts
        cols = slice(part * span * BLOCK, (part + 1) * span * BLOCK)
        for m, (source, buffer) in enumerate(zip(sources, buffers)):
            for i in range(part * span, (part + 1) * span):
                weight_copy(side, source, buffer, sems.at[m, i], i).wait()
            products[m] += lax.dot_general(
                scaled[:, cols],
                buffer[:, cols],
                (((1,), (1,)), ((), ())),
                preferred_element_type=jnp.float32,
            )
    return products, squares


def expand_scratch(steps, rows, units):
    return [
        pltpu.VMEM((units, steps * BLOCK), jnp.bfloat16),
        pltpu.VMEM((units, steps * BLOCK), jnp.bfloat16),
        pltpu.VMEM((rows, steps * BLOCK), jnp.bfloat16),
        pltpu.SemaphoreType.DMA((2, steps)),
    ]


def expand_own(core_at, own_half, gate_rows, up_rows, gain_row):
    steps, rows, _ = own_half.shape
    units = gate_rows.shape[0]

    def kernel(core_ref, x_ref, gate_ref, up_ref, gain_ref, gate_sum, up_sum, squares_sum, gate_buf, up_buf, scaled, sems):
        side = core_ref[0]
        sources, buffers = (gate_ref, up_ref), (gate_buf, up_buf)
        start_weights(side, sources, buffers, sems)
        (gate, upper), squares = expand(side, x_ref, gain_ref, sources, buffers, sems, scaled)
        gate_sum[...] = gate
        up_sum[...] = upper
        squares_sum[...] = squares

    return pl.pallas_call(
        kernel,
        in_specs=[SMEM, VMEM, HBM, HBM, VMEM],
        out_specs=[VMEM, VMEM, VMEM],
        out_shape=[
            jax.ShapeDtypeStruct((rows, units), jnp.float32),
            jax.ShapeDtypeStruct((rows, units), jnp.float32),
            jax.ShapeDtypeStruct((rows, 128), jnp.float32),
        ],
        scratch_shapes=expand_scratch(steps, rows, units),
        compiler_params=pltpu.CompilerParams(vmem_limit_bytes=VMEM_LIMIT),
        name="expand_own",
    )(core_at, own_half, gate_rows, up_rows, gain_row)


def expand_other(core_at, other_half, gate_rows, up_rows, gain_row, sums, w_down, n_tensor, rows_dev):
    steps, rows, _ = other_half.shape
    units, width = w_down.shape
    cols_out = width // n_tensor
    half_rows = rows // 2
    chips = half_rows // rows_dev

    def kernel(
        core_ref, x_ref, gate_ref, up_ref, gain_ref, gate_in, up_in, squares_in, down_ref,
        act_ref, theirs_ref, gate_buf, up_buf, scaled, sems, down_buf, down_sem,
    ):
        side = 1 - core_ref[0]
        sources, buffers = (gate_ref, up_ref), (gate_buf, up_buf)
        start_weights(side, sources, buffers, sems)
        down_copy = pltpu.make_async_copy(down_ref, down_buf, down_sem)
        down_copy.start()
        (gate, upper), squares = expand(side, x_ref, gain_ref, sources, buffers, sems, scaled)
        squares += squares_in[...]
        inverse = lax.rsqrt(jnp.sum(squares, axis=1, keepdims=True) * (1.0 / width) + 1e-05)
        gate = (gate + gate_in[...]) * inverse
        act = gate / (1.0 + jnp.exp(-gate)) * ((upper + up_in[...]) * inverse)
        act_ref[...] = act.astype(act_ref.dtype).reshape(2, half_rows, units)
        down_copy.wait()
        picked = act_ref[side]
        for t in range(n_tensor):
            out = jnp.dot(
                picked,
                down_buf[:, t * cols_out : (t + 1) * cols_out],
                preferred_element_type=jnp.float32,
            )
            theirs_ref[:, t] = out.astype(theirs_ref.dtype).reshape(chips, rows_dev, cols_out)

    return pl.pallas_call(
        kernel,
        in_specs=[SMEM, VMEM, HBM, HBM, VMEM, VMEM, VMEM, VMEM, HBM],
        out_specs=[VMEM, VMEM],
        out_shape=[
            jax.ShapeDtypeStruct((2, half_rows, units), jnp.bfloat16),
            jax.ShapeDtypeStruct((chips, n_tensor, rows_dev, cols_out), jnp.bfloat16),
        ],
        scratch_shapes=expand_scratch(steps, rows, units)
        + [pltpu.VMEM((units, width), jnp.bfloat16), pltpu.SemaphoreType.DMA],
        compiler_params=pltpu.CompilerParams(vmem_limit_bytes=VMEM_LIMIT),
        name="expand_other",
    )(core_at, other_half, gate_rows, up_rows, gain_row, *sums, w_down)


def gather_pages(rows, pool):
    count = rows.shape[0]

    def kernel(rows_ref, pool_ref, out_ref, sem):
        def body(k, carry):
            pltpu.make_async_copy(pool_ref.at[rows_ref[k]], out_ref.at[k], sem).start()
            return carry

        lax.fori_loop(0, count, body, 0, unroll=16)
        pltpu.make_async_copy(pool_ref, out_ref, sem).wait()

    return pl.pallas_call(
        kernel,
        in_specs=[SMEM, HBM],
        out_specs=HBM,
        out_shape=jax.ShapeDtypeStruct((count,) + pool.shape[1:], pool.dtype),
        scratch_shapes=[pltpu.SemaphoreType.DMA],
        name="gather_pages",
    )(rows, pool)


def shrink_own(core_at, act, w_down, n_tensor, rows_dev):
    _, half_rows, units = act.shape
    cols_out = w_down.shape[1] // n_tensor
    chips = half_rows // rows_dev

    def kernel(core_ref, act_ref, down_ref, ours_ref):
        picked = act_ref[core_ref[0]]
        for t in range(n_tensor):
            out = jnp.dot(
                picked,
                down_ref[:, t * cols_out : (t + 1) * cols_out],
                preferred_element_type=jnp.float32,
            )
            ours_ref[:, t] = out.astype(ours_ref.dtype).reshape(chips, rows_dev, cols_out)

    return pl.pallas_call(
        kernel,
        in_specs=[SMEM, VMEM, VMEM],
        out_specs=VMEM,
        out_shape=jax.ShapeDtypeStruct((chips, n_tensor, rows_dev, cols_out), jnp.bfloat16),
        compiler_params=pltpu.CompilerParams(vmem_limit_bytes=VMEM_LIMIT),
        name="shrink_own",
    )(core_at, act, w_down)


def add_cores(ours, from_core):
    chips = ours.shape[0]

    def kernel(a_ref, b_ref, out_ref, buf, sems):
        def copy(i):
            return pltpu.make_async_copy(buf.at[i], out_ref.at[i], sems.at[i])

        for i in range(chips):
            buf[i] = (a_ref[i].astype(jnp.float32) + b_ref[i].astype(jnp.float32)).astype(buf.dtype)
            copy(i).start()
        for i in range(chips):
            copy(i).wait()

    return pl.pallas_call(
        kernel,
        in_specs=[VMEM, VMEM],
        out_specs=HBM,
        out_shape=pltpu.HBM(ours.shape, ours.dtype),
        scratch_shapes=[pltpu.VMEM(ours.shape, ours.dtype), pltpu.SemaphoreType.DMA((chips,))],
        compiler_params=pltpu.CompilerParams(vmem_limit_bytes=VMEM_LIMIT),
        name="add_cores",
    )(ours, from_core)


def page_plan(page_loc, lengths, placement, dev_dp, dev_tensor, n_dp, pslots, page_size):
    n_req = lengths.shape[0]
    max_pages = page_loc.shape[2]
    req_dev = n_req // n_dp
    entries = req_dev * max_pages
    capacity = pslots // n_dp
    loc_head = lax.dynamic_index_in_dim(page_loc, dev_tensor, 0, keepdims=False)
    slot_hot = placement[None, :] == jnp.arange(n_req, dtype=jnp.int32)[:, None]
    len_slot = jnp.sum(jnp.where(slot_hot, lengths[None, :], 0), axis=1)
    loc_slot = jnp.dot(
        slot_hot.astype(jnp.float32), loc_head.astype(jnp.float32), precision=lax.Precision.HIGHEST
    ).astype(jnp.int32)
    pages_slot = (len_slot + page_size - 1) // page_size
    live = jnp.arange(max_pages, dtype=jnp.int32)[None, :] < pages_slot[:, None]
    source = jnp.where(live, loc_slot // pslots, n_dp).reshape(n_dp, entries)
    row = (loc_slot % pslots).reshape(n_dp, entries)
    before = (
        jnp.arange(entries, dtype=jnp.int32)[:, None] < jnp.arange(entries, dtype=jnp.int32)[None, :]
    ).astype(jnp.bfloat16)
    mine_out = source == dev_dp
    rank_out = jnp.dot(
        mine_out.astype(jnp.bfloat16), before, preferred_element_type=jnp.float32
    ).astype(jnp.int32)
    rank_out = jnp.where(mine_out, rank_out, capacity)
    hit = rank_out[:, None, :] == jnp.arange(capacity, dtype=jnp.int32)[None, :, None]
    send_rows = jnp.sum(jnp.where(hit, row[:, None, :], 0), axis=2)
    my_source = lax.dynamic_index_in_dim(source, dev_dp, 0, keepdims=False)
    source_hot = my_source[None, :] == jnp.arange(n_dp, dtype=jnp.int32)[:, None]
    rank_in = jnp.dot(
        source_hot.astype(jnp.bfloat16), before, preferred_element_type=jnp.float32
    ).astype(jnp.int32)
    my_rank = jnp.sum(jnp.where(source_hot, rank_in, 0), axis=0)
    pick = jnp.where(my_source < n_dp, my_source * capacity + my_rank, 0)
    my_len = lax.dynamic_slice_in_dim(len_slot, dev_dp * req_dev, req_dev)
    return send_rows, pick, my_len


def per_device(
    kv_pool,
    page_loc,
    lengths,
    placement,
    queries,
    new_kv,
    resid_in,
    w_out,
    ffn_gain,
    w_gate,
    w_up,
    w_down,
):
    n_dp = lax.axis_size(DP)
    n_tensor = lax.axis_size(TENSOR)
    dev_dp = lax.axis_index(DP)
    dev_cdp = lax.axis_index(CDP)
    dev_tensor = lax.axis_index(TENSOR)
    core = lax.axis_index("c")
    pslots, _, page_size, width_two = kv_pool.shape
    head_dim = width_two // 2
    n_req = lengths.shape[0]
    req_dev = n_req // n_dp
    max_pages = page_loc.shape[2]
    max_len = max_pages * page_size
    cache_len = max_len + page_size
    n_steps = queries.shape[0]
    hq_dev = queries.shape[2]
    width = ffn_gain.shape[0]
    rows_dev = n_steps * req_dev
    rows_all = n_steps * n_req
    capacity = pslots // n_dp

    send_rows, pick, my_len = page_plan(
        page_loc, lengths, placement, dev_dp, dev_tensor, n_dp, pslots, page_size
    )
    outgoing = gather_pages(
        send_rows.reshape(-1), kv_pool.reshape(pslots, page_size, width_two)
    ).reshape(n_dp, capacity, page_size, width_two)
    received = lax.all_to_all(outgoing, DP, 0, 0, tiled=True)
    query = jnp.transpose(queries, (1, 0, 2, 3)).reshape(req_dev, n_steps * hq_dev, head_dim)
    cache, mixed_copies = intake(
        pick,
        my_len,
        received.reshape(pslots, page_size, width_two),
        new_kv.reshape(n_steps, req_dev, width_two).astype(jnp.float32),
        query,
        n_dp,
    )

    mixed_all = lax.all_to_all(mixed_copies, CDP, 0, 0, tiled=True).reshape(
        rows_all, hq_dev * head_dim
    )
    partial_out = jnp.dot(mixed_all, w_out, preferred_element_type=jnp.float32).astype(jnp.bfloat16)
    rows_blk = rows_all // n_tensor
    cols_blk = width // n_dp
    parts = lax.all_to_all(
        partial_out.reshape(n_tensor, rows_blk, cols_blk), TENSOR, 0, 0, tiled=True
    )
    resid_rows = jnp.transpose(
        resid_in.reshape(n_steps, n_dp // 2, 2, req_dev, cols_blk), (2, 1, 0, 3, 4)
    ).reshape(n_tensor, rows_blk, cols_blk)
    resid_blk = lax.dynamic_index_in_dim(resid_rows, dev_tensor, 0, keepdims=False)
    hidden_blk = (
        resid_blk.astype(jnp.float32) + jnp.sum(parts.astype(jnp.float32), axis=0)
    ).astype(jnp.bfloat16)
    chips_dp = n_dp // 2
    own_half = to_all(hidden_blk, CHIPS, chips_dp * n_tensor).reshape(chips_dp, rows_all, cols_blk)
    other_half = lax.ppermute(own_half, "c", [(0, 1), (1, 0)])
    core_at = core.reshape(1).astype(jnp.int32)
    gate_rows = jnp.swapaxes(w_gate, 0, 1)
    up_rows = jnp.swapaxes(w_up, 0, 1)
    gain_row = ffn_gain.reshape(1, width)
    width_out = width // n_tensor
    sums = expand_own(core_at, own_half, gate_rows, up_rows, gain_row)
    act, theirs = expand_other(
        core_at, other_half, gate_rows, up_rows, gain_row, sums, w_down, n_tensor, rows_dev
    )
    from_core = lax.ppermute(theirs, "c", [(0, 1), (1, 0)])
    ours = shrink_own(core_at, act, w_down, n_tensor, rows_dev)
    chip_sum = add_cores(ours, from_core).reshape(chips_dp * n_tensor, rows_dev, width_out)
    pieces = lax.all_to_all(chip_sum, CHIPS, 0, 0, tiled=True)
    ffn_part = jnp.sum(pieces.astype(jnp.float32), axis=0)

    def own_cols(half):
        return lax.dynamic_slice(
            half, (dev_tensor, dev_cdp * rows_dev, 0), (1, rows_dev, cols_blk)
        )[0]

    mine, partners = own_cols(own_half), own_cols(other_half)
    own_hidden = jnp.concatenate(
        [jnp.where(core == 0, mine, partners), jnp.where(core == 0, partners, mine)], axis=1
    )
    block_out = (own_hidden.astype(jnp.float32) + ffn_part).astype(jnp.bfloat16)
    return (block_out.reshape(n_steps, req_dev, width_out), cache.reshape(1, req_dev, cache_len, width_two))


def solution(mesh):
    fine = Mesh(mesh.devices.reshape(2, 4, 2, 4, 2), ("yh", "x", "c", "z", "yl"))
    placed = (
        P(DP, TENSOR, None, None),
        P(),
        P(),
        P(),
        P(None, DP, TENSOR, None),
        P(None, DP, TENSOR, None),
        P(None, None, DP),
        P(TENSOR, DP),
        P(),
        P(None, DP + TENSOR),
        P(None, DP + TENSOR),
        P(DP + TENSOR, None),
    )
    return jax.shard_map(
        per_device,
        mesh=fine,
        in_specs=placed,
        out_specs=(P(None, DP, TENSOR), P(TENSOR, DP, None, None)),
        check_vma=False,
    )
```

```python
import math

import jax
import jax.numpy as jnp
from jax import lax
from jax.experimental import pallas as pl
from jax.experimental.pallas import tpu as pltpu
from jax.sharding import Mesh, PartitionSpec as P

DP = ("yh", "x", "c")
CHIP_DP = ("yh", "x")
TENSOR = ("z", "yl")
CHIPS = ("yh", "x", "z", "yl")


def to_all(block, axes, count):
    copies = lax.optimization_barrier(jnp.broadcast_to(block[None], (count,) + block.shape))
    return lax.all_to_all(copies, axes, 0, 0, tiled=True)

MIB = 1024 * 1024
SMEM = pl.BlockSpec(memory_space=pltpu.SMEM)
VMEM = pl.BlockSpec(memory_space=pltpu.VMEM)
HBM = pl.BlockSpec(memory_space=pltpu.HBM)


def intake(pick, lens, received, fresh, query, n_copies):
    req_dev, n_rows, head_dim = query.shape
    n_steps = fresh.shape[0]
    _, page_size, width_two = received.shape
    max_pages = pick.shape[0] // req_dev
    pages = max_pages + 1
    group = n_rows // n_steps
    scale = 1.0 / math.sqrt(head_dim)
    ahead = 2

    def kernel(pick_ref, len_ref, recv_ref, fresh_ref, q_ref, cache_ref, mixed_ref, buf, heads, in_sems, out_sems):
        def start(r):
            def body(p, carry):
                pltpu.make_async_copy(
                    recv_ref.at[pick_ref[r * max_pages + p]], buf.at[r, p], in_sems.at[r]
                ).start()
                return carry

            lax.fori_loop(0, max_pages, body, 0, unroll=8)

        def copy_out(r):
            return pltpu.make_async_copy(buf.at[r], cache_ref.at[r], out_sems.at[r])

        for r in range(ahead):
            start(r)
        row_at = lax.broadcasted_iota(jnp.int32, (page_size, width_two), 0)
        for r in range(req_dev):
            if r + ahead < req_dev:
                start(r + ahead)
            pltpu.make_async_copy(
                recv_ref.at[pl.ds(0, max_pages)], buf.at[r, pl.ds(0, max_pages)], in_sems.at[r]
            ).wait()
            length = len_ref[r]
            full = length // page_size

            def clear(p, carry):
                buf[r, p] = jnp.zeros((page_size, width_two), buf.dtype)
                return carry

            lax.fori_loop(full + 1, pages, clear, 0)
            edge = buf[r, full].astype(jnp.float32)
            buf[r, full] = jnp.where(row_at < length % page_size, edge, 0.0).astype(buf.dtype)
            for s in range(n_steps):
                at = length + s
                page = buf[r, at // page_size].astype(jnp.float32)
                token = fresh_ref[s, r : r + 1, :]
                buf[r, at // page_size] = jnp.where(
                    row_at == at % page_size, token, page
                ).astype(buf.dtype)
            copy_out(r).start()
            tokens = buf[r].reshape(pages * page_size, width_two)
            scores = scale * lax.dot_general(
                q_ref[r],
                tokens[:, :head_dim],
                (((1,), (1,)), ((), ())),
                preferred_element_type=jnp.float32,
            )
            last = length + lax.broadcasted_iota(jnp.int32, scores.shape, 0) // group
            scores = jnp.where(
                lax.broadcasted_iota(jnp.int32, scores.shape, 1) <= last, scores, -jnp.inf
            )
            expo = jnp.exp(scores - jnp.max(scores, axis=1, keepdims=True))
            total = jnp.sum(expo, axis=1, keepdims=True)
            probs = (expo / total).astype(jnp.bfloat16)
            head_out = jnp.dot(probs, tokens[:, head_dim:], preferred_element_type=jnp.float32)
            for i in range(n_rows):
                heads[i, r : r + 1, :] = head_out[i : i + 1, :]
        for g in range(group):
            block = jnp.concatenate([heads[s * group + g] for s in range(n_steps)], axis=0)
            block = block.astype(mixed_ref.dtype)
            for k in range(n_copies):
                mixed_ref[k, :, g * head_dim : (g + 1) * head_dim] = block
        for r in range(req_dev):
            copy_out(r).wait()

    return pl.pallas_call(
        kernel,
        in_specs=[SMEM, SMEM, HBM, VMEM, VMEM],
        out_specs=[HBM, VMEM],
        out_shape=[
            jax.ShapeDtypeStruct((req_dev, pages, page_size, width_two), received.dtype),
            jax.ShapeDtypeStruct(
                (n_copies, n_steps * req_dev, group * head_dim), received.dtype
            ),
        ],
        scratch_shapes=[
            pltpu.VMEM((req_dev, pages, page_size, width_two), received.dtype),
            pltpu.VMEM((n_rows, req_dev, head_dim), jnp.float32),
            pltpu.SemaphoreType.DMA((req_dev,)),
            pltpu.SemaphoreType.DMA((req_dev,)),
        ],
        compiler_params=pltpu.CompilerParams(vmem_limit_bytes=10 * MIB),
        name="intake",
    )(pick, lens, received, fresh, query)


def feed_forward(hidden, gate_rows, up_rows, gain_row, w_down, n_tensor, rows_dev):
    blocks, rows, cols = hidden.shape
    units, width = w_down.shape
    cols_out = width // n_tensor
    chips = rows // rows_dev
    contract = (((1,), (1,)), ((), ()))

    def kernel(x_ref, gate_ref, up_ref, gain_ref, down_ref, out_ref, scaled):
        squares = 0.0
        for i in range(blocks):
            wide = x_ref[i].astype(jnp.float32)
            square = wide * wide
            squares += sum(square[:, k * 128 : (k + 1) * 128] for k in range(cols // 128))
            scaled[:, i * cols : (i + 1) * cols] = (
                wide * gain_ref[:, i * cols : (i + 1) * cols]
            ).astype(scaled.dtype)
        inverse = lax.rsqrt(jnp.sum(squares, axis=1, keepdims=True) * (1.0 / width) + 1e-05)
        gate = inverse * lax.dot_general(
            scaled[...], gate_ref[...], contract, preferred_element_type=jnp.float32
        )
        upper = inverse * lax.dot_general(
            scaled[...], up_ref[...], contract, preferred_element_type=jnp.float32
        )
        act = (gate / (1.0 + jnp.exp(-gate)) * upper).astype(jnp.bfloat16)
        for t in range(n_tensor):
            out = jnp.dot(
                act,
                down_ref[:, t * cols_out : (t + 1) * cols_out],
                preferred_element_type=jnp.float32,
            )
            out_ref[:, t] = out.astype(out_ref.dtype).reshape(chips, rows_dev, cols_out)

    return pl.pallas_call(
        kernel,
        in_specs=[VMEM] * 5,
        out_specs=VMEM,
        out_shape=jax.ShapeDtypeStruct((chips, n_tensor, rows_dev, cols_out), jnp.bfloat16),
        scratch_shapes=[pltpu.VMEM((rows, width), jnp.bfloat16)],
        compiler_params=pltpu.CompilerParams(vmem_limit_bytes=24 * MIB),
        name="feed_forward",
    )(hidden, gate_rows, up_rows, gain_row, w_down)


def gather_pages(rows, pool, parts):
    count = rows.shape[0]
    span = count // parts
    ahead = 3

    def kernel(rows_ref, pool_ref, out_ref, buf, in_sems, out_sems):
        def start(d):
            def body(k, carry):
                at = d * span + k
                pltpu.make_async_copy(
                    pool_ref.at[rows_ref[at]], buf.at[at], in_sems.at[d]
                ).start()
                return carry

            lax.fori_loop(0, span, body, 0, unroll=8)

        def copy_out(d):
            part = pl.ds(d * span, span)
            return pltpu.make_async_copy(buf.at[part], out_ref.at[part], out_sems.at[d])

        for d in range(ahead):
            start(d)
        for d in range(parts):
            if d + ahead < parts:
                start(d + ahead)
            part = pl.ds(d * span, span)
            pltpu.make_async_copy(pool_ref.at[part], buf.at[part], in_sems.at[d]).wait()
            copy_out(d).start()
        for d in range(parts):
            copy_out(d).wait()

    return pl.pallas_call(
        kernel,
        in_specs=[SMEM, HBM],
        out_specs=HBM,
        out_shape=pltpu.HBM((count,) + pool.shape[1:], pool.dtype),
        scratch_shapes=[
            pltpu.VMEM((count,) + pool.shape[1:], pool.dtype),
            pltpu.SemaphoreType.DMA((parts,)),
            pltpu.SemaphoreType.DMA((parts,)),
        ],
        compiler_params=pltpu.CompilerParams(vmem_limit_bytes=10 * MIB),
        name="gather_pages",
    )(rows, pltpu.with_memory_space_constraint(pool, pltpu.HBM))


def add_cores(ours, from_core):
    chips = ours.shape[0]

    def kernel(a_ref, b_ref, out_ref, buf, sems):
        def copy(i):
            return pltpu.make_async_copy(buf.at[i], out_ref.at[i], sems.at[i])

        for i in range(chips):
            buf[i] = (a_ref[i].astype(jnp.float32) + b_ref[i].astype(jnp.float32)).astype(buf.dtype)
            copy(i).start()
        for i in range(chips):
            copy(i).wait()

    return pl.pallas_call(
        kernel,
        in_specs=[VMEM, VMEM],
        out_specs=HBM,
        out_shape=pltpu.HBM(ours.shape, ours.dtype),
        scratch_shapes=[pltpu.VMEM(ours.shape, ours.dtype), pltpu.SemaphoreType.DMA((chips,))],
        compiler_params=pltpu.CompilerParams(vmem_limit_bytes=12 * MIB),
        name="add_cores",
    )(ours, from_core)


def page_plan(page_loc, lengths, placement, dev_dp, dev_tensor, n_dp, pslots, page_size):
    n_req = lengths.shape[0]
    max_pages = page_loc.shape[2]
    req_dev = n_req // n_dp
    entries = req_dev * max_pages
    capacity = pslots // n_dp
    loc_head = lax.dynamic_index_in_dim(page_loc, dev_tensor, 0, keepdims=False)
    slot_hot = placement[None, :] == jnp.arange(n_req, dtype=jnp.int32)[:, None]
    len_slot = jnp.sum(jnp.where(slot_hot, lengths[None, :], 0), axis=1)
    loc_slot = jnp.dot(
        slot_hot.astype(jnp.float32), loc_head.astype(jnp.float32), precision=lax.Precision.HIGHEST
    ).astype(jnp.int32)
    pages_slot = (len_slot + page_size - 1) // page_size
    live = jnp.arange(max_pages, dtype=jnp.int32)[None, :] < pages_slot[:, None]
    source = jnp.where(live, loc_slot // pslots, n_dp).reshape(n_dp, entries)
    row = (loc_slot % pslots).reshape(n_dp, entries)
    before = (
        jnp.arange(entries, dtype=jnp.int32)[:, None] < jnp.arange(entries, dtype=jnp.int32)[None, :]
    ).astype(jnp.bfloat16)
    mine_out = source == dev_dp
    rank_out = jnp.dot(
        mine_out.astype(jnp.bfloat16), before, preferred_element_type=jnp.float32
    ).astype(jnp.int32)
    rank_out = jnp.where(mine_out, rank_out, capacity)
    hit = rank_out[:, None, :] == jnp.arange(capacity, dtype=jnp.int32)[None, :, None]
    send_rows = jnp.sum(jnp.where(hit, row[:, None, :], 0), axis=2)
    slot = jnp.arange(pslots, dtype=jnp.int32).reshape(n_dp, capacity)
    used = jnp.sum(mine_out.astype(jnp.int32), axis=1, keepdims=True)
    send_rows = jnp.where(slot % capacity < used, send_rows, slot)
    my_source = lax.dynamic_index_in_dim(source, dev_dp, 0, keepdims=False)
    source_hot = my_source[None, :] == jnp.arange(n_dp, dtype=jnp.int32)[:, None]
    rank_in = jnp.dot(
        source_hot.astype(jnp.bfloat16), before, preferred_element_type=jnp.float32
    ).astype(jnp.int32)
    my_rank = jnp.sum(jnp.where(source_hot, rank_in, 0), axis=0)
    pick = jnp.where(
        my_source < n_dp, my_source * capacity + my_rank, jnp.arange(entries, dtype=jnp.int32)
    )
    my_len = lax.dynamic_slice_in_dim(len_slot, dev_dp * req_dev, req_dev)
    return send_rows, pick, my_len


def per_device(
    kv_pool,
    page_loc,
    lengths,
    placement,
    queries,
    new_kv,
    resid_in,
    w_out,
    ffn_gain,
    w_gate,
    w_up,
    w_down,
):
    n_dp = lax.axis_size(DP)
    n_tensor = lax.axis_size(TENSOR)
    dev_dp = lax.axis_index(DP)
    dev_chip = lax.axis_index(CHIP_DP)
    dev_tensor = lax.axis_index(TENSOR)
    core = lax.axis_index("c")
    pslots, _, page_size, width_two = kv_pool.shape
    head_dim = width_two // 2
    n_req = lengths.shape[0]
    req_dev = n_req // n_dp
    max_pages = page_loc.shape[2]
    max_len = max_pages * page_size
    cache_len = max_len + page_size
    n_steps = queries.shape[0]
    hq_dev = queries.shape[2]
    width = ffn_gain.shape[0]
    rows_dev = n_steps * req_dev
    chips_dp = n_dp // 2
    rows_core = n_steps * n_req // 2
    capacity = pslots // n_dp

    send_rows, pick, my_len = page_plan(
        page_loc, lengths, placement, dev_dp, dev_tensor, n_dp, pslots, page_size
    )
    outgoing = gather_pages(
        send_rows.reshape(-1), kv_pool.reshape(pslots, page_size, width_two), n_dp
    ).reshape(n_dp, capacity, page_size, width_two)
    received = lax.all_to_all(outgoing, DP, 0, 0, tiled=True)
    query = jnp.transpose(queries, (1, 0, 2, 3)).reshape(req_dev, n_steps * hq_dev, head_dim)
    cache, mixed_copies = intake(
        pick,
        my_len,
        received.reshape(pslots, page_size, width_two),
        new_kv.reshape(n_steps, req_dev, width_two).astype(jnp.float32),
        query,
        chips_dp,
    )

    cols_dev = width // n_dp
    cols_chip = 2 * cols_dev
    swap = [(0, 1), (1, 0)]

    def both(own, other):
        return jnp.where(
            core == 0,
            jnp.concatenate([own, other], axis=-1),
            jnp.concatenate([other, own], axis=-1),
        )

    w_both = both(w_out, lax.ppermute(w_out, "c", swap))
    resid_rows = jnp.transpose(
        resid_in.reshape(n_steps, chips_dp, 2, req_dev, cols_dev), (2, 1, 0, 3, 4)
    ).reshape(2, n_tensor, rows_core // n_tensor, cols_dev)

    def resid_of(at_core):
        return lax.dynamic_slice(
            resid_rows, (at_core, dev_tensor, 0, 0), (1, 1) + resid_rows.shape[2:]
        )[0, 0]

    resid_blk = both(resid_of(core), lax.ppermute(resid_of(1 - core), "c", swap))
    mixed_rows = lax.all_to_all(mixed_copies, CHIP_DP, 0, 0, tiled=True).reshape(
        rows_core, hq_dev * head_dim
    )
    partial_out = jnp.dot(mixed_rows, w_both, preferred_element_type=jnp.float32).astype(
        jnp.bfloat16
    )
    rows_blk = rows_core // n_tensor
    parts = lax.all_to_all(
        partial_out.reshape(n_tensor, rows_blk, cols_chip), TENSOR, 0, 0, tiled=True
    )
    hidden_blk = (
        resid_blk.astype(jnp.float32) + jnp.sum(parts.astype(jnp.float32), axis=0)
    ).astype(jnp.bfloat16)
    own_rows = to_all(hidden_blk, CHIPS, chips_dp * n_tensor).reshape(
        chips_dp, rows_core, cols_chip
    )
    other_rows = lax.ppermute(own_rows, "c", swap)
    gate_rows = jnp.swapaxes(w_gate, 0, 1)
    up_rows = jnp.swapaxes(w_up, 0, 1)
    gain_row = ffn_gain.reshape(1, width)
    width_out = width // n_tensor

    def block_of(rows):
        return feed_forward(rows, gate_rows, up_rows, gain_row, w_down, n_tensor, rows_dev)

    ours = block_of(own_rows)
    other_rows, ours = lax.optimization_barrier((other_rows, ours))
    theirs = block_of(other_rows)
    from_core = lax.ppermute(theirs, "c", swap)
    chip_sum = add_cores(ours, from_core).reshape(chips_dp * n_tensor, rows_dev, width_out)
    pieces = lax.all_to_all(chip_sum, CHIPS, 0, 0, tiled=True)
    ffn_part = jnp.sum(pieces.astype(jnp.float32), axis=0)
    own_hidden = lax.dynamic_slice(
        own_rows, (dev_tensor, dev_chip * rows_dev, 0), (1, rows_dev, cols_chip)
    )[0]
    block_out = (own_hidden.astype(jnp.float32) + ffn_part).astype(jnp.bfloat16)
    return (block_out.reshape(n_steps, req_dev, width_out), cache.reshape(1, req_dev, cache_len, width_two))


def solution(mesh):
    fine = Mesh(mesh.devices.reshape(2, 4, 2, 4, 2), ("yh", "x", "c", "z", "yl"))
    placed = (
        P(DP, TENSOR, None, None),
        P(),
        P(),
        P(),
        P(None, DP, TENSOR, None),
        P(None, DP, TENSOR, None),
        P(None, None, DP),
        P(TENSOR, DP),
        P(),
        P(None, DP + TENSOR),
        P(None, DP + TENSOR),
        P(DP + TENSOR, None),
    )
    return jax.shard_map(
        per_device,
        mesh=fine,
        in_specs=placed,
        out_specs=(P(None, DP, TENSOR), P(TENSOR, DP, None, None)),
        check_vma=False,
    )
```

```python
import math

import jax
import jax.numpy as jnp
from jax import lax
from jax.experimental import pallas as pl
from jax.experimental.pallas import tpu as pltpu
from jax.sharding import Mesh, PartitionSpec as P

DP = ("yh", "x", "c")
CHIP_DP = ("yh", "x")
TENSOR = ("z", "yl")
CHIPS = ("yh", "x", "z", "yl")


def to_all(block, axes, count):
    copies = lax.optimization_barrier(jnp.broadcast_to(block[None], (count,) + block.shape))
    return lax.all_to_all(copies, axes, 0, 0, tiled=True)

MIB = 1024 * 1024
SMEM = pl.BlockSpec(memory_space=pltpu.SMEM)
VMEM = pl.BlockSpec(memory_space=pltpu.VMEM)
HBM = pl.BlockSpec(memory_space=pltpu.HBM)


def intake(pick, lens, received, fresh, query, n_copies):
    req_dev, n_rows, head_dim = query.shape
    n_steps = fresh.shape[0]
    _, page_size, width_two = received.shape
    max_pages = pick.shape[0] // req_dev
    pages = max_pages + 1
    group = n_rows // n_steps
    scale = 1.0 / math.sqrt(head_dim)
    parts = 8

    def kernel(pick_ref, len_ref, recv_ref, fresh_ref, q_ref, cache_ref, mixed_ref, recv_buf, buf, heads, in_sems, out_sems):
        def copy_in(i):
            part = pl.ds(i * (recv_ref.shape[0] // parts), recv_ref.shape[0] // parts)
            return pltpu.make_async_copy(recv_ref.at[part], recv_buf.at[part], in_sems.at[i])

        def copy_out(r):
            return pltpu.make_async_copy(buf.at[r], cache_ref.at[r], out_sems.at[r])

        for i in range(parts):
            copy_in(i).start()
        for i in range(parts):
            copy_in(i).wait()
        row_at = lax.broadcasted_iota(jnp.int32, (page_size, width_two), 0)
        for r in range(req_dev):

            def move(p, carry):
                buf[r, p] = recv_buf[pick_ref[r * max_pages + p]]
                return carry

            lax.fori_loop(0, max_pages, move, 0, unroll=16)
            length = len_ref[r]
            full = length // page_size

            def clear(p, carry):
                buf[r, p] = jnp.zeros((page_size, width_two), buf.dtype)
                return carry

            lax.fori_loop(full + 1, pages, clear, 0)
            edge = buf[r, full].astype(jnp.float32)
            buf[r, full] = jnp.where(row_at < length % page_size, edge, 0.0).astype(buf.dtype)
            for s in range(n_steps):
                at = length + s
                page = buf[r, at // page_size].astype(jnp.float32)
                token = fresh_ref[s, r : r + 1, :]
                buf[r, at // page_size] = jnp.where(
                    row_at == at % page_size, token, page
                ).astype(buf.dtype)
            copy_out(r).start()
        for r in range(req_dev):
            length = len_ref[r]
            tokens = buf[r].reshape(pages * page_size, width_two)
            scores = scale * lax.dot_general(
                q_ref[r],
                tokens[:, :head_dim],
                (((1,), (1,)), ((), ())),
                preferred_element_type=jnp.float32,
            )
            last = length + lax.broadcasted_iota(jnp.int32, scores.shape, 0) // group
            scores = jnp.where(
                lax.broadcasted_iota(jnp.int32, scores.shape, 1) <= last, scores, -jnp.inf
            )
            expo = jnp.exp(scores - jnp.max(scores, axis=1, keepdims=True))
            total = jnp.sum(expo, axis=1, keepdims=True)
            probs = (expo / total).astype(jnp.bfloat16)
            head_out = jnp.dot(probs, tokens[:, head_dim:], preferred_element_type=jnp.float32)
            for i in range(n_rows):
                heads[i, r : r + 1, :] = head_out[i : i + 1, :]
        for g in range(group):
            block = jnp.concatenate([heads[s * group + g] for s in range(n_steps)], axis=0)
            block = block.astype(mixed_ref.dtype)
            for k in range(n_copies):
                mixed_ref[k, :, g * head_dim : (g + 1) * head_dim] = block
        for r in range(req_dev):
            copy_out(r).wait()

    return pl.pallas_call(
        kernel,
        in_specs=[SMEM, SMEM, HBM, VMEM, VMEM],
        out_specs=[HBM, VMEM],
        out_shape=[
            jax.ShapeDtypeStruct((req_dev, pages, page_size, width_two), received.dtype),
            jax.ShapeDtypeStruct(
                (n_copies, n_steps * req_dev, group * head_dim), received.dtype
            ),
        ],
        scratch_shapes=[
            pltpu.VMEM(received.shape, received.dtype),
            pltpu.VMEM((req_dev, pages, page_size, width_two), received.dtype),
            pltpu.VMEM((n_rows, req_dev, head_dim), jnp.float32),
            pltpu.SemaphoreType.DMA((parts,)),
            pltpu.SemaphoreType.DMA((req_dev,)),
        ],
        compiler_params=pltpu.CompilerParams(vmem_limit_bytes=16 * MIB),
        name="intake",
    )(pick, lens, pltpu.with_memory_space_constraint(received, pltpu.HBM), fresh, query)


def feed_forward(hidden, gate_rows, up_rows, gain_row, w_down, n_tensor, rows_dev):
    blocks, rows, cols = hidden.shape
    units, width = w_down.shape
    cols_out = width // n_tensor
    chips = rows // rows_dev
    contract = (((1,), (1,)), ((), ()))
    parts = 4
    span = width // parts

    def kernel(x_ref, gate_hbm, up_hbm, gain_ref, down_hbm, out_ref, scaled, gate_buf, up_buf, down_buf, sems):
        def copy(m, i):
            source, buffer = [(gate_hbm, gate_buf), (up_hbm, up_buf), (down_hbm, down_buf)][m]
            part = pl.ds(i * span, span)
            return pltpu.make_async_copy(source.at[:, part], buffer.at[:, part], sems.at[m, i])

        for i in range(parts):
            copy(0, i).start()
            copy(1, i).start()
        for i in range(parts):
            copy(2, i).start()
        squares = 0.0
        gate = 0.0
        upper = 0.0
        for i in range(blocks):
            wide = x_ref[i].astype(jnp.float32)
            square = wide * wide
            squares += sum(square[:, k * 128 : (k + 1) * 128] for k in range(cols // 128))
            scaled[:, i * cols : (i + 1) * cols] = (
                wide * gain_ref[:, i * cols : (i + 1) * cols]
            ).astype(scaled.dtype)
        for i in range(parts):
            part = slice(i * span, (i + 1) * span)
            copy(0, i).wait()
            gate += lax.dot_general(
                scaled[:, part], gate_buf[:, part], contract, preferred_element_type=jnp.float32
            )
            copy(1, i).wait()
            upper += lax.dot_general(
                scaled[:, part], up_buf[:, part], contract, preferred_element_type=jnp.float32
            )
        inverse = lax.rsqrt(jnp.sum(squares, axis=1, keepdims=True) * (1.0 / width) + 1e-05)
        gate = gate * inverse
        upper = upper * inverse
        act = (gate / (1.0 + jnp.exp(-gate)) * upper).astype(jnp.bfloat16)
        for t in range(n_tensor):
            if t % (n_tensor // parts) == 0:
                copy(2, t // (n_tensor // parts)).wait()
            out = jnp.dot(
                act,
                down_buf[:, t * cols_out : (t + 1) * cols_out],
                preferred_element_type=jnp.float32,
            )
            out_ref[:, t] = out.astype(out_ref.dtype).reshape(chips, rows_dev, cols_out)

    return pl.pallas_call(
        kernel,
        in_specs=[VMEM, HBM, HBM, VMEM, HBM],
        out_specs=VMEM,
        out_shape=jax.ShapeDtypeStruct((chips, n_tensor, rows_dev, cols_out), jnp.bfloat16),
        scratch_shapes=[
            pltpu.VMEM((rows, width), jnp.bfloat16),
            pltpu.VMEM((units, width), jnp.bfloat16),
            pltpu.VMEM((units, width), jnp.bfloat16),
            pltpu.VMEM((units, width), jnp.bfloat16),
            pltpu.SemaphoreType.DMA((3, parts)),
        ],
        compiler_params=pltpu.CompilerParams(vmem_limit_bytes=28 * MIB),
        name="feed_forward",
    )(
        hidden,
        pltpu.with_memory_space_constraint(gate_rows, pltpu.HBM),
        pltpu.with_memory_space_constraint(up_rows, pltpu.HBM),
        gain_row,
        pltpu.with_memory_space_constraint(w_down, pltpu.HBM),
    )


def add_pieces(pieces, hidden, n_steps):
    count, rows, cols = pieces.shape
    parts = 8
    span = count // parts

    def kernel(pieces_hbm, hidden_ref, out_ref, buf, sems):
        def copy(i):
            part = pl.ds(i * span, span)
            return pltpu.make_async_copy(pieces_hbm.at[part], buf.at[part], sems.at[i])

        for i in range(parts):
            copy(i).start()
        total = hidden_ref[...].astype(jnp.float32)
        for i in range(parts):
            copy(i).wait()
            total += jnp.sum(buf[i * span : (i + 1) * span].astype(jnp.float32), axis=0)
        out_ref[...] = total.reshape(n_steps, rows // n_steps, cols).astype(out_ref.dtype)

    return pl.pallas_call(
        kernel,
        in_specs=[HBM, VMEM],
        out_specs=VMEM,
        out_shape=jax.ShapeDtypeStruct((n_steps, rows // n_steps, cols), pieces.dtype),
        scratch_shapes=[
            pltpu.VMEM(pieces.shape, pieces.dtype),
            pltpu.SemaphoreType.DMA((parts,)),
        ],
        compiler_params=pltpu.CompilerParams(vmem_limit_bytes=10 * MIB),
        name="add_pieces",
    )(pieces, hidden)


def exact_dot(left, right, contract):
    return lax.dot_general(
        left.astype(jnp.bfloat16),
        right.astype(jnp.bfloat16),
        (contract, ((), ())),
        preferred_element_type=jnp.float32,
    )


def pack_pages(place, page_loc, lengths, placement, pool, n_dp):
    pslots, page_size, width_two = pool.shape
    _, max_pages, n_req = page_loc.shape
    req_dev = n_req // n_dp
    capacity = pslots // n_dp
    low = 32

    def kernel(place_ref, loc_hbm, len_ref, placement_ref, pool_hbm, out_hbm, loc, pool_buf, out_buf, rows_vec, rows, loc_sem, pool_sem, rows_sem, out_sems):
        me = place_ref[0]
        pool_copy = pltpu.make_async_copy(pool_hbm, pool_buf, pool_sem)
        loc_copy = pltpu.make_async_copy(loc_hbm.at[place_ref[1]], loc, loc_sem)
        loc_copy.start()
        pool_copy.start()
        shape = (n_req, n_req)
        down = lax.broadcasted_iota(jnp.int32, shape, 0)
        across = lax.broadcasted_iota(jnp.int32, shape, 1)
        slot_hot = jnp.where(placement_ref[...] == down, 1.0, 0.0)
        lens = jnp.broadcast_to(len_ref[...], (8, n_req))
        loc_copy.wait()
        at = loc[...]
        pieces = jnp.concatenate(
            [at // pslots, at % pslots // low, at % low, lens // low, lens % low], axis=0
        )
        by_slot = exact_dot(pieces.astype(jnp.float32), slot_hot, ((1,), (1,)))
        source = by_slot[:max_pages]
        row = by_slot[max_pages : 2 * max_pages] * low + by_slot[2 * max_pages : 3 * max_pages]
        len_row = by_slot[3 * max_pages : 3 * max_pages + 1] * low + by_slot[3 * max_pages + 8 : 3 * max_pages + 9]
        page_at = lax.broadcasted_iota(jnp.int32, (max_pages, n_req), 0).astype(jnp.float32)
        mine = (page_at * page_size < len_row) & (source == me.astype(jnp.float32))
        ones = jnp.where(mine, 1.0, 0.0)
        earlier = jnp.where(
            lax.broadcasted_iota(jnp.int32, (max_pages, max_pages), 1)
            < lax.broadcasted_iota(jnp.int32, (max_pages, max_pages), 0),
            1.0,
            0.0,
        )
        in_group = jnp.where((down // req_dev == across // req_dev) & (down < across), 1.0, 0.0)
        count = jnp.broadcast_to(jnp.sum(ones, axis=0, keepdims=True), (8, n_req))
        rank = exact_dot(earlier, ones, ((1,), (0,))) + exact_dot(count, in_group, ((1,), (0,)))[:1]
        rank = jnp.where(mine, rank, -1.0)
        found = jnp.concatenate(
            [
                jnp.sum(jnp.where(rank == float(k), row, 0.0), axis=0, keepdims=True)
                for k in range(capacity)
            ],
            axis=0,
        ).astype(jnp.int32)
        group = jnp.where(down // req_dev == across, 1.0, 0.0)
        high_part = exact_dot((found // low).astype(jnp.float32), group, ((1,), (0,)))
        low_part = exact_dot((found % low).astype(jnp.float32), group, ((1,), (0,)))
        rows_vec[...] = (high_part * low + low_part).astype(jnp.int32)
        rows_copy = pltpu.make_async_copy(rows_vec, rows, rows_sem)
        rows_copy.start()
        rows_copy.wait()
        pool_copy.wait()

        def copy_out(d):
            part = pl.ds(d * capacity, capacity)
            return pltpu.make_async_copy(out_buf.at[part], out_hbm.at[part], out_sems.at[d])

        for d in range(n_dp):

            def move(k, carry):
                out_buf[d * capacity + k] = pool_buf[rows[k, d]]
                return carry

            lax.fori_loop(0, capacity, move, 0, unroll=16)
            copy_out(d).start()
        for d in range(n_dp):
            copy_out(d).wait()

    return pl.pallas_call(
        kernel,
        in_specs=[SMEM, HBM, VMEM, VMEM, HBM],
        out_specs=HBM,
        out_shape=pltpu.HBM(pool.shape, pool.dtype),
        scratch_shapes=[
            pltpu.VMEM((max_pages, n_req), jnp.int32),
            pltpu.VMEM(pool.shape, pool.dtype),
            pltpu.VMEM(pool.shape, pool.dtype),
            pltpu.VMEM((capacity, n_req), jnp.int32),
            pltpu.SMEM((capacity, n_req), jnp.int32),
            pltpu.SemaphoreType.DMA,
            pltpu.SemaphoreType.DMA,
            pltpu.SemaphoreType.DMA,
            pltpu.SemaphoreType.DMA((n_dp,)),
        ],
        compiler_params=pltpu.CompilerParams(vmem_limit_bytes=16 * MIB),
        name="pack_pages",
    )(
        place,
        page_loc,
        lengths,
        placement,
        pltpu.with_memory_space_constraint(pool, pltpu.HBM),
    )


def add_cores(ours, from_core):
    chips = ours.shape[0]

    def kernel(a_ref, b_ref, out_ref, buf, sems):
        def copy(i):
            return pltpu.make_async_copy(buf.at[i], out_ref.at[i], sems.at[i])

        for i in range(chips):
            buf[i] = (a_ref[i].astype(jnp.float32) + b_ref[i].astype(jnp.float32)).astype(buf.dtype)
            copy(i).start()
        for i in range(chips):
            copy(i).wait()

    return pl.pallas_call(
        kernel,
        in_specs=[VMEM, VMEM],
        out_specs=HBM,
        out_shape=pltpu.HBM(ours.shape, ours.dtype),
        scratch_shapes=[pltpu.VMEM(ours.shape, ours.dtype), pltpu.SemaphoreType.DMA((chips,))],
        compiler_params=pltpu.CompilerParams(vmem_limit_bytes=12 * MIB),
        name="add_cores",
    )(ours, from_core)


def page_picks(page_loc, lengths, placement, dev_dp, dev_tensor, n_dp, pslots, page_size):
    n_req = lengths.shape[0]
    max_pages = page_loc.shape[2]
    req_dev = n_req // n_dp
    entries = req_dev * max_pages
    capacity = pslots // n_dp
    loc_head = lax.dynamic_index_in_dim(page_loc, dev_tensor, 0, keepdims=False)
    my_slots = dev_dp * req_dev + jnp.arange(req_dev, dtype=jnp.int32)
    slot_hot = placement[None, :] == my_slots[:, None]
    my_len = jnp.sum(jnp.where(slot_hot, lengths[None, :], 0), axis=1)
    my_loc = jnp.dot(
        slot_hot.astype(jnp.float32), loc_head.astype(jnp.float32), precision=lax.Precision.HIGHEST
    ).astype(jnp.int32)
    pages_slot = (my_len + page_size - 1) // page_size
    live = jnp.arange(max_pages, dtype=jnp.int32)[None, :] < pages_slot[:, None]
    my_source = jnp.where(live, my_loc // pslots, n_dp).reshape(entries)
    before = (
        jnp.arange(entries, dtype=jnp.int32)[:, None] < jnp.arange(entries, dtype=jnp.int32)[None, :]
    ).astype(jnp.bfloat16)
    source_hot = my_source[None, :] == jnp.arange(n_dp, dtype=jnp.int32)[:, None]
    rank_in = jnp.dot(
        source_hot.astype(jnp.bfloat16), before, preferred_element_type=jnp.float32
    ).astype(jnp.int32)
    my_rank = jnp.sum(jnp.where(source_hot, rank_in, 0), axis=0)
    pick = jnp.where(my_source < n_dp, my_source * capacity + my_rank, 0)
    return pick, my_len


def per_device(
    kv_pool,
    page_loc,
    lengths,
    placement,
    queries,
    new_kv,
    resid_in,
    w_out,
    ffn_gain,
    w_gate,
    w_up,
    w_down,
):
    n_dp = lax.axis_size(DP)
    n_tensor = lax.axis_size(TENSOR)
    dev_dp = lax.axis_index(DP)
    dev_chip = lax.axis_index(CHIP_DP)
    dev_tensor = lax.axis_index(TENSOR)
    core = lax.axis_index("c")
    pslots, _, page_size, width_two = kv_pool.shape
    head_dim = width_two // 2
    n_req = lengths.shape[0]
    req_dev = n_req // n_dp
    max_pages = page_loc.shape[2]
    max_len = max_pages * page_size
    cache_len = max_len + page_size
    n_steps = queries.shape[0]
    hq_dev = queries.shape[2]
    width = ffn_gain.shape[0]
    rows_dev = n_steps * req_dev
    chips_dp = n_dp // 2
    rows_core = n_steps * n_req // 2
    capacity = pslots // n_dp

    outgoing = pack_pages(
        jnp.stack([dev_dp, dev_tensor]).astype(jnp.int32),
        jnp.swapaxes(page_loc, 1, 2),
        lengths.reshape(1, n_req),
        placement.reshape(1, n_req),
        kv_pool.reshape(pslots, page_size, width_two),
        n_dp,
    )
    outgoing, page_loc, lengths, placement = lax.optimization_barrier(
        (outgoing, page_loc, lengths, placement)
    )
    pick, my_len = page_picks(
        page_loc, lengths, placement, dev_dp, dev_tensor, n_dp, pslots, page_size
    )
    outgoing = outgoing.reshape(n_dp, capacity, page_size, width_two)
    received = lax.all_to_all(outgoing, DP, 0, 0, tiled=True)
    query = jnp.transpose(queries, (1, 0, 2, 3)).reshape(req_dev, n_steps * hq_dev, head_dim)
    cache, mixed_copies = intake(
        pick,
        my_len,
        received.reshape(pslots, page_size, width_two),
        new_kv.reshape(n_steps, req_dev, width_two).astype(jnp.float32),
        query,
        chips_dp,
    )

    cols_dev = width // n_dp
    cols_chip = 2 * cols_dev
    swap = [(0, 1), (1, 0)]

    def both(own, other):
        return jnp.where(
            core == 0,
            jnp.concatenate([own, other], axis=-1),
            jnp.concatenate([other, own], axis=-1),
        )

    w_both = both(w_out, lax.ppermute(w_out, "c", swap))
    resid_rows = jnp.transpose(
        resid_in.reshape(n_steps, chips_dp, 2, req_dev, cols_dev), (2, 1, 0, 3, 4)
    ).reshape(2, n_tensor, rows_core // n_tensor, cols_dev)

    def resid_of(at_core):
        return lax.dynamic_slice(
            resid_rows, (at_core, dev_tensor, 0, 0), (1, 1) + resid_rows.shape[2:]
        )[0, 0]

    resid_blk = both(resid_of(core), lax.ppermute(resid_of(1 - core), "c", swap))
    mixed_rows = lax.all_to_all(mixed_copies, CHIP_DP, 0, 0, tiled=True).reshape(
        rows_core, hq_dev * head_dim
    )
    partial_out = jnp.dot(mixed_rows, w_both, preferred_element_type=jnp.float32).astype(
        jnp.bfloat16
    )
    rows_blk = rows_core // n_tensor
    parts = lax.all_to_all(
        partial_out.reshape(n_tensor, rows_blk, cols_chip), TENSOR, 0, 0, tiled=True
    )
    hidden_blk = (
        resid_blk.astype(jnp.float32) + jnp.sum(parts.astype(jnp.float32), axis=0)
    ).astype(jnp.bfloat16)
    own_rows = to_all(hidden_blk, CHIPS, chips_dp * n_tensor).reshape(
        chips_dp, rows_core, cols_chip
    )
    other_rows = lax.ppermute(own_rows, "c", swap)
    gate_rows = jnp.swapaxes(w_gate, 0, 1)
    up_rows = jnp.swapaxes(w_up, 0, 1)
    gain_row = ffn_gain.reshape(1, width)
    width_out = width // n_tensor

    def block_of(rows):
        return feed_forward(rows, gate_rows, up_rows, gain_row, w_down, n_tensor, rows_dev)

    ours = block_of(own_rows)
    other_rows, ours = lax.optimization_barrier((other_rows, ours))
    theirs = block_of(other_rows)
    from_core = lax.ppermute(theirs, "c", swap)
    chip_sum = add_cores(ours, from_core).reshape(chips_dp * n_tensor, rows_dev, width_out)
    pieces = lax.all_to_all(chip_sum, CHIPS, 0, 0, tiled=True)
    own_hidden = lax.dynamic_slice(
        own_rows, (dev_tensor, dev_chip * rows_dev, 0), (1, rows_dev, cols_chip)
    )[0]
    block_out = add_pieces(pieces, own_hidden, n_steps)
    return (block_out, cache.reshape(1, req_dev, cache_len, width_two))


def solution(mesh):
    fine = Mesh(mesh.devices.reshape(2, 4, 2, 4, 2), ("yh", "x", "c", "z", "yl"))
    placed = (
        P(DP, TENSOR, None, None),
        P(),
        P(),
        P(),
        P(None, DP, TENSOR, None),
        P(None, DP, TENSOR, None),
        P(None, None, DP),
        P(TENSOR, DP),
        P(),
        P(None, DP + TENSOR),
        P(None, DP + TENSOR),
        P(DP + TENSOR, None),
    )
    return jax.shard_map(
        per_device,
        mesh=fine,
        in_specs=placed,
        out_specs=(P(None, DP, TENSOR), P(TENSOR, DP, None, None)),
        check_vma=False,
    )
```

```python
import math

import jax
import jax.numpy as jnp
from jax import lax
from jax.experimental import pallas as pl
from jax.experimental.pallas import tpu as pltpu
from jax.sharding import Mesh, PartitionSpec as P

DP = ("yh", "x", "c")
CHIP_DP = ("yh", "x")
TENSOR = ("z", "yl")
CHIPS = ("yh", "x", "z", "yl")


def to_all(block, axes, count):
    copies = lax.optimization_barrier(jnp.broadcast_to(block[None], (count,) + block.shape))
    return lax.all_to_all(copies, axes, 0, 0, tiled=True)

MIB = 1024 * 1024
SMEM = pl.BlockSpec(memory_space=pltpu.SMEM)
VMEM = pl.BlockSpec(memory_space=pltpu.VMEM)
HBM = pl.BlockSpec(memory_space=pltpu.HBM)


def intake(pick, lens, received, fresh, query, n_copies):
    req_dev, n_rows, head_dim = query.shape
    n_steps = fresh.shape[0]
    _, page_size, width_two = received.shape
    max_pages = pick.shape[0] // req_dev
    pages = max_pages + 1
    group = n_rows // n_steps
    scale = 1.0 / math.sqrt(head_dim)
    parts = 4

    def kernel(pick_ref, len_ref, recv_ref, fresh_ref, q_ref, cache_ref, mixed_ref, recv_buf, buf, scores, probs, heads, in_sems, out_sems):
        def copy_out(r):
            return pltpu.make_async_copy(buf.at[r], cache_ref.at[r], out_sems.at[r])

        def copy_in(half, i):
            span = recv_ref.shape[0] // parts
            part = (pl.ds(i * span, span), slice(None), pl.ds(half * head_dim, head_dim))
            return pltpu.make_async_copy(recv_ref.at[part], recv_buf.at[part], in_sems.at[half, i])

        def fill(half, r):
            lanes = slice(half * head_dim, (half + 1) * head_dim)

            def move(p, carry):
                buf[r, p, :, lanes] = recv_buf[pick_ref[r * max_pages + p], :, lanes]
                return carry

            lax.fori_loop(0, max_pages, move, 0, unroll=16)
            length = len_ref[r]
            full = length // page_size

            def clear(p, carry):
                buf[r, p, :, lanes] = jnp.zeros((page_size, head_dim), buf.dtype)
                return carry

            lax.fori_loop(full + 1, pages, clear, 0)
            edge = buf[r, full, :, lanes].astype(jnp.float32)
            buf[r, full, :, lanes] = jnp.where(row_at < length % page_size, edge, 0.0).astype(
                buf.dtype
            )
            for s in range(n_steps):
                at = length + s
                page = buf[r, at // page_size, :, lanes].astype(jnp.float32)
                token = fresh_ref[s, r : r + 1, lanes]
                buf[r, at // page_size, :, lanes] = jnp.where(
                    row_at == at % page_size, token, page
                ).astype(buf.dtype)

        for half in range(2):
            for i in range(parts):
                copy_in(half, i).start()
        row_at = lax.broadcasted_iota(jnp.int32, (page_size, head_dim), 0)
        for i in range(parts):
            copy_in(0, i).wait()
        for r in range(req_dev):
            fill(0, r)
        for r in range(req_dev):
            keys = buf[r, :, :, :head_dim].reshape(pages * page_size, head_dim)
            part = scale * lax.dot_general(
                q_ref[r], keys, (((1,), (1,)), ((), ())), preferred_element_type=jnp.float32
            )
            last = len_ref[r] + lax.broadcasted_iota(jnp.int32, part.shape, 0) // group
            scores[r * n_rows : (r + 1) * n_rows] = jnp.where(
                lax.broadcasted_iota(jnp.int32, part.shape, 1) <= last, part, -jnp.inf
            )
        for i in range(parts):
            copy_in(1, i).wait()
        for r in range(req_dev):
            fill(1, r)
            copy_out(r).start()
        expo = jnp.exp(scores[...] - jnp.max(scores[...], axis=1, keepdims=True))
        probs[...] = (expo / jnp.sum(expo, axis=1, keepdims=True)).astype(probs.dtype)
        for r in range(req_dev):
            values = buf[r, :, :, head_dim:].reshape(pages * page_size, head_dim)
            head_out = jnp.dot(
                probs[r * n_rows : (r + 1) * n_rows], values, preferred_element_type=jnp.float32
            )
            for i in range(n_rows):
                heads[i, r : r + 1, :] = head_out[i : i + 1, :]
        for g in range(group):
            block = jnp.concatenate([heads[s * group + g] for s in range(n_steps)], axis=0)
            block = block.astype(mixed_ref.dtype)
            for k in range(n_copies):
                mixed_ref[k, :, g * head_dim : (g + 1) * head_dim] = block
        for r in range(req_dev):
            copy_out(r).wait()

    return pl.pallas_call(
        kernel,
        in_specs=[SMEM, SMEM, HBM, VMEM, VMEM],
        out_specs=[HBM, VMEM],
        out_shape=[
            jax.ShapeDtypeStruct((req_dev, pages, page_size, width_two), received.dtype),
            jax.ShapeDtypeStruct(
                (n_copies, n_steps * req_dev, group * head_dim), received.dtype
            ),
        ],
        scratch_shapes=[
            pltpu.VMEM(received.shape, received.dtype),
            pltpu.VMEM((req_dev, pages, page_size, width_two), received.dtype),
            pltpu.VMEM((req_dev * n_rows, pages * page_size), jnp.float32),
            pltpu.VMEM((req_dev * n_rows, pages * page_size), jnp.bfloat16),
            pltpu.VMEM((n_rows, req_dev, head_dim), jnp.float32),
            pltpu.SemaphoreType.DMA((2, parts)),
            pltpu.SemaphoreType.DMA((req_dev,)),
        ],
        compiler_params=pltpu.CompilerParams(vmem_limit_bytes=16 * MIB),
        name="intake",
    )(pick, lens, pltpu.with_memory_space_constraint(received, pltpu.HBM), fresh, query)


def feed_forward(hidden, gate_rows, up_rows, gain_row, w_down, n_tensor, rows_dev, keep):
    blocks, rows, cols = hidden.shape
    units, width = w_down.shape
    cols_out = width // n_tensor
    chips = rows // rows_dev
    contract = (((1,), (1,)), ((), ()))
    parts = 4
    span = width // parts

    def kernel(x_ref, gate_ref, up_in, gain_ref, down_in, out_ref, *rest):
        if keep:
            up_ref, down_ref, scaled, sems = rest
        else:
            up_ref, down_ref, scaled = up_in, down_in, rest[0]

        def copy(m, i):
            source, target = [(up_in, up_ref), (down_in, down_ref)][m]
            part = pl.ds(i * span, span)
            return pltpu.make_async_copy(source.at[:, part], target.at[:, part], sems.at[m, i])

        if keep:
            for m in range(2):
                for i in range(parts):
                    copy(m, i).start()
        squares = 0.0
        for i in range(blocks):
            wide = x_ref[i].astype(jnp.float32)
            square = wide * wide
            squares += sum(square[:, k * 128 : (k + 1) * 128] for k in range(cols // 128))
            scaled[:, i * cols : (i + 1) * cols] = (
                wide * gain_ref[:, i * cols : (i + 1) * cols]
            ).astype(scaled.dtype)
        gate = lax.dot_general(
            scaled[...], gate_ref[...], contract, preferred_element_type=jnp.float32
        )
        if keep:
            upper = 0.0
            for i in range(parts):
                part = slice(i * span, (i + 1) * span)
                copy(0, i).wait()
                upper += lax.dot_general(
                    scaled[:, part], up_ref[:, part], contract, preferred_element_type=jnp.float32
                )
        else:
            upper = lax.dot_general(
                scaled[...], up_ref[...], contract, preferred_element_type=jnp.float32
            )
        inverse = lax.rsqrt(jnp.sum(squares, axis=1, keepdims=True) * (1.0 / width) + 1e-05)
        gate = gate * inverse
        upper = upper * inverse
        act = (gate / (1.0 + jnp.exp(-gate)) * upper).astype(jnp.bfloat16)
        for t in range(n_tensor):
            if keep and t % (n_tensor // parts) == 0:
                copy(1, t // (n_tensor // parts)).wait()
            out = jnp.dot(
                act,
                down_ref[:, t * cols_out : (t + 1) * cols_out],
                preferred_element_type=jnp.float32,
            )
            out_ref[:, t] = out.astype(out_ref.dtype).reshape(chips, rows_dev, cols_out)

    weights = HBM if keep else VMEM
    out_shape = [jax.ShapeDtypeStruct((chips, n_tensor, rows_dev, cols_out), jnp.bfloat16)]
    scratch = [pltpu.VMEM((rows, width), jnp.bfloat16)]
    if keep:
        out_shape += [pltpu.VMEM((units, width), jnp.bfloat16)] * 2
        scratch += [pltpu.SemaphoreType.DMA((2, parts))]
        up_rows = pltpu.with_memory_space_constraint(up_rows, pltpu.HBM)
        w_down = pltpu.with_memory_space_constraint(w_down, pltpu.HBM)
    return pl.pallas_call(
        kernel,
        in_specs=[VMEM, VMEM, weights, VMEM, weights],
        out_specs=[VMEM] * len(out_shape),
        out_shape=out_shape,
        scratch_shapes=scratch,
        compiler_params=pltpu.CompilerParams(vmem_limit_bytes=28 * MIB),
        name="feed_forward",
    )(hidden, gate_rows, up_rows, gain_row, w_down)


def add_pieces(pieces, hidden, n_steps):
    count, rows, cols = pieces.shape
    parts = 4
    span = count // parts

    def kernel(pieces_hbm, hidden_ref, out_ref, buf, sems):
        def copy(i):
            part = pl.ds(i * span, span)
            return pltpu.make_async_copy(pieces_hbm.at[part], buf.at[part], sems.at[i])

        for i in range(parts):
            copy(i).start()
        total = hidden_ref[...].astype(jnp.float32)
        for i in range(parts):
            copy(i).wait()
            total += jnp.sum(buf[i * span : (i + 1) * span].astype(jnp.float32), axis=0)
        out_ref[...] = total.reshape(n_steps, rows // n_steps, cols).astype(out_ref.dtype)

    return pl.pallas_call(
        kernel,
        in_specs=[HBM, VMEM],
        out_specs=VMEM,
        out_shape=jax.ShapeDtypeStruct((n_steps, rows // n_steps, cols), pieces.dtype),
        scratch_shapes=[
            pltpu.VMEM(pieces.shape, pieces.dtype),
            pltpu.SemaphoreType.DMA((parts,)),
        ],
        compiler_params=pltpu.CompilerParams(vmem_limit_bytes=10 * MIB),
        name="add_pieces",
    )(pltpu.with_memory_space_constraint(pieces, pltpu.HBM), hidden)


def exact_dot(left, right, contract):
    return lax.dot_general(
        left.astype(jnp.bfloat16),
        right.astype(jnp.bfloat16),
        (contract, ((), ())),
        preferred_element_type=jnp.float32,
    )


def pack_pages(place, page_loc, lengths, placement, pool, n_dp):
    pslots, page_size, width_two = pool.shape
    _, max_pages, n_req = page_loc.shape
    req_dev = n_req // n_dp
    capacity = pslots // n_dp
    low = 32

    def kernel(place_ref, loc_hbm, len_hbm, placement_hbm, pool_hbm, out_hbm, loc, len_ref, placement_ref, pool_buf, out_buf, rows_vec, rows, loc_sem, len_sem, placement_sem, pool_sem, rows_sem, out_sems):
        me = place_ref[0]
        len_copy = pltpu.make_async_copy(len_hbm, len_ref, len_sem)
        placement_copy = pltpu.make_async_copy(placement_hbm, placement_ref, placement_sem)
        pool_copy = pltpu.make_async_copy(pool_hbm, pool_buf, pool_sem)
        loc_copy = pltpu.make_async_copy(loc_hbm.at[place_ref[1]], loc, loc_sem)
        loc_copy.start()
        len_copy.start()
        placement_copy.start()
        pool_copy.start()
        shape = (n_req, n_req)
        down = lax.broadcasted_iota(jnp.int32, shape, 0)
        across = lax.broadcasted_iota(jnp.int32, shape, 1)
        placement_copy.wait()
        slot_hot = jnp.where(placement_ref[...] == down, 1.0, 0.0)
        len_copy.wait()
        lens = jnp.broadcast_to(len_ref[...], (8, n_req))
        loc_copy.wait()
        at = loc[...]
        pieces = jnp.concatenate(
            [at // pslots, at % pslots // low, at % low, lens // low, lens % low], axis=0
        )
        by_slot = exact_dot(pieces.astype(jnp.float32), slot_hot, ((1,), (1,)))
        source = by_slot[:max_pages]
        row = by_slot[max_pages : 2 * max_pages] * low + by_slot[2 * max_pages : 3 * max_pages]
        len_row = by_slot[3 * max_pages : 3 * max_pages + 1] * low + by_slot[3 * max_pages + 8 : 3 * max_pages + 9]
        page_at = lax.broadcasted_iota(jnp.int32, (max_pages, n_req), 0).astype(jnp.float32)
        mine = (page_at * page_size < len_row) & (source == me.astype(jnp.float32))
        ones = jnp.where(mine, 1.0, 0.0)
        earlier = jnp.where(
            lax.broadcasted_iota(jnp.int32, (max_pages, max_pages), 1)
            < lax.broadcasted_iota(jnp.int32, (max_pages, max_pages), 0),
            1.0,
            0.0,
        )
        in_group = jnp.where((down // req_dev == across // req_dev) & (down < across), 1.0, 0.0)
        count = jnp.broadcast_to(jnp.sum(ones, axis=0, keepdims=True), (8, n_req))
        rank = exact_dot(earlier, ones, ((1,), (0,))) + exact_dot(count, in_group, ((1,), (0,)))[:1]
        rank = jnp.where(mine, rank, -1.0)
        found = jnp.concatenate(
            [
                jnp.sum(jnp.where(rank == float(k), row, 0.0), axis=0, keepdims=True)
                for k in range(capacity)
            ],
            axis=0,
        ).astype(jnp.int32)
        group = jnp.where(down // req_dev == across, 1.0, 0.0)
        high_part = exact_dot((found // low).astype(jnp.float32), group, ((1,), (0,)))
        low_part = exact_dot((found % low).astype(jnp.float32), group, ((1,), (0,)))
        rows_vec[...] = (high_part * low + low_part).astype(jnp.int32)
        rows_copy = pltpu.make_async_copy(rows_vec, rows, rows_sem)
        rows_copy.start()
        rows_copy.wait()
        pool_copy.wait()

        def copy_out(d):
            part = pl.ds(d * capacity, capacity)
            return pltpu.make_async_copy(out_buf.at[part], out_hbm.at[part], out_sems.at[d])

        for d in range(n_dp):

            def move(k, carry):
                out_buf[d * capacity + k] = pool_buf[rows[k, d]]
                return carry

            lax.fori_loop(0, capacity, move, 0, unroll=16)
            copy_out(d).start()
        for d in range(n_dp):
            copy_out(d).wait()

    return pl.pallas_call(
        kernel,
        in_specs=[SMEM, HBM, HBM, HBM, HBM],
        out_specs=HBM,
        out_shape=pltpu.HBM(pool.shape, pool.dtype),
        scratch_shapes=[
            pltpu.VMEM((max_pages, n_req), jnp.int32),
            pltpu.VMEM((1, n_req), jnp.int32),
            pltpu.VMEM((1, n_req), jnp.int32),
            pltpu.VMEM(pool.shape, pool.dtype),
            pltpu.VMEM(pool.shape, pool.dtype),
            pltpu.VMEM((capacity, n_req), jnp.int32),
            pltpu.SMEM((capacity, n_req), jnp.int32),
            pltpu.SemaphoreType.DMA,
            pltpu.SemaphoreType.DMA,
            pltpu.SemaphoreType.DMA,
            pltpu.SemaphoreType.DMA,
            pltpu.SemaphoreType.DMA,
            pltpu.SemaphoreType.DMA((n_dp,)),
        ],
        compiler_params=pltpu.CompilerParams(vmem_limit_bytes=16 * MIB),
        name="pack_pages",
    )(
        place,
        *[
            pltpu.with_memory_space_constraint(array, pltpu.HBM)
            for array in (page_loc, lengths, placement, pool)
        ],
    )


def add_cores(ours, from_core):
    chips = ours.shape[0]

    def kernel(a_ref, b_ref, out_ref, buf, sems):
        def copy(i):
            return pltpu.make_async_copy(buf.at[i], out_ref.at[i], sems.at[i])

        for i in range(chips):
            buf[i] = (a_ref[i].astype(jnp.float32) + b_ref[i].astype(jnp.float32)).astype(buf.dtype)
            copy(i).start()
        for i in range(chips):
            copy(i).wait()

    return pl.pallas_call(
        kernel,
        in_specs=[VMEM, VMEM],
        out_specs=HBM,
        out_shape=pltpu.HBM(ours.shape, ours.dtype),
        scratch_shapes=[pltpu.VMEM(ours.shape, ours.dtype), pltpu.SemaphoreType.DMA((chips,))],
        compiler_params=pltpu.CompilerParams(vmem_limit_bytes=12 * MIB),
        name="add_cores",
    )(ours, from_core)


def page_picks(page_loc, lengths, placement, dev_dp, dev_tensor, n_dp, pslots, page_size):
    n_req = lengths.shape[0]
    max_pages = page_loc.shape[2]
    req_dev = n_req // n_dp
    entries = req_dev * max_pages
    capacity = pslots // n_dp
    loc_head = lax.dynamic_index_in_dim(page_loc, dev_tensor, 0, keepdims=False)
    my_slots = dev_dp * req_dev + jnp.arange(req_dev, dtype=jnp.int32)
    slot_hot = placement[None, :] == my_slots[:, None]
    my_len = jnp.sum(jnp.where(slot_hot, lengths[None, :], 0), axis=1)
    my_loc = jnp.dot(
        slot_hot.astype(jnp.float32), loc_head.astype(jnp.float32), precision=lax.Precision.HIGHEST
    ).astype(jnp.int32)
    pages_slot = (my_len + page_size - 1) // page_size
    live = jnp.arange(max_pages, dtype=jnp.int32)[None, :] < pages_slot[:, None]
    my_source = jnp.where(live, my_loc // pslots, n_dp).reshape(entries)
    before = (
        jnp.arange(entries, dtype=jnp.int32)[:, None] < jnp.arange(entries, dtype=jnp.int32)[None, :]
    ).astype(jnp.bfloat16)
    source_hot = my_source[None, :] == jnp.arange(n_dp, dtype=jnp.int32)[:, None]
    rank_in = jnp.dot(
        source_hot.astype(jnp.bfloat16), before, preferred_element_type=jnp.float32
    ).astype(jnp.int32)
    my_rank = jnp.sum(jnp.where(source_hot, rank_in, 0), axis=0)
    pick = jnp.where(my_source < n_dp, my_source * capacity + my_rank, 0)
    return pick, my_len


def per_device(
    kv_pool,
    page_loc,
    lengths,
    placement,
    queries,
    new_kv,
    resid_in,
    w_out,
    ffn_gain,
    w_gate,
    w_up,
    w_down,
):
    n_dp = lax.axis_size(DP)
    n_tensor = lax.axis_size(TENSOR)
    dev_dp = lax.axis_index(DP)
    dev_chip = lax.axis_index(CHIP_DP)
    dev_tensor = lax.axis_index(TENSOR)
    core = lax.axis_index("c")
    pslots, _, page_size, width_two = kv_pool.shape
    head_dim = width_two // 2
    n_req = lengths.shape[0]
    req_dev = n_req // n_dp
    max_pages = page_loc.shape[2]
    max_len = max_pages * page_size
    cache_len = max_len + page_size
    n_steps = queries.shape[0]
    hq_dev = queries.shape[2]
    width = ffn_gain.shape[0]
    rows_dev = n_steps * req_dev
    chips_dp = n_dp // 2
    rows_core = n_steps * n_req // 2
    capacity = pslots // n_dp

    outgoing = pack_pages(
        jnp.stack([dev_dp, dev_tensor]).astype(jnp.int32),
        jnp.swapaxes(page_loc, 1, 2),
        lengths.reshape(1, n_req),
        placement.reshape(1, n_req),
        kv_pool.reshape(pslots, page_size, width_two),
        n_dp,
    )
    outgoing, page_loc, lengths, placement = lax.optimization_barrier(
        (outgoing, page_loc, lengths, placement)
    )
    pick, my_len = page_picks(
        page_loc, lengths, placement, dev_dp, dev_tensor, n_dp, pslots, page_size
    )
    outgoing = outgoing.reshape(n_dp, capacity, page_size, width_two)
    received = lax.all_to_all(outgoing, DP, 0, 0, tiled=True)
    query = jnp.transpose(queries, (1, 0, 2, 3)).reshape(req_dev, n_steps * hq_dev, head_dim)
    cache, mixed_copies = intake(
        pick,
        my_len,
        received.reshape(pslots, page_size, width_two),
        new_kv.reshape(n_steps, req_dev, width_two).astype(jnp.float32),
        query,
        chips_dp,
    )

    cols_dev = width // n_dp
    cols_chip = 2 * cols_dev
    swap = [(0, 1), (1, 0)]

    def both(own, other):
        return jnp.where(
            core == 0,
            jnp.concatenate([own, other], axis=-1),
            jnp.concatenate([other, own], axis=-1),
        )

    w_both = both(w_out, lax.ppermute(w_out, "c", swap))
    resid_rows = jnp.transpose(
        resid_in.reshape(n_steps, chips_dp, 2, req_dev, cols_dev), (2, 1, 0, 3, 4)
    ).reshape(2, n_tensor, rows_core // n_tensor, cols_dev)

    def resid_of(at_core):
        return lax.dynamic_slice(
            resid_rows, (at_core, dev_tensor, 0, 0), (1, 1) + resid_rows.shape[2:]
        )[0, 0]

    resid_blk = both(resid_of(core), lax.ppermute(resid_of(1 - core), "c", swap))
    mixed_rows = lax.all_to_all(mixed_copies, CHIP_DP, 0, 0, tiled=True).reshape(
        rows_core, hq_dev * head_dim
    )
    partial_out = jnp.dot(mixed_rows, w_both, preferred_element_type=jnp.float32).astype(
        jnp.bfloat16
    )
    rows_blk = rows_core // n_tensor
    parts = lax.all_to_all(
        partial_out.reshape(n_tensor, rows_blk, cols_chip), TENSOR, 0, 0, tiled=True
    )
    hidden_blk = (
        resid_blk.astype(jnp.float32) + jnp.sum(parts.astype(jnp.float32), axis=0)
    ).astype(jnp.bfloat16)
    own_rows = to_all(hidden_blk, CHIPS, chips_dp * n_tensor).reshape(
        chips_dp, rows_core, cols_chip
    )
    other_rows = lax.ppermute(own_rows, "c", swap)
    gate_rows = jnp.swapaxes(w_gate, 0, 1)
    up_rows = jnp.swapaxes(w_up, 0, 1)
    gain_row = ffn_gain.reshape(1, width)
    width_out = width // n_tensor

    ours, up_near, down_near = feed_forward(
        own_rows, gate_rows, up_rows, gain_row, w_down, n_tensor, rows_dev, True
    )
    other_rows, ours = lax.optimization_barrier((other_rows, ours))
    (theirs,) = feed_forward(
        other_rows, gate_rows, up_near, gain_row, down_near, n_tensor, rows_dev, False
    )
    from_core = lax.ppermute(theirs, "c", swap)
    chip_sum = add_cores(ours, from_core).reshape(chips_dp * n_tensor, rows_dev, width_out)
    pieces = lax.all_to_all(chip_sum, CHIPS, 0, 0, tiled=True)
    own_hidden = lax.dynamic_slice(
        own_rows, (dev_tensor, dev_chip * rows_dev, 0), (1, rows_dev, cols_chip)
    )[0]
    block_out = add_pieces(pieces, own_hidden, n_steps)
    return (block_out, cache.reshape(1, req_dev, cache_len, width_two))


def solution(mesh):
    fine = Mesh(mesh.devices.reshape(2, 4, 2, 4, 2), ("yh", "x", "c", "z", "yl"))
    placed = (
        P(DP, TENSOR, None, None),
        P(),
        P(),
        P(),
        P(None, DP, TENSOR, None),
        P(None, DP, TENSOR, None),
        P(None, None, DP),
        P(TENSOR, DP),
        P(),
        P(None, DP + TENSOR),
        P(None, DP + TENSOR),
        P(DP + TENSOR, None),
    )
    return jax.shard_map(
        per_device,
        mesh=fine,
        in_specs=placed,
        out_specs=(P(None, DP, TENSOR), P(TENSOR, DP, None, None)),
        check_vma=False,
    )
```

```python
import math

import jax
import jax.numpy as jnp
from jax import lax
from jax.experimental import pallas as pl
from jax.experimental.pallas import tpu as pltpu
from jax.sharding import Mesh, PartitionSpec as P

DP = ("yh", "x", "c")
CHIP_DP = ("yh", "x")
TENSOR = ("z", "yl")
CHIPS = ("yh", "x", "z", "yl")


def to_all(block, axes, count):
    copies = lax.optimization_barrier(jnp.broadcast_to(block[None], (count,) + block.shape))
    return lax.all_to_all(copies, axes, 0, 0, tiled=True)

MIB = 1024 * 1024
SMEM = pl.BlockSpec(memory_space=pltpu.SMEM)
VMEM = pl.BlockSpec(memory_space=pltpu.VMEM)
HBM = pl.BlockSpec(memory_space=pltpu.HBM)


def intake(pick, received, fresh, query, n_copies):
    req_dev, n_rows, head_dim = query.shape
    n_steps = fresh.shape[0]
    _, page_size, width_two = received.shape
    max_pages = pick.shape[0] - 8
    pages = max_pages + 1
    group = n_rows // n_steps
    scale = 1.0 / math.sqrt(head_dim)
    def kernel(pick_ref, recv_ref, fresh_ref, q_ref, cache_ref, mixed_ref, buf, scores, probs, heads, out_sems):
        def copy_out(r):
            return pltpu.make_async_copy(buf.at[r], cache_ref.at[r], out_sems.at[r])

        row_at = lax.broadcasted_iota(jnp.int32, (page_size, width_two), 0)
        for r in range(req_dev):

            def move(p, carry):
                buf[r, p] = recv_ref[pick_ref[p, r]]
                return carry

            lax.fori_loop(0, max_pages, move, 0, unroll=16)
            length = pick_ref[max_pages, r]
            full = length // page_size

            def clear(p, carry):
                buf[r, p] = jnp.zeros((page_size, width_two), buf.dtype)
                return carry

            lax.fori_loop(full + 1, pages, clear, 0)
            edge = buf[r, full].astype(jnp.float32)
            buf[r, full] = jnp.where(row_at < length % page_size, edge, 0.0).astype(buf.dtype)
            for s in range(n_steps):
                at = length + s
                page = buf[r, at // page_size].astype(jnp.float32)
                token = fresh_ref[s, r : r + 1, :]
                buf[r, at // page_size] = jnp.where(
                    row_at == at % page_size, token, page
                ).astype(buf.dtype)
            copy_out(r).start()
        for r in range(req_dev):
            keys = buf[r, :, :, :head_dim].reshape(pages * page_size, head_dim)
            part = scale * lax.dot_general(
                q_ref[r], keys, (((1,), (1,)), ((), ())), preferred_element_type=jnp.float32
            )
            last = pick_ref[max_pages, r] + lax.broadcasted_iota(jnp.int32, part.shape, 0) // group
            scores[r * n_rows : (r + 1) * n_rows] = jnp.where(
                lax.broadcasted_iota(jnp.int32, part.shape, 1) <= last, part, -jnp.inf
            )
        expo = jnp.exp(scores[...] - jnp.max(scores[...], axis=1, keepdims=True))
        probs[...] = (expo / jnp.sum(expo, axis=1, keepdims=True)).astype(probs.dtype)
        for r in range(req_dev):
            values = buf[r, :, :, head_dim:].reshape(pages * page_size, head_dim)
            head_out = jnp.dot(
                probs[r * n_rows : (r + 1) * n_rows], values, preferred_element_type=jnp.float32
            )
            for i in range(n_rows):
                heads[i, r : r + 1, :] = head_out[i : i + 1, :]
        for g in range(group):
            block = jnp.concatenate([heads[s * group + g] for s in range(n_steps)], axis=0)
            block = block.astype(mixed_ref.dtype)
            for k in range(n_copies):
                mixed_ref[k, :, g * head_dim : (g + 1) * head_dim] = block
        for r in range(req_dev):
            copy_out(r).wait()

    return pl.pallas_call(
        kernel,
        in_specs=[SMEM, VMEM, VMEM, VMEM],
        out_specs=[HBM, VMEM],
        out_shape=[
            jax.ShapeDtypeStruct((req_dev, pages, page_size, width_two), received.dtype),
            jax.ShapeDtypeStruct(
                (n_copies, n_steps * req_dev, group * head_dim), received.dtype
            ),
        ],
        scratch_shapes=[
            pltpu.VMEM((req_dev, pages, page_size, width_two), received.dtype),
            pltpu.VMEM((req_dev * n_rows, pages * page_size), jnp.float32),
            pltpu.VMEM((req_dev * n_rows, pages * page_size), jnp.bfloat16),
            pltpu.VMEM((n_rows, req_dev, head_dim), jnp.float32),
            pltpu.SemaphoreType.DMA((req_dev,)),
        ],
        compiler_params=pltpu.CompilerParams(vmem_limit_bytes=20 * MIB),
        name="intake",
    )(pick, received, fresh, query)


def feed_forward(hidden, gate_rows, up_rows, gain_row, w_down, n_tensor, rows_dev, place=None):
    keep = place is not None
    blocks, rows, cols = hidden.shape
    units, width = w_down.shape
    cols_out = width // n_tensor
    chips = rows // rows_dev
    contract = (((1,), (1,)), ((), ()))
    parts = 4
    span = width // parts

    def kernel(x_ref, gate_ref, up_in, gain_ref, down_in, out_ref, *rest):
        if keep:
            place_ref, out_ref, up_ref, down_ref, part_ref, scaled, sems = (out_ref,) + rest
        else:
            up_ref, down_ref, scaled = up_in, down_in, rest[0]

        def copy(m, i):
            source, target = [(up_in, up_ref), (down_in, down_ref)][m]
            part = pl.ds(i * span, span)
            return pltpu.make_async_copy(source.at[:, part], target.at[:, part], sems.at[m, i])

        if keep:
            for m in range(2):
                for i in range(parts):
                    copy(m, i).start()
            mine = pl.ds(pl.multiple_of(place_ref[2] * rows_dev, rows_dev), rows_dev)
            part_ref[...] = x_ref[place_ref[1], mine, :]
        squares = 0.0
        for i in range(blocks):
            wide = x_ref[i].astype(jnp.float32)
            square = wide * wide
            squares += sum(square[:, k * 128 : (k + 1) * 128] for k in range(cols // 128))
            scaled[:, i * cols : (i + 1) * cols] = (
                wide * gain_ref[:, i * cols : (i + 1) * cols]
            ).astype(scaled.dtype)
        gate = lax.dot_general(
            scaled[...], gate_ref[...], contract, preferred_element_type=jnp.float32
        )
        if keep:
            upper = 0.0
            for i in range(parts):
                part = slice(i * span, (i + 1) * span)
                copy(0, i).wait()
                upper += lax.dot_general(
                    scaled[:, part], up_ref[:, part], contract, preferred_element_type=jnp.float32
                )
        else:
            upper = lax.dot_general(
                scaled[...], up_ref[...], contract, preferred_element_type=jnp.float32
            )
        inverse = lax.rsqrt(jnp.sum(squares, axis=1, keepdims=True) * (1.0 / width) + 1e-05)
        gate = gate * inverse
        upper = upper * inverse
        act = (gate / (1.0 + jnp.exp(-gate)) * upper).astype(jnp.bfloat16)
        for t in range(n_tensor):
            if keep and t % (n_tensor // parts) == 0:
                copy(1, t // (n_tensor // parts)).wait()
            out = jnp.dot(
                act,
                down_ref[:, t * cols_out : (t + 1) * cols_out],
                preferred_element_type=jnp.float32,
            )
            out_ref[:, t] = out.astype(out_ref.dtype).reshape(chips, rows_dev, cols_out)

    weights = HBM if keep else VMEM
    out_shape = [jax.ShapeDtypeStruct((chips, n_tensor, rows_dev, cols_out), jnp.bfloat16)]
    scratch = [pltpu.VMEM((rows, width), jnp.bfloat16)]
    if keep:
        out_shape += [pltpu.VMEM((units, width), jnp.bfloat16)] * 2
        out_shape += [jax.ShapeDtypeStruct((rows_dev, cols), hidden.dtype)]
        scratch += [pltpu.SemaphoreType.DMA((2, parts))]
        up_rows = pltpu.with_memory_space_constraint(up_rows, pltpu.HBM)
        w_down = pltpu.with_memory_space_constraint(w_down, pltpu.HBM)
    return pl.pallas_call(
        kernel,
        in_specs=[VMEM, VMEM, weights, VMEM, weights] + [SMEM] * keep,
        out_specs=[VMEM] * len(out_shape),
        out_shape=out_shape,
        scratch_shapes=scratch,
        compiler_params=pltpu.CompilerParams(vmem_limit_bytes=28 * MIB),
        name="feed_forward",
    )(hidden, gate_rows, up_rows, gain_row, w_down, *([place] if keep else []))


def add_pieces(pieces, hidden, n_steps):
    count, rows, cols = pieces.shape

    def kernel(pieces_ref, hidden_ref, out_ref):
        total = hidden_ref[...].astype(jnp.float32)
        for i in range(count):
            total += pieces_ref[i].astype(jnp.float32)
        out_ref[...] = total.reshape(n_steps, rows // n_steps, cols).astype(out_ref.dtype)

    return pl.pallas_call(
        kernel,
        in_specs=[VMEM, VMEM],
        out_specs=VMEM,
        out_shape=jax.ShapeDtypeStruct((n_steps, rows // n_steps, cols), pieces.dtype),
        compiler_params=pltpu.CompilerParams(vmem_limit_bytes=10 * MIB),
        name="add_pieces",
    )(pieces, hidden)


def exact_dot(left, right, contract):
    return lax.dot_general(
        left.astype(jnp.bfloat16),
        right.astype(jnp.bfloat16),
        (contract, ((), ())),
        preferred_element_type=jnp.float32,
    )


def pack_pages(place, page_loc, lengths, placement, pool, n_dp):
    pslots, page_size, width_two = pool.shape
    _, max_pages, n_req = page_loc.shape
    req_dev = n_req // n_dp
    capacity = pslots // n_dp
    low = 32

    def kernel(place_ref, loc_hbm, len_hbm, placement_hbm, pool_hbm, out_buf, pick_ref, loc, len_ref, placement_ref, pool_buf, rows_vec, rows, loc_sem, len_sem, placement_sem, pool_sem, rows_sem):
        me = place_ref[0]
        len_copy = pltpu.make_async_copy(len_hbm, len_ref, len_sem)
        placement_copy = pltpu.make_async_copy(placement_hbm, placement_ref, placement_sem)
        pool_copy = pltpu.make_async_copy(pool_hbm, pool_buf, pool_sem)
        loc_copy = pltpu.make_async_copy(loc_hbm.at[place_ref[1]], loc, loc_sem)
        loc_copy.start()
        len_copy.start()
        placement_copy.start()
        pool_copy.start()
        shape = (n_req, n_req)
        down = lax.broadcasted_iota(jnp.int32, shape, 0)
        across = lax.broadcasted_iota(jnp.int32, shape, 1)
        placement_copy.wait()
        slot_hot = jnp.where(placement_ref[...] == down, 1.0, 0.0)
        len_copy.wait()
        lens = jnp.broadcast_to(len_ref[...], (8, n_req))
        loc_copy.wait()
        at = loc[...]
        pieces = jnp.concatenate(
            [at // pslots, at % pslots // low, at % low, lens // low, lens % low], axis=0
        )
        by_slot = exact_dot(pieces.astype(jnp.float32), slot_hot, ((1,), (1,)))
        source = by_slot[:max_pages]
        row = by_slot[max_pages : 2 * max_pages] * low + by_slot[2 * max_pages : 3 * max_pages]
        len_row = by_slot[3 * max_pages : 3 * max_pages + 1] * low + by_slot[3 * max_pages + 8 : 3 * max_pages + 9]
        page_at = lax.broadcasted_iota(jnp.int32, (max_pages, n_req), 0).astype(jnp.float32)
        source = jnp.where(page_at * page_size < len_row, source, float(n_dp))
        mine = source == me.astype(jnp.float32)
        ones = jnp.where(mine, 1.0, 0.0)
        earlier = jnp.where(
            lax.broadcasted_iota(jnp.int32, (max_pages, max_pages), 1)
            < lax.broadcasted_iota(jnp.int32, (max_pages, max_pages), 0),
            1.0,
            0.0,
        )
        in_group = jnp.where((down // req_dev == across // req_dev) & (down < across), 1.0, 0.0)
        count = jnp.broadcast_to(jnp.sum(ones, axis=0, keepdims=True), (8, n_req))
        rank = exact_dot(earlier, ones, ((1,), (0,))) + exact_dot(count, in_group, ((1,), (0,)))[:1]
        rank = jnp.where(mine, rank, -1.0)
        found = jnp.concatenate(
            [
                jnp.sum(jnp.where(rank == float(k), row, 0.0), axis=0, keepdims=True)
                for k in range(capacity)
            ],
            axis=0,
        ).astype(jnp.int32)
        group = jnp.where(down // req_dev == across, 1.0, 0.0)
        high_part = exact_dot((found // low).astype(jnp.float32), group, ((1,), (0,)))
        low_part = exact_dot((found % low).astype(jnp.float32), group, ((1,), (0,)))
        rows_vec[...] = (high_part * low + low_part).astype(jnp.int32)
        rows_copy = pltpu.make_async_copy(rows_vec, rows, rows_sem)
        rows_copy.start()
        own = jnp.where(down == me * req_dev + across % req_dev, 1.0, 0.0)
        ahead = jnp.concatenate([source, jnp.floor(len_row * (1.0 / low)), len_row - jnp.floor(len_row * (1.0 / low)) * low], axis=0)
        ahead = jnp.concatenate([ahead, jnp.zeros((6, n_req), jnp.float32)], axis=0)
        own_cols = exact_dot(ahead, own, ((1,), (0,)))
        lane = lax.broadcasted_iota(jnp.int32, (max_pages, n_req), 1)
        hit = own_cols[:max_pages] == (lane // req_dev).astype(jnp.float32)
        ones = jnp.where(hit, 1.0, 0.0)
        count = jnp.broadcast_to(jnp.sum(ones, axis=0, keepdims=True), (8, n_req))
        rank = exact_dot(earlier, ones, ((1,), (0,))) + exact_dot(count, in_group, ((1,), (0,)))[:1]
        spot = jnp.where(hit, rank + 1.0, 0.0)
        requests = jnp.where(down % req_dev == across, 1.0, 0.0)
        base = jnp.where(hit, (lane // req_dev).astype(jnp.float32), 0.0)
        pick = exact_dot(base, requests, ((1,), (0,))) * capacity
        pick += exact_dot(spot, requests, ((1,), (0,))) - 1.0
        own_len = own_cols[max_pages : max_pages + 1] * low + own_cols[max_pages + 1 : max_pages + 2]
        pick_ref[:max_pages] = jnp.maximum(pick, 0.0).astype(jnp.int32)
        pick_ref[max_pages:] = jnp.broadcast_to(own_len, (8, n_req)).astype(jnp.int32)
        rows_copy.wait()
        pool_copy.wait()

        for d in range(n_dp):

            def move(k, carry):
                out_buf[d * capacity + k] = pool_buf[rows[k, d]]
                return carry

            lax.fori_loop(0, capacity, move, 0, unroll=16)

    return pl.pallas_call(
        kernel,
        in_specs=[SMEM, HBM, HBM, HBM, HBM],
        out_specs=[VMEM, VMEM],
        out_shape=[
            jax.ShapeDtypeStruct(pool.shape, pool.dtype),
            jax.ShapeDtypeStruct((max_pages + 8, n_req), jnp.int32),
        ],
        scratch_shapes=[
            pltpu.VMEM((max_pages, n_req), jnp.int32),
            pltpu.VMEM((1, n_req), jnp.int32),
            pltpu.VMEM((1, n_req), jnp.int32),
            pltpu.VMEM(pool.shape, pool.dtype),
            pltpu.VMEM((capacity, n_req), jnp.int32),
            pltpu.SMEM((capacity, n_req), jnp.int32),
            pltpu.SemaphoreType.DMA,
            pltpu.SemaphoreType.DMA,
            pltpu.SemaphoreType.DMA,
            pltpu.SemaphoreType.DMA,
            pltpu.SemaphoreType.DMA,
        ],
        compiler_params=pltpu.CompilerParams(vmem_limit_bytes=20 * MIB),
        name="pack_pages",
    )(
        place,
        *[
            pltpu.with_memory_space_constraint(array, pltpu.HBM)
            for array in (page_loc, lengths, placement, pool)
        ],
    )


def add_cores(ours, from_core):
    def kernel(a_ref, b_ref, out_ref):
        for i in range(ours.shape[0]):
            out_ref[i] = (a_ref[i].astype(jnp.float32) + b_ref[i].astype(jnp.float32)).astype(
                out_ref.dtype
            )

    return pl.pallas_call(
        kernel,
        in_specs=[VMEM, VMEM],
        out_specs=VMEM,
        out_shape=jax.ShapeDtypeStruct(ours.shape, ours.dtype),
        compiler_params=pltpu.CompilerParams(vmem_limit_bytes=12 * MIB),
        name="add_cores",
    )(ours, from_core)


def per_device(
    kv_pool,
    page_loc,
    lengths,
    placement,
    queries,
    new_kv,
    resid_in,
    w_out,
    ffn_gain,
    w_gate,
    w_up,
    w_down,
):
    n_dp = lax.axis_size(DP)
    n_tensor = lax.axis_size(TENSOR)
    dev_dp = lax.axis_index(DP)
    dev_chip = lax.axis_index(CHIP_DP)
    dev_tensor = lax.axis_index(TENSOR)
    core = lax.axis_index("c")
    pslots, _, page_size, width_two = kv_pool.shape
    head_dim = width_two // 2
    n_req = lengths.shape[0]
    req_dev = n_req // n_dp
    max_pages = page_loc.shape[2]
    max_len = max_pages * page_size
    cache_len = max_len + page_size
    n_steps = queries.shape[0]
    hq_dev = queries.shape[2]
    width = ffn_gain.shape[0]
    rows_dev = n_steps * req_dev
    chips_dp = n_dp // 2
    rows_core = n_steps * n_req // 2
    capacity = pslots // n_dp

    place = jnp.stack([dev_dp, dev_tensor, dev_chip]).astype(jnp.int32)
    outgoing, pick = pack_pages(
        place,
        jnp.swapaxes(page_loc, 1, 2),
        lengths.reshape(1, n_req),
        placement.reshape(1, n_req),
        kv_pool.reshape(pslots, page_size, width_two),
        n_dp,
    )
    query = jnp.transpose(queries, (1, 0, 2, 3)).reshape(req_dev, n_steps * hq_dev, head_dim)
    fresh = new_kv.reshape(n_steps, req_dev, width_two).astype(jnp.float32)

    cols_dev = width // n_dp
    cols_chip = 2 * cols_dev
    swap = [(0, 1), (1, 0)]

    def both(own, other):
        return jnp.where(
            core == 0,
            jnp.concatenate([own, other], axis=-1),
            jnp.concatenate([other, own], axis=-1),
        )

    resid_rows = jnp.transpose(
        resid_in.reshape(n_steps, chips_dp, 2, req_dev, cols_dev), (2, 1, 0, 3, 4)
    ).reshape(2, n_tensor, rows_core // n_tensor, cols_dev)

    def resid_of(at_core):
        return lax.dynamic_slice(
            resid_rows, (at_core, dev_tensor, 0, 0), (1, 1) + resid_rows.shape[2:]
        )[0, 0]

    resid_blk = both(resid_of(core), lax.ppermute(resid_of(1 - core), "c", swap))
    w_other = lax.ppermute(w_out, "c", swap)
    outgoing, pick, query, fresh, resid_blk, w_other, place = lax.optimization_barrier(
        (outgoing, pick, query, fresh, resid_blk, w_other, place)
    )
    received = lax.all_to_all(
        outgoing.reshape(n_dp, capacity, page_size, width_two), DP, 0, 0, tiled=True
    )
    cache, mixed_copies = intake(
        pick, received.reshape(pslots, page_size, width_two), fresh, query, chips_dp
    )

    w_both = both(w_out, w_other)
    mixed_rows = lax.all_to_all(mixed_copies, CHIP_DP, 0, 0, tiled=True).reshape(
        rows_core, hq_dev * head_dim
    )
    partial_out = jnp.dot(mixed_rows, w_both, preferred_element_type=jnp.float32).astype(
        jnp.bfloat16
    )
    rows_blk = rows_core // n_tensor
    parts = lax.all_to_all(
        partial_out.reshape(n_tensor, rows_blk, cols_chip), TENSOR, 0, 0, tiled=True
    )
    hidden_blk = (
        resid_blk.astype(jnp.float32) + jnp.sum(parts.astype(jnp.float32), axis=0)
    ).astype(jnp.bfloat16)
    own_rows = to_all(hidden_blk, CHIPS, chips_dp * n_tensor).reshape(
        chips_dp, rows_core, cols_chip
    )
    other_rows = lax.ppermute(own_rows, "c", swap)
    gate_rows = jnp.swapaxes(w_gate, 0, 1)
    up_rows = jnp.swapaxes(w_up, 0, 1)
    gain_row = ffn_gain.reshape(1, width)
    width_out = width // n_tensor

    ours, up_near, down_near, own_hidden = feed_forward(
        own_rows, gate_rows, up_rows, gain_row, w_down, n_tensor, rows_dev, place
    )
    other_rows, ours = lax.optimization_barrier((other_rows, ours))
    (theirs,) = feed_forward(
        other_rows, gate_rows, up_near, gain_row, down_near, n_tensor, rows_dev
    )
    from_core = lax.ppermute(theirs, "c", swap)
    chip_sum = add_cores(ours, from_core).reshape(chips_dp * n_tensor, rows_dev, width_out)
    pieces = lax.all_to_all(chip_sum, CHIPS, 0, 0, tiled=True)
    block_out = add_pieces(pieces, own_hidden, n_steps)
    return (block_out, cache.reshape(1, req_dev, cache_len, width_two))


def solution(mesh):
    fine = Mesh(mesh.devices.reshape(2, 4, 2, 4, 2), ("yh", "x", "c", "z", "yl"))
    placed = (
        P(DP, TENSOR, None, None),
        P(),
        P(),
        P(),
        P(None, DP, TENSOR, None),
        P(None, DP, TENSOR, None),
        P(None, None, DP),
        P(TENSOR, DP),
        P(),
        P(None, DP + TENSOR),
        P(None, DP + TENSOR),
        P(DP + TENSOR, None),
    )
    return jax.shard_map(
        per_device,
        mesh=fine,
        in_specs=placed,
        out_specs=(P(None, DP, TENSOR), P(TENSOR, DP, None, None)),
        check_vma=False,
    )
```

```python
import math

import jax
import jax.numpy as jnp
from jax import lax
from jax.experimental import pallas as pl
from jax.experimental.pallas import tpu as pltpu
from jax.sharding import Mesh, PartitionSpec as P

DP = ("yh", "x", "c")
CHIP_DP = ("yh", "x")
TENSOR = ("z", "yl")
CHIPS = ("yh", "x", "z", "yl")


def to_all(block, axes, count):
    copies = lax.optimization_barrier(jnp.broadcast_to(block[None], (count,) + block.shape))
    return lax.all_to_all(copies, axes, 0, 0, tiled=True)

MIB = 1024 * 1024
SMEM = pl.BlockSpec(memory_space=pltpu.SMEM)
VMEM = pl.BlockSpec(memory_space=pltpu.VMEM)
HBM = pl.BlockSpec(memory_space=pltpu.HBM)


def intake(pick, received, fresh, query, n_copies):
    req_dev, n_rows, head_dim = query.shape
    n_steps = fresh.shape[0]
    _, page_size, width_two = received.shape
    max_pages = pick.shape[0] - 8
    pages = max_pages + 1
    group = n_rows // n_steps
    scale = 1.0 / math.sqrt(head_dim)
    def kernel(pick_ref, recv_ref, fresh_ref, q_ref, cache_ref, mixed_ref, buf, scores, probs, heads, out_sems):
        def copy_out(r):
            return pltpu.make_async_copy(buf.at[r], cache_ref.at[r], out_sems.at[r])

        row_at = lax.broadcasted_iota(jnp.int32, (page_size, width_two), 0)
        tokens_new = [fresh_ref[s].astype(jnp.float32) for s in range(n_steps)]
        for r in range(req_dev):

            def move(p, carry):
                buf[r, p] = recv_ref[pick_ref[p, r]]
                return carry

            lax.fori_loop(0, max_pages, move, 0, unroll=16)
            length = pick_ref[max_pages, r]
            full = length // page_size

            def clear(p, carry):
                buf[r, p] = jnp.zeros((page_size, width_two), buf.dtype)
                return carry

            lax.fori_loop(full + 1, pages, clear, 0)
            edge = buf[r, full].astype(jnp.float32)
            buf[r, full] = jnp.where(row_at < length % page_size, edge, 0.0).astype(buf.dtype)
            for s in range(n_steps):
                at = length + s
                page = buf[r, at // page_size].astype(jnp.float32)
                token = tokens_new[s][r : r + 1]
                buf[r, at // page_size] = jnp.where(
                    row_at == at % page_size, token, page
                ).astype(buf.dtype)
            copy_out(r).start()
        for r in range(req_dev):
            keys = buf[r, :, :, :head_dim].reshape(pages * page_size, head_dim)
            part = scale * lax.dot_general(
                q_ref[r], keys, (((1,), (1,)), ((), ())), preferred_element_type=jnp.float32
            )
            last = pick_ref[max_pages, r] + lax.broadcasted_iota(jnp.int32, part.shape, 0) // group
            scores[r * n_rows : (r + 1) * n_rows] = jnp.where(
                lax.broadcasted_iota(jnp.int32, part.shape, 1) <= last, part, -jnp.inf
            )
        expo = jnp.exp(scores[...] - jnp.max(scores[...], axis=1, keepdims=True))
        probs[...] = (expo / jnp.sum(expo, axis=1, keepdims=True)).astype(probs.dtype)
        for r in range(req_dev):
            values = buf[r, :, :, head_dim:].reshape(pages * page_size, head_dim)
            head_out = jnp.dot(
                probs[r * n_rows : (r + 1) * n_rows], values, preferred_element_type=jnp.float32
            )
            for i in range(n_rows):
                heads[i, r : r + 1, :] = head_out[i : i + 1, :]
        for g in range(group):
            block = jnp.concatenate([heads[s * group + g] for s in range(n_steps)], axis=0)
            block = block.astype(mixed_ref.dtype)
            for k in range(n_copies):
                mixed_ref[k, :, g * head_dim : (g + 1) * head_dim] = block
        for r in range(req_dev):
            copy_out(r).wait()

    return pl.pallas_call(
        kernel,
        in_specs=[SMEM, VMEM, VMEM, VMEM],
        out_specs=[HBM, VMEM],
        out_shape=[
            jax.ShapeDtypeStruct((req_dev, pages, page_size, width_two), received.dtype),
            jax.ShapeDtypeStruct(
                (n_copies, n_steps * req_dev, group * head_dim), received.dtype
            ),
        ],
        scratch_shapes=[
            pltpu.VMEM((req_dev, pages, page_size, width_two), received.dtype),
            pltpu.VMEM((req_dev * n_rows, pages * page_size), jnp.float32),
            pltpu.VMEM((req_dev * n_rows, pages * page_size), jnp.bfloat16),
            pltpu.VMEM((n_rows, req_dev, head_dim), jnp.float32),
            pltpu.SemaphoreType.DMA((req_dev,)),
        ],
        compiler_params=pltpu.CompilerParams(vmem_limit_bytes=20 * MIB),
        name="intake",
    )(pick, received, fresh, query)


PARTS = 4
NT = (((1,), (1,)), ((), ()))


def in_parts(source, target, sems):
    span = target.shape[1] // PARTS
    copies = []
    for i in range(PARTS):
        part = pl.ds(i * span, span)
        copies.append(pltpu.make_async_copy(source.at[:, part], target.at[:, part], sems.at[i]))
        copies[-1].start()
    return copies


def scale_rows(x_ref, gain_ref, scaled):
    blocks, _, cols = x_ref.shape
    squares = 0.0
    for i in range(blocks):
        wide = x_ref[i].astype(jnp.float32)
        square = wide * wide
        squares += sum(square[:, k * 128 : (k + 1) * 128] for k in range(cols // 128))
        scaled[:, i * cols : (i + 1) * cols] = (
            wide * gain_ref[:, i * cols : (i + 1) * cols]
        ).astype(scaled.dtype)
    mean = jnp.sum(squares, axis=1, keepdims=True) * (1.0 / (blocks * cols))
    return lax.rsqrt(mean + 1e-05)


def activate(gate, upper):
    return (gate / (1.0 + jnp.exp(-gate)) * upper).astype(jnp.bfloat16)


def down_to(out_ref, act, down_ref, waits=()):
    chips, n_tensor, rows_dev, cols_out = out_ref.shape
    for t in range(n_tensor):
        if waits and t % (n_tensor // PARTS) == 0:
            waits[t // (n_tensor // PARTS)].wait()
        out = jnp.dot(
            act,
            down_ref[:, t * cols_out : (t + 1) * cols_out],
            preferred_element_type=jnp.float32,
        )
        out_ref[:, t] = out.astype(out_ref.dtype).reshape(chips, rows_dev, cols_out)


def expand_own(hidden, gate_rows, up_rows, gain_row, place, rows_dev):
    _, rows, cols = hidden.shape
    units, width = up_rows.shape

    def kernel(place_ref, x_ref, gate_ref, up_hbm, gain_ref, act_ref, up_ref, part_ref, scaled, sems):
        copies = in_parts(up_hbm, up_ref, sems)
        mine = pl.ds(pl.multiple_of(place_ref[2] * rows_dev, rows_dev), rows_dev)
        part_ref[...] = x_ref[place_ref[1], mine, :]
        inverse = scale_rows(x_ref, gain_ref, scaled)
        gate = lax.dot_general(scaled[...], gate_ref[...], NT, preferred_element_type=jnp.float32)
        upper = 0.0
        span = width // PARTS
        for i in range(PARTS):
            part = slice(i * span, (i + 1) * span)
            copies[i].wait()
            upper += lax.dot_general(
                scaled[:, part], up_ref[:, part], NT, preferred_element_type=jnp.float32
            )
        act_ref[...] = activate(gate * inverse, upper * inverse)

    return pl.pallas_call(
        kernel,
        in_specs=[SMEM, VMEM, VMEM, HBM, VMEM],
        out_specs=[VMEM] * 3,
        out_shape=[
            pltpu.VMEM((rows, units), jnp.bfloat16),
            pltpu.VMEM((units, width), jnp.bfloat16),
            jax.ShapeDtypeStruct((rows_dev, cols), hidden.dtype),
        ],
        scratch_shapes=[
            pltpu.VMEM((rows, width), jnp.bfloat16),
            pltpu.SemaphoreType.DMA((PARTS,)),
        ],
        compiler_params=pltpu.CompilerParams(vmem_limit_bytes=24 * MIB),
        name="expand_own",
    )(place, hidden, gate_rows, pltpu.with_memory_space_constraint(up_rows, pltpu.HBM), gain_row)


def feed_forward(hidden, gate_rows, up_rows, gain_row, w_down, n_tensor, rows_dev):
    _, rows, _ = hidden.shape
    units, width = w_down.shape

    def kernel(x_ref, gate_ref, up_ref, gain_ref, down_hbm, out_ref, down_ref, scaled, sems):
        copies = in_parts(down_hbm, down_ref, sems)
        inverse = scale_rows(x_ref, gain_ref, scaled)
        gate = lax.dot_general(scaled[...], gate_ref[...], NT, preferred_element_type=jnp.float32)
        upper = lax.dot_general(scaled[...], up_ref[...], NT, preferred_element_type=jnp.float32)
        down_to(out_ref, activate(gate * inverse, upper * inverse), down_ref, copies)

    return pl.pallas_call(
        kernel,
        in_specs=[VMEM, VMEM, VMEM, VMEM, HBM],
        out_specs=[VMEM] * 2,
        out_shape=[
            jax.ShapeDtypeStruct(
                (rows // rows_dev, n_tensor, rows_dev, width // n_tensor), jnp.bfloat16
            ),
            pltpu.VMEM((units, width), jnp.bfloat16),
        ],
        scratch_shapes=[
            pltpu.VMEM((rows, width), jnp.bfloat16),
            pltpu.SemaphoreType.DMA((PARTS,)),
        ],
        compiler_params=pltpu.CompilerParams(vmem_limit_bytes=28 * MIB),
        name="feed_forward",
    )(hidden, gate_rows, up_rows, gain_row, pltpu.with_memory_space_constraint(w_down, pltpu.HBM))


def shrink_own(act, w_down, n_tensor, rows_dev):
    def kernel(act_ref, down_ref, out_ref):
        down_to(out_ref, act_ref[...], down_ref)

    return pl.pallas_call(
        kernel,
        in_specs=[VMEM, VMEM],
        out_specs=VMEM,
        out_shape=jax.ShapeDtypeStruct(
            (act.shape[0] // rows_dev, n_tensor, rows_dev, w_down.shape[1] // n_tensor),
            jnp.bfloat16,
        ),
        compiler_params=pltpu.CompilerParams(vmem_limit_bytes=16 * MIB),
        name="shrink_own",
    )(act, w_down)


def add_pieces(pieces, hidden, n_steps):
    count, rows, cols = pieces.shape

    def kernel(pieces_ref, hidden_ref, out_ref):
        total = hidden_ref[...].astype(jnp.float32)
        for i in range(count):
            total += pieces_ref[i].astype(jnp.float32)
        out_ref[...] = total.reshape(n_steps, rows // n_steps, cols).astype(out_ref.dtype)

    return pl.pallas_call(
        kernel,
        in_specs=[VMEM, VMEM],
        out_specs=VMEM,
        out_shape=jax.ShapeDtypeStruct((n_steps, rows // n_steps, cols), pieces.dtype),
        compiler_params=pltpu.CompilerParams(vmem_limit_bytes=10 * MIB),
        name="add_pieces",
    )(pieces, hidden)


def exact_dot(left, right, contract):
    return lax.dot_general(
        left.astype(jnp.bfloat16),
        right.astype(jnp.bfloat16),
        (contract, ((), ())),
        preferred_element_type=jnp.float32,
    )


def pack_pages(place, page_loc, lengths, placement, pool, n_dp):
    pslots, page_size, width_two = pool.shape
    _, max_pages, n_req = page_loc.shape
    req_dev = n_req // n_dp
    capacity = pslots // n_dp
    low = 32

    def kernel(place_ref, loc_hbm, len_hbm, placement_hbm, pool_hbm, out_buf, pick_ref, loc, len_ref, placement_ref, pool_buf, rows_vec, rows, loc_sem, len_sem, placement_sem, pool_sem, rows_sem):
        me = place_ref[0]
        len_copy = pltpu.make_async_copy(len_hbm, len_ref, len_sem)
        placement_copy = pltpu.make_async_copy(placement_hbm, placement_ref, placement_sem)
        pool_copy = pltpu.make_async_copy(pool_hbm, pool_buf, pool_sem)
        loc_copy = pltpu.make_async_copy(loc_hbm.at[place_ref[1]], loc, loc_sem)
        loc_copy.start()
        len_copy.start()
        placement_copy.start()
        pool_copy.start()
        shape = (n_req, n_req)
        down = lax.broadcasted_iota(jnp.int32, shape, 0)
        across = lax.broadcasted_iota(jnp.int32, shape, 1)
        placement_copy.wait()
        slot_hot = jnp.where(placement_ref[...] == down, 1.0, 0.0)
        len_copy.wait()
        lens = jnp.broadcast_to(len_ref[...], (8, n_req))
        loc_copy.wait()
        at = loc[...]
        pieces = jnp.concatenate(
            [at // pslots, at % pslots // low, at % low, lens // low, lens % low], axis=0
        )
        by_slot = exact_dot(pieces.astype(jnp.float32), slot_hot, ((1,), (1,)))
        source = by_slot[:max_pages]
        row = by_slot[max_pages : 2 * max_pages] * low + by_slot[2 * max_pages : 3 * max_pages]
        len_row = by_slot[3 * max_pages : 3 * max_pages + 1] * low + by_slot[3 * max_pages + 8 : 3 * max_pages + 9]
        page_at = lax.broadcasted_iota(jnp.int32, (max_pages, n_req), 0).astype(jnp.float32)
        source = jnp.where(page_at * page_size < len_row, source, float(n_dp))
        mine = source == me.astype(jnp.float32)
        ones = jnp.where(mine, 1.0, 0.0)
        earlier = jnp.where(
            lax.broadcasted_iota(jnp.int32, (max_pages, max_pages), 1)
            < lax.broadcasted_iota(jnp.int32, (max_pages, max_pages), 0),
            1.0,
            0.0,
        )
        in_group = jnp.where((down // req_dev == across // req_dev) & (down < across), 1.0, 0.0)
        count = jnp.broadcast_to(jnp.sum(ones, axis=0, keepdims=True), (8, n_req))
        rank = exact_dot(earlier, ones, ((1,), (0,))) + exact_dot(count, in_group, ((1,), (0,)))[:1]
        rank = jnp.where(mine, rank, -1.0)
        found = jnp.concatenate(
            [
                jnp.sum(jnp.where(rank == float(k), row, 0.0), axis=0, keepdims=True)
                for k in range(capacity)
            ],
            axis=0,
        ).astype(jnp.int32)
        group = jnp.where(down // req_dev == across, 1.0, 0.0)
        high_part = exact_dot((found // low).astype(jnp.float32), group, ((1,), (0,)))
        low_part = exact_dot((found % low).astype(jnp.float32), group, ((1,), (0,)))
        rows_vec[...] = (high_part * low + low_part).astype(jnp.int32)
        rows_copy = pltpu.make_async_copy(rows_vec, rows, rows_sem)
        rows_copy.start()
        own = jnp.where(down == me * req_dev + across % req_dev, 1.0, 0.0)
        ahead = jnp.concatenate([source, jnp.floor(len_row * (1.0 / low)), len_row - jnp.floor(len_row * (1.0 / low)) * low], axis=0)
        ahead = jnp.concatenate([ahead, jnp.zeros((6, n_req), jnp.float32)], axis=0)
        own_cols = exact_dot(ahead, own, ((1,), (0,)))
        lane = lax.broadcasted_iota(jnp.int32, (max_pages, n_req), 1)
        hit = own_cols[:max_pages] == (lane // req_dev).astype(jnp.float32)
        ones = jnp.where(hit, 1.0, 0.0)
        count = jnp.broadcast_to(jnp.sum(ones, axis=0, keepdims=True), (8, n_req))
        rank = exact_dot(earlier, ones, ((1,), (0,))) + exact_dot(count, in_group, ((1,), (0,)))[:1]
        spot = jnp.where(hit, rank + 1.0, 0.0)
        requests = jnp.where(down % req_dev == across, 1.0, 0.0)
        base = jnp.where(hit, (lane // req_dev).astype(jnp.float32), 0.0)
        pick = exact_dot(base, requests, ((1,), (0,))) * capacity
        pick += exact_dot(spot, requests, ((1,), (0,))) - 1.0
        own_len = own_cols[max_pages : max_pages + 1] * low + own_cols[max_pages + 1 : max_pages + 2]
        pick_ref[:max_pages] = jnp.maximum(pick, 0.0).astype(jnp.int32)
        pick_ref[max_pages:] = jnp.broadcast_to(own_len, (8, n_req)).astype(jnp.int32)
        rows_copy.wait()
        pool_copy.wait()

        for d in range(n_dp):

            def move(k, carry):
                out_buf[d * capacity + k] = pool_buf[rows[k, d]]
                return carry

            lax.fori_loop(0, capacity, move, 0, unroll=16)

    return pl.pallas_call(
        kernel,
        in_specs=[SMEM, HBM, HBM, HBM, HBM],
        out_specs=[VMEM, VMEM],
        out_shape=[
            jax.ShapeDtypeStruct(pool.shape, pool.dtype),
            jax.ShapeDtypeStruct((max_pages + 8, n_req), jnp.int32),
        ],
        scratch_shapes=[
            pltpu.VMEM((max_pages, n_req), jnp.int32),
            pltpu.VMEM((1, n_req), jnp.int32),
            pltpu.VMEM((1, n_req), jnp.int32),
            pltpu.VMEM(pool.shape, pool.dtype),
            pltpu.VMEM((capacity, n_req), jnp.int32),
            pltpu.SMEM((capacity, n_req), jnp.int32),
            pltpu.SemaphoreType.DMA,
            pltpu.SemaphoreType.DMA,
            pltpu.SemaphoreType.DMA,
            pltpu.SemaphoreType.DMA,
            pltpu.SemaphoreType.DMA,
        ],
        compiler_params=pltpu.CompilerParams(vmem_limit_bytes=20 * MIB),
        name="pack_pages",
    )(
        place,
        *[
            pltpu.with_memory_space_constraint(array, pltpu.HBM)
            for array in (page_loc, lengths, placement, pool)
        ],
    )


def add_cores(ours, from_core):
    def kernel(a_ref, b_ref, out_ref):
        for i in range(ours.shape[0]):
            out_ref[i] = (a_ref[i].astype(jnp.float32) + b_ref[i].astype(jnp.float32)).astype(
                out_ref.dtype
            )

    return pl.pallas_call(
        kernel,
        in_specs=[VMEM, VMEM],
        out_specs=VMEM,
        out_shape=jax.ShapeDtypeStruct(ours.shape, ours.dtype),
        compiler_params=pltpu.CompilerParams(vmem_limit_bytes=12 * MIB),
        name="add_cores",
    )(ours, from_core)


def per_device(
    kv_pool,
    page_loc,
    lengths,
    placement,
    queries,
    new_kv,
    resid_in,
    w_out,
    ffn_gain,
    w_gate,
    w_up,
    w_down,
):
    n_dp = lax.axis_size(DP)
    n_tensor = lax.axis_size(TENSOR)
    dev_dp = lax.axis_index(DP)
    dev_chip = lax.axis_index(CHIP_DP)
    dev_tensor = lax.axis_index(TENSOR)
    core = lax.axis_index("c")
    pslots, _, page_size, width_two = kv_pool.shape
    head_dim = width_two // 2
    n_req = lengths.shape[0]
    req_dev = n_req // n_dp
    max_pages = page_loc.shape[2]
    max_len = max_pages * page_size
    cache_len = max_len + page_size
    n_steps = queries.shape[0]
    hq_dev = queries.shape[2]
    width = ffn_gain.shape[0]
    rows_dev = n_steps * req_dev
    chips_dp = n_dp // 2
    rows_core = n_steps * n_req // 2
    capacity = pslots // n_dp

    place = jnp.stack([dev_dp, dev_tensor, dev_chip]).astype(jnp.int32)
    outgoing, pick = pack_pages(
        place,
        jnp.swapaxes(page_loc, 1, 2),
        lengths.reshape(1, n_req),
        placement.reshape(1, n_req),
        kv_pool.reshape(pslots, page_size, width_two),
        n_dp,
    )
    query = jnp.transpose(queries, (1, 0, 2, 3)).reshape(req_dev, n_steps * hq_dev, head_dim)
    fresh = new_kv.reshape(n_steps, req_dev, width_two)

    cols_dev = width // n_dp
    cols_chip = 2 * cols_dev
    swap = [(0, 1), (1, 0)]

    def both(own, other):
        return jnp.where(
            core == 0,
            jnp.concatenate([own, other], axis=-1),
            jnp.concatenate([other, own], axis=-1),
        )

    def resid_of(at_core):
        return lax.dynamic_slice(
            resid_in,
            (0, (2 * dev_tensor + at_core) * req_dev, 0),
            (n_steps, req_dev, cols_dev),
        ).reshape(rows_dev, cols_dev)

    resid_blk = both(resid_of(core), lax.ppermute(resid_of(1 - core), "c", swap))
    w_other = lax.ppermute(w_out, "c", swap)
    outgoing, pick, query, resid_blk, w_other, place = lax.optimization_barrier(
        (outgoing, pick, query, resid_blk, w_other, place)
    )
    received = lax.all_to_all(
        outgoing.reshape(n_dp, capacity, page_size, width_two), DP, 0, 0, tiled=True
    )
    cache, mixed_copies = intake(
        pick, received.reshape(pslots, page_size, width_two), fresh, query, chips_dp
    )

    w_both = both(w_out, w_other)
    mixed_rows = lax.all_to_all(mixed_copies, CHIP_DP, 0, 0, tiled=True).reshape(
        rows_core, hq_dev * head_dim
    )
    partial_out = jnp.dot(mixed_rows, w_both, preferred_element_type=jnp.float32).astype(
        jnp.bfloat16
    )
    rows_blk = rows_core // n_tensor
    parts = lax.all_to_all(
        partial_out.reshape(n_tensor, rows_blk, cols_chip), TENSOR, 0, 0, tiled=True
    )
    hidden_blk = (
        resid_blk.astype(jnp.float32) + jnp.sum(parts.astype(jnp.float32), axis=0)
    ).astype(jnp.bfloat16)
    own_rows = to_all(hidden_blk, CHIPS, chips_dp * n_tensor).reshape(
        chips_dp, rows_core, cols_chip
    )
    other_rows = lax.ppermute(own_rows, "c", swap)
    gate_rows = jnp.swapaxes(w_gate, 0, 1)
    up_rows = jnp.swapaxes(w_up, 0, 1)
    gain_row = ffn_gain.reshape(1, width)
    width_out = width // n_tensor

    act_own, up_near, own_hidden = expand_own(
        own_rows, gate_rows, up_rows, gain_row, place, rows_dev
    )
    other_rows, act_own = lax.optimization_barrier((other_rows, act_own))
    theirs, down_near = feed_forward(
        other_rows, gate_rows, up_near, gain_row, w_down, n_tensor, rows_dev
    )
    from_core = lax.ppermute(theirs, "c", swap)
    ours = shrink_own(act_own, down_near, n_tensor, rows_dev)
    chip_sum = add_cores(ours, from_core).reshape(chips_dp * n_tensor, rows_dev, width_out)
    pieces = lax.all_to_all(chip_sum, CHIPS, 0, 0, tiled=True)
    block_out = add_pieces(pieces, own_hidden, n_steps)
    return (block_out, cache.reshape(1, req_dev, cache_len, width_two))


def solution(mesh):
    fine = Mesh(mesh.devices.reshape(2, 4, 2, 4, 2), ("yh", "x", "c", "z", "yl"))
    placed = (
        P(DP, TENSOR, None, None),
        P(),
        P(),
        P(),
        P(None, DP, TENSOR, None),
        P(None, DP, TENSOR, None),
        P(None, None, DP),
        P(TENSOR, DP),
        P(),
        P(None, DP + TENSOR),
        P(None, DP + TENSOR),
        P(DP + TENSOR, None),
    )
    return jax.shard_map(
        per_device,
        mesh=fine,
        in_specs=placed,
        out_specs=(P(None, DP, TENSOR), P(TENSOR, DP, None, None)),
        check_vma=False,
    )
```

```python
import math

import jax
import jax.numpy as jnp
from jax import lax
from jax.experimental import pallas as pl
from jax.experimental.pallas import tpu as pltpu
from jax.sharding import Mesh, PartitionSpec as P

DP = ("yh", "x", "c")
CHIP_DP = ("yh", "x")
TENSOR = ("z", "yl")
CHIPS = ("yh", "x", "z", "yl")


def to_all(block, axes, count):
    copies = lax.optimization_barrier(jnp.broadcast_to(block[None], (count,) + block.shape))
    return lax.all_to_all(copies, axes, 0, 0, tiled=True)

MIB = 1024 * 1024
SMEM = pl.BlockSpec(memory_space=pltpu.SMEM)
VMEM = pl.BlockSpec(memory_space=pltpu.VMEM)
HBM = pl.BlockSpec(memory_space=pltpu.HBM)


def intake(pick, received, fresh, query, up_rows, n_copies):
    req_dev, n_rows, head_dim = query.shape
    n_steps = fresh.shape[0]
    _, page_size, width_two = received.shape
    max_pages = pick.shape[0] - 8
    pages = max_pages + 1
    group = n_rows // n_steps
    scale = 1.0 / math.sqrt(head_dim)
    def kernel(pick_ref, recv_ref, fresh_ref, q_ref, up_hbm, cache_ref, mixed_ref, up_ref, buf, scores, probs, heads, out_sems, up_sem):
        def copy_out(r):
            return pltpu.make_async_copy(buf.at[r], cache_ref.at[r], out_sems.at[r])

        row_at = lax.broadcasted_iota(jnp.int32, (page_size, width_two), 0)
        tokens_new = [fresh_ref[s].astype(jnp.float32) for s in range(n_steps)]
        for r in range(req_dev):

            def move(p, carry):
                buf[r, p] = recv_ref[pick_ref[p, r]]
                return carry

            lax.fori_loop(0, max_pages, move, 0, unroll=16)
            length = pick_ref[max_pages, r]
            full = length // page_size

            def clear(p, carry):
                buf[r, p] = jnp.zeros((page_size, width_two), buf.dtype)
                return carry

            lax.fori_loop(full + 1, pages, clear, 0)
            edge = buf[r, full].astype(jnp.float32)
            buf[r, full] = jnp.where(row_at < length % page_size, edge, 0.0).astype(buf.dtype)
            for s in range(n_steps):
                at = length + s
                page = buf[r, at // page_size].astype(jnp.float32)
                token = tokens_new[s][r : r + 1]
                buf[r, at // page_size] = jnp.where(
                    row_at == at % page_size, token, page
                ).astype(buf.dtype)
            copy_out(r).start()
        up_copy = pltpu.make_async_copy(up_hbm, up_ref, up_sem)
        up_copy.start()
        for r in range(req_dev):
            keys = buf[r, :, :, :head_dim].reshape(pages * page_size, head_dim)
            part = scale * lax.dot_general(
                q_ref[r], keys, (((1,), (1,)), ((), ())), preferred_element_type=jnp.float32
            )
            last = pick_ref[max_pages, r] + lax.broadcasted_iota(jnp.int32, part.shape, 0) // group
            scores[r * n_rows : (r + 1) * n_rows] = jnp.where(
                lax.broadcasted_iota(jnp.int32, part.shape, 1) <= last, part, -jnp.inf
            )
        expo = jnp.exp(scores[...] - jnp.max(scores[...], axis=1, keepdims=True))
        probs[...] = (expo / jnp.sum(expo, axis=1, keepdims=True)).astype(probs.dtype)
        for r in range(req_dev):
            values = buf[r, :, :, head_dim:].reshape(pages * page_size, head_dim)
            head_out = jnp.dot(
                probs[r * n_rows : (r + 1) * n_rows], values, preferred_element_type=jnp.float32
            )
            for i in range(n_rows):
                heads[i, r : r + 1, :] = head_out[i : i + 1, :]
        for g in range(group):
            block = jnp.concatenate([heads[s * group + g] for s in range(n_steps)], axis=0)
            block = block.astype(mixed_ref.dtype)
            for k in range(n_copies):
                mixed_ref[k, :, g * head_dim : (g + 1) * head_dim] = block
        for r in range(req_dev):
            copy_out(r).wait()
        up_copy.wait()

    return pl.pallas_call(
        kernel,
        in_specs=[SMEM, VMEM, VMEM, VMEM, HBM],
        out_specs=[HBM, VMEM, VMEM],
        out_shape=[
            jax.ShapeDtypeStruct((req_dev, pages, page_size, width_two), received.dtype),
            jax.ShapeDtypeStruct(
                (n_copies, n_steps * req_dev, group * head_dim), received.dtype
            ),
            pltpu.VMEM(up_rows.shape, up_rows.dtype),
        ],
        scratch_shapes=[
            pltpu.VMEM((req_dev, pages, page_size, width_two), received.dtype),
            pltpu.VMEM((req_dev * n_rows, pages * page_size), jnp.float32),
            pltpu.VMEM((req_dev * n_rows, pages * page_size), jnp.bfloat16),
            pltpu.VMEM((n_rows, req_dev, head_dim), jnp.float32),
            pltpu.SemaphoreType.DMA((req_dev,)),
            pltpu.SemaphoreType.DMA,
        ],
        compiler_params=pltpu.CompilerParams(vmem_limit_bytes=20 * MIB),
        name="intake",
    )(pick, received, fresh, query, pltpu.with_memory_space_constraint(up_rows, pltpu.HBM))


PARTS = 4
NT = (((1,), (1,)), ((), ()))


def in_parts(source, target, sems):
    span = target.shape[1] // PARTS
    copies = []
    for i in range(PARTS):
        part = pl.ds(i * span, span)
        copies.append(pltpu.make_async_copy(source.at[:, part], target.at[:, part], sems.at[i]))
        copies[-1].start()
    return copies


def scale_rows(x_ref, gain_ref, scaled):
    blocks, _, cols = x_ref.shape
    squares = 0.0
    for i in range(blocks):
        wide = x_ref[i].astype(jnp.float32)
        square = wide * wide
        squares += sum(square[:, k * 128 : (k + 1) * 128] for k in range(cols // 128))
        scaled[:, i * cols : (i + 1) * cols] = (
            wide * gain_ref[:, i * cols : (i + 1) * cols]
        ).astype(scaled.dtype)
    mean = jnp.sum(squares, axis=1, keepdims=True) * (1.0 / (blocks * cols))
    return lax.rsqrt(mean + 1e-05)


def activate(gate, upper):
    return (gate / (1.0 + jnp.exp(-gate)) * upper).astype(jnp.bfloat16)


def down_to(out_ref, act, down_ref, waits=()):
    chips, n_tensor, rows_dev, cols_out = out_ref.shape
    for t in range(n_tensor):
        if waits and t % (n_tensor // PARTS) == 0:
            waits[t // (n_tensor // PARTS)].wait()
        out = jnp.dot(
            act,
            down_ref[:, t * cols_out : (t + 1) * cols_out],
            preferred_element_type=jnp.float32,
        )
        out_ref[:, t] = out.astype(out_ref.dtype).reshape(chips, rows_dev, cols_out)


def expand_own(hidden, gate_rows, up_rows, gain_row, place, rows_dev):
    _, rows, cols = hidden.shape
    units, width = up_rows.shape

    def kernel(place_ref, x_ref, gate_ref, up_ref, gain_ref, act_ref, part_ref, scaled):
        mine = pl.ds(pl.multiple_of(place_ref[2] * rows_dev, rows_dev), rows_dev)
        part_ref[...] = x_ref[place_ref[1], mine, :]
        inverse = scale_rows(x_ref, gain_ref, scaled)
        gate = lax.dot_general(scaled[...], gate_ref[...], NT, preferred_element_type=jnp.float32)
        upper = lax.dot_general(scaled[...], up_ref[...], NT, preferred_element_type=jnp.float32)
        act_ref[...] = activate(gate * inverse, upper * inverse)

    return pl.pallas_call(
        kernel,
        in_specs=[SMEM, VMEM, VMEM, VMEM, VMEM],
        out_specs=[VMEM] * 2,
        out_shape=[
            pltpu.VMEM((rows, units), jnp.bfloat16),
            jax.ShapeDtypeStruct((rows_dev, cols), hidden.dtype),
        ],
        scratch_shapes=[pltpu.VMEM((rows, width), jnp.bfloat16)],
        compiler_params=pltpu.CompilerParams(vmem_limit_bytes=24 * MIB),
        name="expand_own",
    )(place, hidden, gate_rows, up_rows, gain_row)


def feed_forward(hidden, gate_rows, up_rows, gain_row, w_down, n_tensor, rows_dev):
    _, rows, _ = hidden.shape
    units, width = w_down.shape

    def kernel(x_ref, gate_ref, up_ref, gain_ref, down_hbm, out_ref, down_ref, scaled, sems):
        copies = in_parts(down_hbm, down_ref, sems)
        inverse = scale_rows(x_ref, gain_ref, scaled)
        gate = lax.dot_general(scaled[...], gate_ref[...], NT, preferred_element_type=jnp.float32)
        upper = lax.dot_general(scaled[...], up_ref[...], NT, preferred_element_type=jnp.float32)
        down_to(out_ref, activate(gate * inverse, upper * inverse), down_ref, copies)

    return pl.pallas_call(
        kernel,
        in_specs=[VMEM, VMEM, VMEM, VMEM, HBM],
        out_specs=[VMEM] * 2,
        out_shape=[
            jax.ShapeDtypeStruct(
                (rows // rows_dev, n_tensor, rows_dev, width // n_tensor), jnp.bfloat16
            ),
            pltpu.VMEM((units, width), jnp.bfloat16),
        ],
        scratch_shapes=[
            pltpu.VMEM((rows, width), jnp.bfloat16),
            pltpu.SemaphoreType.DMA((PARTS,)),
        ],
        compiler_params=pltpu.CompilerParams(vmem_limit_bytes=28 * MIB),
        name="feed_forward",
    )(hidden, gate_rows, up_rows, gain_row, pltpu.with_memory_space_constraint(w_down, pltpu.HBM))


def shrink_own(act, w_down, n_tensor, rows_dev):
    def kernel(act_ref, down_ref, out_ref):
        down_to(out_ref, act_ref[...], down_ref)

    return pl.pallas_call(
        kernel,
        in_specs=[VMEM, VMEM],
        out_specs=VMEM,
        out_shape=jax.ShapeDtypeStruct(
            (act.shape[0] // rows_dev, n_tensor, rows_dev, w_down.shape[1] // n_tensor),
            jnp.bfloat16,
        ),
        compiler_params=pltpu.CompilerParams(vmem_limit_bytes=16 * MIB),
        name="shrink_own",
    )(act, w_down)


def add_pieces(pieces, hidden, n_steps):
    count, rows, cols = pieces.shape

    def kernel(pieces_ref, hidden_ref, out_ref):
        total = hidden_ref[...].astype(jnp.float32)
        for i in range(count):
            total += pieces_ref[i].astype(jnp.float32)
        out_ref[...] = total.reshape(n_steps, rows // n_steps, cols).astype(out_ref.dtype)

    return pl.pallas_call(
        kernel,
        in_specs=[VMEM, VMEM],
        out_specs=VMEM,
        out_shape=jax.ShapeDtypeStruct((n_steps, rows // n_steps, cols), pieces.dtype),
        compiler_params=pltpu.CompilerParams(vmem_limit_bytes=10 * MIB),
        name="add_pieces",
    )(pieces, hidden)


def exact_dot(left, right, contract):
    return lax.dot_general(
        left.astype(jnp.bfloat16),
        right.astype(jnp.bfloat16),
        (contract, ((), ())),
        preferred_element_type=jnp.float32,
    )


def pack_pages(place, page_loc, lengths, placement, pool, n_dp):
    pslots, page_size, width_two = pool.shape
    _, max_pages, n_req = page_loc.shape
    req_dev = n_req // n_dp
    capacity = pslots // n_dp
    low = 32

    def kernel(place_ref, loc_hbm, len_hbm, placement_hbm, pool_hbm, out_buf, pick_ref, loc, len_ref, placement_ref, pool_buf, rows_vec, rows, loc_sem, len_sem, placement_sem, pool_sem, rows_sem):
        me = place_ref[0]
        len_copy = pltpu.make_async_copy(len_hbm, len_ref, len_sem)
        placement_copy = pltpu.make_async_copy(placement_hbm, placement_ref, placement_sem)
        pool_copy = pltpu.make_async_copy(pool_hbm, pool_buf, pool_sem)
        loc_copy = pltpu.make_async_copy(loc_hbm.at[place_ref[1]], loc, loc_sem)
        loc_copy.start()
        len_copy.start()
        placement_copy.start()
        pool_copy.start()
        shape = (n_req, n_req)
        down = lax.broadcasted_iota(jnp.int32, shape, 0)
        across = lax.broadcasted_iota(jnp.int32, shape, 1)
        placement_copy.wait()
        slot_hot = jnp.where(placement_ref[...] == down, 1.0, 0.0)
        len_copy.wait()
        lens = jnp.broadcast_to(len_ref[...], (8, n_req))
        loc_copy.wait()
        at = loc[...]
        pieces = jnp.concatenate(
            [at // pslots, at % pslots // low, at % low, lens // low, lens % low], axis=0
        )
        by_slot = exact_dot(pieces.astype(jnp.float32), slot_hot, ((1,), (1,)))
        source = by_slot[:max_pages]
        row = by_slot[max_pages : 2 * max_pages] * low + by_slot[2 * max_pages : 3 * max_pages]
        len_row = by_slot[3 * max_pages : 3 * max_pages + 1] * low + by_slot[3 * max_pages + 8 : 3 * max_pages + 9]
        page_at = lax.broadcasted_iota(jnp.int32, (max_pages, n_req), 0).astype(jnp.float32)
        source = jnp.where(page_at * page_size < len_row, source, float(n_dp))
        mine = source == me.astype(jnp.float32)
        ones = jnp.where(mine, 1.0, 0.0)
        earlier = jnp.where(
            lax.broadcasted_iota(jnp.int32, (max_pages, max_pages), 1)
            < lax.broadcasted_iota(jnp.int32, (max_pages, max_pages), 0),
            1.0,
            0.0,
        )
        in_group = jnp.where((down // req_dev == across // req_dev) & (down < across), 1.0, 0.0)
        count = jnp.broadcast_to(jnp.sum(ones, axis=0, keepdims=True), (8, n_req))
        rank = exact_dot(earlier, ones, ((1,), (0,))) + exact_dot(count, in_group, ((1,), (0,)))[:1]
        rank = jnp.where(mine, rank, -1.0)
        found = jnp.concatenate(
            [
                jnp.sum(jnp.where(rank == float(k), row, 0.0), axis=0, keepdims=True)
                for k in range(capacity)
            ],
            axis=0,
        ).astype(jnp.int32)
        group = jnp.where(down // req_dev == across, 1.0, 0.0)
        high_part = exact_dot((found // low).astype(jnp.float32), group, ((1,), (0,)))
        low_part = exact_dot((found % low).astype(jnp.float32), group, ((1,), (0,)))
        rows_vec[...] = (high_part * low + low_part).astype(jnp.int32)
        rows_copy = pltpu.make_async_copy(rows_vec, rows, rows_sem)
        rows_copy.start()
        own = jnp.where(down == me * req_dev + across % req_dev, 1.0, 0.0)
        ahead = jnp.concatenate([source, jnp.floor(len_row * (1.0 / low)), len_row - jnp.floor(len_row * (1.0 / low)) * low], axis=0)
        ahead = jnp.concatenate([ahead, jnp.zeros((6, n_req), jnp.float32)], axis=0)
        own_cols = exact_dot(ahead, own, ((1,), (0,)))
        lane = lax.broadcasted_iota(jnp.int32, (max_pages, n_req), 1)
        hit = own_cols[:max_pages] == (lane // req_dev).astype(jnp.float32)
        ones = jnp.where(hit, 1.0, 0.0)
        count = jnp.broadcast_to(jnp.sum(ones, axis=0, keepdims=True), (8, n_req))
        rank = exact_dot(earlier, ones, ((1,), (0,))) + exact_dot(count, in_group, ((1,), (0,)))[:1]
        spot = jnp.where(hit, rank + 1.0, 0.0)
        requests = jnp.where(down % req_dev == across, 1.0, 0.0)
        base = jnp.where(hit, (lane // req_dev).astype(jnp.float32), 0.0)
        pick = exact_dot(base, requests, ((1,), (0,))) * capacity
        pick += exact_dot(spot, requests, ((1,), (0,))) - 1.0
        own_len = own_cols[max_pages : max_pages + 1] * low + own_cols[max_pages + 1 : max_pages + 2]
        pick_ref[:max_pages] = jnp.maximum(pick, 0.0).astype(jnp.int32)
        pick_ref[max_pages:] = jnp.broadcast_to(own_len, (8, n_req)).astype(jnp.int32)
        rows_copy.wait()
        pool_copy.wait()

        for d in range(n_dp):

            def move(k, carry):
                out_buf[d * capacity + k] = pool_buf[rows[k, d]]
                return carry

            lax.fori_loop(0, capacity, move, 0, unroll=16)

    return pl.pallas_call(
        kernel,
        in_specs=[SMEM, HBM, HBM, HBM, HBM],
        out_specs=[VMEM, VMEM],
        out_shape=[
            jax.ShapeDtypeStruct(pool.shape, pool.dtype),
            jax.ShapeDtypeStruct((max_pages + 8, n_req), jnp.int32),
        ],
        scratch_shapes=[
            pltpu.VMEM((max_pages, n_req), jnp.int32),
            pltpu.VMEM((1, n_req), jnp.int32),
            pltpu.VMEM((1, n_req), jnp.int32),
            pltpu.VMEM(pool.shape, pool.dtype),
            pltpu.VMEM((capacity, n_req), jnp.int32),
            pltpu.SMEM((capacity, n_req), jnp.int32),
            pltpu.SemaphoreType.DMA,
            pltpu.SemaphoreType.DMA,
            pltpu.SemaphoreType.DMA,
            pltpu.SemaphoreType.DMA,
            pltpu.SemaphoreType.DMA,
        ],
        compiler_params=pltpu.CompilerParams(vmem_limit_bytes=20 * MIB),
        name="pack_pages",
    )(
        place,
        *[
            pltpu.with_memory_space_constraint(array, pltpu.HBM)
            for array in (page_loc, lengths, placement, pool)
        ],
    )


def add_cores(ours, from_core):
    def kernel(a_ref, b_ref, out_ref):
        for i in range(ours.shape[0]):
            out_ref[i] = (a_ref[i].astype(jnp.float32) + b_ref[i].astype(jnp.float32)).astype(
                out_ref.dtype
            )

    return pl.pallas_call(
        kernel,
        in_specs=[VMEM, VMEM],
        out_specs=VMEM,
        out_shape=jax.ShapeDtypeStruct(ours.shape, ours.dtype),
        compiler_params=pltpu.CompilerParams(vmem_limit_bytes=12 * MIB),
        name="add_cores",
    )(ours, from_core)


def per_device(
    kv_pool,
    page_loc,
    lengths,
    placement,
    queries,
    new_kv,
    resid_in,
    w_out,
    ffn_gain,
    w_gate,
    w_up,
    w_down,
):
    n_dp = lax.axis_size(DP)
    n_tensor = lax.axis_size(TENSOR)
    dev_dp = lax.axis_index(DP)
    dev_chip = lax.axis_index(CHIP_DP)
    dev_tensor = lax.axis_index(TENSOR)
    core = lax.axis_index("c")
    pslots, _, page_size, width_two = kv_pool.shape
    head_dim = width_two // 2
    n_req = lengths.shape[0]
    req_dev = n_req // n_dp
    max_pages = page_loc.shape[2]
    max_len = max_pages * page_size
    cache_len = max_len + page_size
    n_steps = queries.shape[0]
    hq_dev = queries.shape[2]
    width = ffn_gain.shape[0]
    rows_dev = n_steps * req_dev
    chips_dp = n_dp // 2
    rows_core = n_steps * n_req // 2
    capacity = pslots // n_dp

    place = jnp.stack([dev_dp, dev_tensor, dev_chip]).astype(jnp.int32)
    outgoing, pick = pack_pages(
        place,
        jnp.swapaxes(page_loc, 1, 2),
        lengths.reshape(1, n_req),
        placement.reshape(1, n_req),
        kv_pool.reshape(pslots, page_size, width_two),
        n_dp,
    )
    query = jnp.transpose(queries, (1, 0, 2, 3)).reshape(req_dev, n_steps * hq_dev, head_dim)
    fresh = new_kv.reshape(n_steps, req_dev, width_two)

    cols_dev = width // n_dp
    cols_chip = 2 * cols_dev
    swap = [(0, 1), (1, 0)]

    def both(own, other):
        return jnp.where(
            core == 0,
            jnp.concatenate([own, other], axis=-1),
            jnp.concatenate([other, own], axis=-1),
        )

    def resid_of(at_core):
        return lax.dynamic_slice(
            resid_in,
            (0, (2 * dev_tensor + at_core) * req_dev, 0),
            (n_steps, req_dev, cols_dev),
        ).reshape(rows_dev, cols_dev)

    resid_blk = both(resid_of(core), lax.ppermute(resid_of(1 - core), "c", swap))
    w_other = lax.ppermute(w_out, "c", swap)
    outgoing, pick, query, resid_blk, w_other, place = lax.optimization_barrier(
        (outgoing, pick, query, resid_blk, w_other, place)
    )
    received = lax.all_to_all(
        outgoing.reshape(n_dp, capacity, page_size, width_two), DP, 0, 0, tiled=True
    )
    cache, mixed_copies, up_near = intake(
        pick,
        received.reshape(pslots, page_size, width_two),
        fresh,
        query,
        jnp.swapaxes(w_up, 0, 1),
        chips_dp,
    )

    w_both = both(w_out, w_other)
    mixed_rows = lax.all_to_all(mixed_copies, CHIP_DP, 0, 0, tiled=True).reshape(
        rows_core, hq_dev * head_dim
    )
    partial_out = jnp.dot(mixed_rows, w_both, preferred_element_type=jnp.float32).astype(
        jnp.bfloat16
    )
    rows_blk = rows_core // n_tensor
    parts = lax.all_to_all(
        partial_out.reshape(n_tensor, rows_blk, cols_chip), TENSOR, 0, 0, tiled=True
    )
    hidden_blk = (
        resid_blk.astype(jnp.float32) + jnp.sum(parts.astype(jnp.float32), axis=0)
    ).astype(jnp.bfloat16)
    own_rows = to_all(hidden_blk, CHIPS, chips_dp * n_tensor).reshape(
        chips_dp, rows_core, cols_chip
    )
    other_rows = lax.ppermute(own_rows, "c", swap)
    gate_rows = jnp.swapaxes(w_gate, 0, 1)
    gain_row = ffn_gain.reshape(1, width)
    width_out = width // n_tensor

    act_own, own_hidden = expand_own(own_rows, gate_rows, up_near, gain_row, place, rows_dev)
    other_rows, act_own = lax.optimization_barrier((other_rows, act_own))
    theirs, down_near = feed_forward(
        other_rows, gate_rows, up_near, gain_row, w_down, n_tensor, rows_dev
    )
    from_core = lax.ppermute(theirs, "c", swap)
    ours = shrink_own(act_own, down_near, n_tensor, rows_dev)
    chip_sum = add_cores(ours, from_core).reshape(chips_dp * n_tensor, rows_dev, width_out)
    pieces = lax.all_to_all(chip_sum, CHIPS, 0, 0, tiled=True)
    block_out = add_pieces(pieces, own_hidden, n_steps)
    return (block_out, cache.reshape(1, req_dev, cache_len, width_two))


def solution(mesh):
    fine = Mesh(mesh.devices.reshape(2, 4, 2, 4, 2), ("yh", "x", "c", "z", "yl"))
    placed = (
        P(DP, TENSOR, None, None),
        P(),
        P(),
        P(),
        P(None, DP, TENSOR, None),
        P(None, DP, TENSOR, None),
        P(None, None, DP),
        P(TENSOR, DP),
        P(),
        P(None, DP + TENSOR),
        P(None, DP + TENSOR),
        P(DP + TENSOR, None),
    )
    return jax.shard_map(
        per_device,
        mesh=fine,
        in_specs=placed,
        out_specs=(P(None, DP, TENSOR), P(TENSOR, DP, None, None)),
        check_vma=False,
    )
```

```python
import math

import jax
import jax.numpy as jnp
from jax import lax
from jax.experimental import pallas as pl
from jax.experimental.pallas import tpu as pltpu
from jax.sharding import Mesh, PartitionSpec as P

DP = ("yh", "x", "c")
CHIP_DP = ("yh", "x")
TENSOR = ("z", "yl")
CHIPS = ("yh", "x", "z", "yl")


def to_all(block, axes, count):
    copies = lax.optimization_barrier(jnp.broadcast_to(block[None], (count,) + block.shape))
    return lax.all_to_all(copies, axes, 0, 0, tiled=True)

MIB = 1024 * 1024
SMEM = pl.BlockSpec(memory_space=pltpu.SMEM)
VMEM = pl.BlockSpec(memory_space=pltpu.VMEM)
HBM = pl.BlockSpec(memory_space=pltpu.HBM)


def intake(pick, received, fresh, query, up_rows, n_copies):
    req_dev, n_rows, head_dim = query.shape
    n_steps = fresh.shape[0]
    _, page_size, width_two = received.shape
    max_pages = pick.shape[0] - 8
    pages = max_pages + 1
    group = n_rows // n_steps
    scale = 1.0 / math.sqrt(head_dim)
    def kernel(pick_ref, recv_ref, fresh_ref, q_ref, up_hbm, cache_ref, mixed_ref, up_ref, buf, scores, probs, heads, out_sems, up_sem):
        def copy_out(r):
            return pltpu.make_async_copy(buf.at[r], cache_ref.at[r], out_sems.at[r])

        up_copy = pltpu.make_async_copy(up_hbm, up_ref, up_sem)
        up_copy.start()
        row_at = lax.broadcasted_iota(jnp.int32, (page_size, width_two), 0)
        tokens_new = [fresh_ref[s].astype(jnp.float32) for s in range(n_steps)]
        for r in range(req_dev):

            def move(p, carry):
                buf[r, p] = recv_ref[pick_ref[p, r]]
                return carry

            lax.fori_loop(0, max_pages, move, 0, unroll=16)
            length = pick_ref[max_pages, r]
            full = length // page_size

            def clear(p, carry):
                buf[r, p] = jnp.zeros((page_size, width_two), buf.dtype)
                return carry

            lax.fori_loop(full + 1, pages, clear, 0)
            edge = buf[r, full].astype(jnp.float32)
            buf[r, full] = jnp.where(row_at < length % page_size, edge, 0.0).astype(buf.dtype)
            for s in range(n_steps):
                at = length + s
                page = buf[r, at // page_size].astype(jnp.float32)
                token = tokens_new[s][r : r + 1]
                buf[r, at // page_size] = jnp.where(
                    row_at == at % page_size, token, page
                ).astype(buf.dtype)
            copy_out(r).start()
        for r in range(req_dev):
            keys = buf[r, :, :, :head_dim].reshape(pages * page_size, head_dim)
            part = scale * lax.dot_general(
                q_ref[r], keys, (((1,), (1,)), ((), ())), preferred_element_type=jnp.float32
            )
            last = pick_ref[max_pages, r] + lax.broadcasted_iota(jnp.int32, part.shape, 0) // group
            scores[r * n_rows : (r + 1) * n_rows] = jnp.where(
                lax.broadcasted_iota(jnp.int32, part.shape, 1) <= last, part, -jnp.inf
            )
        expo = jnp.exp(scores[...] - jnp.max(scores[...], axis=1, keepdims=True))
        probs[...] = (expo / jnp.sum(expo, axis=1, keepdims=True)).astype(probs.dtype)
        for r in range(req_dev):
            values = buf[r, :, :, head_dim:].reshape(pages * page_size, head_dim)
            head_out = jnp.dot(
                probs[r * n_rows : (r + 1) * n_rows], values, preferred_element_type=jnp.float32
            )
            for i in range(n_rows):
                heads[i, r : r + 1, :] = head_out[i : i + 1, :]
        for g in range(group):
            block = jnp.concatenate([heads[s * group + g] for s in range(n_steps)], axis=0)
            block = block.astype(mixed_ref.dtype)
            for k in range(n_copies):
                mixed_ref[k, :, g * head_dim : (g + 1) * head_dim] = block
        for r in range(req_dev):
            copy_out(r).wait()
        up_copy.wait()

    return pl.pallas_call(
        kernel,
        in_specs=[SMEM, VMEM, VMEM, VMEM, HBM],
        out_specs=[HBM, VMEM, VMEM],
        out_shape=[
            jax.ShapeDtypeStruct((req_dev, pages, page_size, width_two), received.dtype),
            jax.ShapeDtypeStruct(
                (n_copies, n_steps * req_dev, group * head_dim), received.dtype
            ),
            pltpu.VMEM(up_rows.shape, up_rows.dtype),
        ],
        scratch_shapes=[
            pltpu.VMEM((req_dev, pages, page_size, width_two), received.dtype),
            pltpu.VMEM((req_dev * n_rows, pages * page_size), jnp.float32),
            pltpu.VMEM((req_dev * n_rows, pages * page_size), jnp.bfloat16),
            pltpu.VMEM((n_rows, req_dev, head_dim), jnp.float32),
            pltpu.SemaphoreType.DMA((req_dev,)),
            pltpu.SemaphoreType.DMA,
        ],
        compiler_params=pltpu.CompilerParams(vmem_limit_bytes=20 * MIB),
        name="intake",
    )(pick, received, fresh, query, pltpu.with_memory_space_constraint(up_rows, pltpu.HBM))


NT = (((1,), (1,)), ((), ()))


def scale_rows(x_ref, gain_ref, scaled):
    blocks, _, cols = x_ref.shape
    squares = 0.0
    for i in range(blocks):
        wide = x_ref[i].astype(jnp.float32)
        square = wide * wide
        squares += sum(square[:, k * 128 : (k + 1) * 128] for k in range(cols // 128))
        scaled[:, i * cols : (i + 1) * cols] = (
            wide * gain_ref[:, i * cols : (i + 1) * cols]
        ).astype(scaled.dtype)
    mean = jnp.sum(squares, axis=1, keepdims=True) * (1.0 / (blocks * cols))
    return lax.rsqrt(mean + 1e-05)


def activate(gate, upper):
    return (gate / (1.0 + jnp.exp(-gate)) * upper).astype(jnp.bfloat16)


def down_to(out_ref, act, down_ref):
    chips, n_tensor, rows_dev, cols_out = out_ref.shape
    for t in range(n_tensor):
        out = jnp.dot(
            act,
            down_ref[:, t * cols_out : (t + 1) * cols_out],
            preferred_element_type=jnp.float32,
        )
        out_ref[:, t] = out.astype(out_ref.dtype).reshape(chips, rows_dev, cols_out)


def expand_own(hidden, gate_rows, up_rows, gain_row, place, rows_dev):
    _, rows, cols = hidden.shape
    units, width = up_rows.shape

    def kernel(place_ref, x_ref, gate_ref, up_ref, gain_ref, act_ref, part_ref, scaled):
        mine = pl.ds(pl.multiple_of(place_ref[2] * rows_dev, rows_dev), rows_dev)
        part_ref[...] = x_ref[place_ref[1], mine, :]
        inverse = scale_rows(x_ref, gain_ref, scaled)
        gate = lax.dot_general(scaled[...], gate_ref[...], NT, preferred_element_type=jnp.float32)
        upper = lax.dot_general(scaled[...], up_ref[...], NT, preferred_element_type=jnp.float32)
        act_ref[...] = activate(gate * inverse, upper * inverse)

    return pl.pallas_call(
        kernel,
        in_specs=[SMEM, VMEM, VMEM, VMEM, VMEM],
        out_specs=[VMEM] * 2,
        out_shape=[
            pltpu.VMEM((rows, units), jnp.bfloat16),
            jax.ShapeDtypeStruct((rows_dev, cols), hidden.dtype),
        ],
        scratch_shapes=[pltpu.VMEM((rows, width), jnp.bfloat16)],
        compiler_params=pltpu.CompilerParams(vmem_limit_bytes=24 * MIB),
        name="expand_own",
    )(place, hidden, gate_rows, up_rows, gain_row)


def feed_forward(hidden, gate_rows, up_rows, gain_row, w_down, n_tensor, rows_dev):
    _, rows, _ = hidden.shape
    units, width = w_down.shape

    def kernel(x_ref, gate_ref, up_ref, gain_ref, down_hbm, out_ref, down_ref, scaled, sem):
        down_copy = pltpu.make_async_copy(down_hbm, down_ref, sem)
        down_copy.start()
        inverse = scale_rows(x_ref, gain_ref, scaled)
        gate = lax.dot_general(scaled[...], gate_ref[...], NT, preferred_element_type=jnp.float32)
        upper = lax.dot_general(scaled[...], up_ref[...], NT, preferred_element_type=jnp.float32)
        act = activate(gate * inverse, upper * inverse)
        down_copy.wait()
        down_to(out_ref, act, down_ref)

    return pl.pallas_call(
        kernel,
        in_specs=[VMEM, VMEM, VMEM, VMEM, HBM],
        out_specs=[VMEM] * 2,
        out_shape=[
            jax.ShapeDtypeStruct(
                (rows // rows_dev, n_tensor, rows_dev, width // n_tensor), jnp.bfloat16
            ),
            pltpu.VMEM((units, width), jnp.bfloat16),
        ],
        scratch_shapes=[
            pltpu.VMEM((rows, width), jnp.bfloat16),
            pltpu.SemaphoreType.DMA,
        ],
        compiler_params=pltpu.CompilerParams(vmem_limit_bytes=28 * MIB),
        name="feed_forward",
    )(hidden, gate_rows, up_rows, gain_row, pltpu.with_memory_space_constraint(w_down, pltpu.HBM))


def shrink_own(act, w_down, n_tensor, rows_dev):
    def kernel(act_ref, down_ref, out_ref):
        down_to(out_ref, act_ref[...], down_ref)

    return pl.pallas_call(
        kernel,
        in_specs=[VMEM, VMEM],
        out_specs=VMEM,
        out_shape=jax.ShapeDtypeStruct(
            (act.shape[0] // rows_dev, n_tensor, rows_dev, w_down.shape[1] // n_tensor),
            jnp.bfloat16,
        ),
        compiler_params=pltpu.CompilerParams(vmem_limit_bytes=16 * MIB),
        name="shrink_own",
    )(act, w_down)


def add_pieces(pieces, hidden, n_steps):
    count, rows, cols = pieces.shape

    def kernel(pieces_ref, hidden_ref, out_ref):
        total = hidden_ref[...].astype(jnp.float32)
        for i in range(count):
            total += pieces_ref[i].astype(jnp.float32)
        out_ref[...] = total.reshape(n_steps, rows // n_steps, cols).astype(out_ref.dtype)

    return pl.pallas_call(
        kernel,
        in_specs=[VMEM, VMEM],
        out_specs=VMEM,
        out_shape=jax.ShapeDtypeStruct((n_steps, rows // n_steps, cols), pieces.dtype),
        compiler_params=pltpu.CompilerParams(vmem_limit_bytes=10 * MIB),
        name="add_pieces",
    )(pieces, hidden)


def exact_dot(left, right, contract):
    return lax.dot_general(
        left.astype(jnp.bfloat16),
        right.astype(jnp.bfloat16),
        (contract, ((), ())),
        preferred_element_type=jnp.float32,
    )


def pack_pages(place, page_loc, lengths, placement, pool, n_dp):
    pslots, page_size, width_two = pool.shape
    _, max_pages, n_req = page_loc.shape
    req_dev = n_req // n_dp
    capacity = pslots // n_dp
    low = 32

    def kernel(place_ref, loc_hbm, len_hbm, placement_hbm, pool_hbm, out_buf, pick_ref, loc, len_ref, placement_ref, pool_buf, rows_vec, rows, loc_sem, len_sem, placement_sem, pool_sem, rows_sem):
        me = place_ref[0]
        len_copy = pltpu.make_async_copy(len_hbm, len_ref, len_sem)
        placement_copy = pltpu.make_async_copy(placement_hbm, placement_ref, placement_sem)
        pool_copy = pltpu.make_async_copy(pool_hbm, pool_buf, pool_sem)
        loc_copy = pltpu.make_async_copy(loc_hbm.at[place_ref[1]], loc, loc_sem)
        loc_copy.start()
        len_copy.start()
        placement_copy.start()
        pool_copy.start()
        shape = (n_req, n_req)
        down = lax.broadcasted_iota(jnp.int32, shape, 0)
        across = lax.broadcasted_iota(jnp.int32, shape, 1)
        placement_copy.wait()
        slot_hot = jnp.where(placement_ref[...] == down, 1.0, 0.0)
        len_copy.wait()
        lens = jnp.broadcast_to(len_ref[...], (8, n_req))
        loc_copy.wait()
        at = loc[...]
        pieces = jnp.concatenate(
            [at // pslots, at % pslots // low, at % low, lens // low, lens % low], axis=0
        )
        by_slot = exact_dot(pieces.astype(jnp.float32), slot_hot, ((1,), (1,)))
        source = by_slot[:max_pages]
        row = by_slot[max_pages : 2 * max_pages] * low + by_slot[2 * max_pages : 3 * max_pages]
        len_row = by_slot[3 * max_pages : 3 * max_pages + 1] * low + by_slot[3 * max_pages + 8 : 3 * max_pages + 9]
        page_at = lax.broadcasted_iota(jnp.int32, (max_pages, n_req), 0).astype(jnp.float32)
        source = jnp.where(page_at * page_size < len_row, source, float(n_dp))
        mine = source == me.astype(jnp.float32)
        ones = jnp.where(mine, 1.0, 0.0)
        earlier = jnp.where(
            lax.broadcasted_iota(jnp.int32, (max_pages, max_pages), 1)
            < lax.broadcasted_iota(jnp.int32, (max_pages, max_pages), 0),
            1.0,
            0.0,
        )
        in_group = jnp.where((down // req_dev == across // req_dev) & (down < across), 1.0, 0.0)
        count = jnp.broadcast_to(jnp.sum(ones, axis=0, keepdims=True), (8, n_req))
        rank = exact_dot(earlier, ones, ((1,), (0,))) + exact_dot(count, in_group, ((1,), (0,)))[:1]
        rank = jnp.where(mine, rank, -1.0)
        found = jnp.concatenate(
            [
                jnp.sum(jnp.where(rank == float(k), row, 0.0), axis=0, keepdims=True)
                for k in range(capacity)
            ],
            axis=0,
        ).astype(jnp.int32)
        group = jnp.where(down // req_dev == across, 1.0, 0.0)
        high_part = exact_dot((found // low).astype(jnp.float32), group, ((1,), (0,)))
        low_part = exact_dot((found % low).astype(jnp.float32), group, ((1,), (0,)))
        rows_vec[...] = (high_part * low + low_part).astype(jnp.int32)
        rows_copy = pltpu.make_async_copy(rows_vec, rows, rows_sem)
        rows_copy.start()
        own = jnp.where(down == me * req_dev + across % req_dev, 1.0, 0.0)
        ahead = jnp.concatenate([source, jnp.floor(len_row * (1.0 / low)), len_row - jnp.floor(len_row * (1.0 / low)) * low], axis=0)
        ahead = jnp.concatenate([ahead, jnp.zeros((6, n_req), jnp.float32)], axis=0)
        own_cols = exact_dot(ahead, own, ((1,), (0,)))
        lane = lax.broadcasted_iota(jnp.int32, (max_pages, n_req), 1)
        hit = own_cols[:max_pages] == (lane // req_dev).astype(jnp.float32)
        ones = jnp.where(hit, 1.0, 0.0)
        count = jnp.broadcast_to(jnp.sum(ones, axis=0, keepdims=True), (8, n_req))
        rank = exact_dot(earlier, ones, ((1,), (0,))) + exact_dot(count, in_group, ((1,), (0,)))[:1]
        spot = jnp.where(hit, rank + 1.0, 0.0)
        requests = jnp.where(down % req_dev == across, 1.0, 0.0)
        base = jnp.where(hit, (lane // req_dev).astype(jnp.float32), 0.0)
        pick = exact_dot(base, requests, ((1,), (0,))) * capacity
        pick += exact_dot(spot, requests, ((1,), (0,))) - 1.0
        own_len = own_cols[max_pages : max_pages + 1] * low + own_cols[max_pages + 1 : max_pages + 2]
        pick_ref[:max_pages] = jnp.maximum(pick, 0.0).astype(jnp.int32)
        pick_ref[max_pages:] = jnp.broadcast_to(own_len, (8, n_req)).astype(jnp.int32)
        rows_copy.wait()
        pool_copy.wait()

        for d in range(n_dp):

            def move(k, carry):
                out_buf[d * capacity + k] = pool_buf[rows[k, d]]
                return carry

            lax.fori_loop(0, capacity, move, 0, unroll=16)

    return pl.pallas_call(
        kernel,
        in_specs=[SMEM, HBM, HBM, HBM, HBM],
        out_specs=[VMEM, VMEM],
        out_shape=[
            jax.ShapeDtypeStruct(pool.shape, pool.dtype),
            jax.ShapeDtypeStruct((max_pages + 8, n_req), jnp.int32),
        ],
        scratch_shapes=[
            pltpu.VMEM((max_pages, n_req), jnp.int32),
            pltpu.VMEM((1, n_req), jnp.int32),
            pltpu.VMEM((1, n_req), jnp.int32),
            pltpu.VMEM(pool.shape, pool.dtype),
            pltpu.VMEM((capacity, n_req), jnp.int32),
            pltpu.SMEM((capacity, n_req), jnp.int32),
            pltpu.SemaphoreType.DMA,
            pltpu.SemaphoreType.DMA,
            pltpu.SemaphoreType.DMA,
            pltpu.SemaphoreType.DMA,
            pltpu.SemaphoreType.DMA,
        ],
        compiler_params=pltpu.CompilerParams(vmem_limit_bytes=20 * MIB),
        name="pack_pages",
    )(
        place,
        *[
            pltpu.with_memory_space_constraint(array, pltpu.HBM)
            for array in (page_loc, lengths, placement, pool)
        ],
    )


def add_cores(ours, from_core):
    def kernel(a_ref, b_ref, out_ref):
        for i in range(ours.shape[0]):
            out_ref[i] = (a_ref[i].astype(jnp.float32) + b_ref[i].astype(jnp.float32)).astype(
                out_ref.dtype
            )

    return pl.pallas_call(
        kernel,
        in_specs=[VMEM, VMEM],
        out_specs=VMEM,
        out_shape=jax.ShapeDtypeStruct(ours.shape, ours.dtype),
        compiler_params=pltpu.CompilerParams(vmem_limit_bytes=12 * MIB),
        name="add_cores",
    )(ours, from_core)


def per_device(
    kv_pool,
    page_loc,
    lengths,
    placement,
    queries,
    new_kv,
    resid_in,
    w_out,
    ffn_gain,
    w_gate,
    w_up,
    w_down,
):
    n_dp = lax.axis_size(DP)
    n_tensor = lax.axis_size(TENSOR)
    dev_dp = lax.axis_index(DP)
    dev_chip = lax.axis_index(CHIP_DP)
    dev_tensor = lax.axis_index(TENSOR)
    core = lax.axis_index("c")
    pslots, _, page_size, width_two = kv_pool.shape
    head_dim = width_two // 2
    n_req = lengths.shape[0]
    req_dev = n_req // n_dp
    max_pages = page_loc.shape[2]
    max_len = max_pages * page_size
    cache_len = max_len + page_size
    n_steps = queries.shape[0]
    hq_dev = queries.shape[2]
    width = ffn_gain.shape[0]
    rows_dev = n_steps * req_dev
    chips_dp = n_dp // 2
    rows_core = n_steps * n_req // 2
    capacity = pslots // n_dp

    place = jnp.stack([dev_dp, dev_tensor, dev_chip]).astype(jnp.int32)
    outgoing, pick = pack_pages(
        place,
        jnp.swapaxes(page_loc, 1, 2),
        lengths.reshape(1, n_req),
        placement.reshape(1, n_req),
        kv_pool.reshape(pslots, page_size, width_two),
        n_dp,
    )
    query = jnp.transpose(queries, (1, 0, 2, 3)).reshape(req_dev, n_steps * hq_dev, head_dim)
    fresh = new_kv.reshape(n_steps, req_dev, width_two)

    cols_dev = width // n_dp
    cols_chip = 2 * cols_dev
    swap = [(0, 1), (1, 0)]

    def both(own, other):
        return jnp.where(
            core == 0,
            jnp.concatenate([own, other], axis=-1),
            jnp.concatenate([other, own], axis=-1),
        )

    def resid_of(at_core):
        return lax.dynamic_slice(
            resid_in,
            (0, (2 * dev_tensor + at_core) * req_dev, 0),
            (n_steps, req_dev, cols_dev),
        ).reshape(rows_dev, cols_dev)

    resid_blk = both(resid_of(core), lax.ppermute(resid_of(1 - core), "c", swap))
    w_other = lax.ppermute(w_out, "c", swap)
    outgoing, pick, query, resid_blk, w_other, place = lax.optimization_barrier(
        (outgoing, pick, query, resid_blk, w_other, place)
    )
    received = lax.all_to_all(
        outgoing.reshape(n_dp, capacity, page_size, width_two), DP, 0, 0, tiled=True
    )
    cache, mixed_copies, up_near = intake(
        pick,
        received.reshape(pslots, page_size, width_two),
        fresh,
        query,
        jnp.swapaxes(w_up, 0, 1),
        chips_dp,
    )

    w_both = both(w_out, w_other)
    mixed_rows = lax.all_to_all(mixed_copies, CHIP_DP, 0, 0, tiled=True).reshape(
        rows_core, hq_dev * head_dim
    )
    partial_out = jnp.dot(mixed_rows, w_both, preferred_element_type=jnp.float32).astype(
        jnp.bfloat16
    )
    rows_blk = rows_core // n_tensor
    parts = lax.all_to_all(
        partial_out.reshape(n_tensor, rows_blk, cols_chip), TENSOR, 0, 0, tiled=True
    )
    hidden_blk = (
        resid_blk.astype(jnp.float32) + jnp.sum(parts.astype(jnp.float32), axis=0)
    ).astype(jnp.bfloat16)
    own_rows = to_all(hidden_blk, CHIPS, chips_dp * n_tensor).reshape(
        chips_dp, rows_core, cols_chip
    )
    other_rows = lax.ppermute(own_rows, "c", swap)
    gate_rows = jnp.swapaxes(w_gate, 0, 1)
    gain_row = ffn_gain.reshape(1, width)
    width_out = width // n_tensor

    act_own, own_hidden = expand_own(own_rows, gate_rows, up_near, gain_row, place, rows_dev)
    other_rows, act_own = lax.optimization_barrier((other_rows, act_own))
    theirs, down_near = feed_forward(
        other_rows, gate_rows, up_near, gain_row, w_down, n_tensor, rows_dev
    )
    from_core = lax.ppermute(theirs, "c", swap)
    ours = shrink_own(act_own, down_near, n_tensor, rows_dev)
    chip_sum = add_cores(ours, from_core).reshape(chips_dp * n_tensor, rows_dev, width_out)
    pieces = lax.all_to_all(chip_sum, CHIPS, 0, 0, tiled=True)
    block_out = add_pieces(pieces, own_hidden, n_steps)
    return (block_out, cache.reshape(1, req_dev, cache_len, width_two))


def solution(mesh):
    fine = Mesh(mesh.devices.reshape(2, 4, 2, 4, 2), ("yh", "x", "c", "z", "yl"))
    placed = (
        P(DP, TENSOR, None, None),
        P(),
        P(),
        P(),
        P(None, DP, TENSOR, None),
        P(None, DP, TENSOR, None),
        P(None, None, DP),
        P(TENSOR, DP),
        P(),
        P(None, DP + TENSOR),
        P(None, DP + TENSOR),
        P(DP + TENSOR, None),
    )
    return jax.shard_map(
        per_device,
        mesh=fine,
        in_specs=placed,
        out_specs=(P(None, DP, TENSOR), P(TENSOR, DP, None, None)),
        check_vma=False,
    )
```

```python
import math

import jax
import jax.numpy as jnp
from jax import lax
from jax.experimental import pallas as pl
from jax.experimental.pallas import tpu as pltpu
from jax.sharding import Mesh, PartitionSpec as P

DP = ("yh", "x", "c")
CHIP_DP = ("yh", "x")
TENSOR = ("z", "yl")
CHIPS = ("yh", "x", "z", "yl")
MIB = 1024 * 1024
SMEM = pl.BlockSpec(memory_space=pltpu.SMEM)
VMEM = pl.BlockSpec(memory_space=pltpu.VMEM)
HBM = pl.BlockSpec(memory_space=pltpu.HBM)


def intake(pick, received, fresh, query, up_rows, up_begun, n_copies):
    req_dev, n_rows, head_dim = query.shape
    n_steps = fresh.shape[0]
    _, page_size, width_two = received.shape
    max_pages = pick.shape[0] - 8
    pages = max_pages + 1
    group = n_rows // n_steps
    scale = 1.0 / math.sqrt(head_dim)

    def kernel(pick_ref, recv_ref, fresh_ref, q_ref, up_hbm, up_in, cache_ref, mixed_ref, up_ref, buf, scores, probs, heads, out_sems, up_sem):
        def copy_out(r):
            return pltpu.make_async_copy(buf.at[r], cache_ref.at[r], out_sems.at[r])

        rest = pl.ds(up_hbm.shape[0] // 2, up_hbm.shape[0] // 2)
        up_copy = pltpu.make_async_copy(up_hbm.at[rest], up_ref.at[rest], up_sem)
        up_copy.start()
        row_at = lax.broadcasted_iota(jnp.int32, (page_size, width_two), 0)
        tokens_new = [fresh_ref[s].astype(jnp.float32) for s in range(n_steps)]
        for r in range(req_dev):

            def move(p, carry):
                buf[r, p] = recv_ref[pick_ref[p, r]]
                return carry

            lax.fori_loop(0, max_pages, move, 0, unroll=16)
            length = pick_ref[max_pages, r]
            full = length // page_size

            def clear(p, carry):
                buf[r, p] = jnp.zeros((page_size, width_two), buf.dtype)
                return carry

            lax.fori_loop(full + 1, pages, clear, 0)
            edge = buf[r, full].astype(jnp.float32)
            buf[r, full] = jnp.where(row_at < length % page_size, edge, 0.0).astype(buf.dtype)
            for s in range(n_steps):
                at = length + s
                page = buf[r, at // page_size].astype(jnp.float32)
                token = tokens_new[s][r : r + 1]
                buf[r, at // page_size] = jnp.where(
                    row_at == at % page_size, token, page
                ).astype(buf.dtype)
            copy_out(r).start()
        for r in range(req_dev):
            keys = buf[r, :, :, :head_dim].reshape(pages * page_size, head_dim)
            part = scale * lax.dot_general(
                q_ref[r], keys, (((1,), (1,)), ((), ())), preferred_element_type=jnp.float32
            )
            last = pick_ref[max_pages, r] + lax.broadcasted_iota(jnp.int32, part.shape, 0) // group
            scores[r * n_rows : (r + 1) * n_rows] = jnp.where(
                lax.broadcasted_iota(jnp.int32, part.shape, 1) <= last, part, -jnp.inf
            )
        expo = jnp.exp(scores[...] - jnp.max(scores[...], axis=1, keepdims=True))
        probs[...] = (expo / jnp.sum(expo, axis=1, keepdims=True)).astype(probs.dtype)
        for r in range(req_dev):
            values = buf[r, :, :, head_dim:].reshape(pages * page_size, head_dim)
            head_out = jnp.dot(
                probs[r * n_rows : (r + 1) * n_rows], values, preferred_element_type=jnp.float32
            )
            for i in range(n_rows):
                heads[i, r : r + 1, :] = head_out[i : i + 1, :]
        for g in range(group):
            block = jnp.concatenate([heads[s * group + g] for s in range(n_steps)], axis=0)
            block = block.astype(mixed_ref.dtype)
            for k in range(n_copies):
                mixed_ref[k, :, g * head_dim : (g + 1) * head_dim] = block
        for r in range(req_dev):
            copy_out(r).wait()
        up_copy.wait()

    return pl.pallas_call(
        kernel,
        in_specs=[SMEM, VMEM, VMEM, VMEM, HBM, VMEM],
        out_specs=[HBM, VMEM, VMEM],
        out_shape=[
            jax.ShapeDtypeStruct((req_dev, pages, page_size, width_two), received.dtype),
            jax.ShapeDtypeStruct(
                (n_copies, n_steps * req_dev, group * head_dim), received.dtype
            ),
            pltpu.VMEM(up_rows.shape, up_rows.dtype),
        ],
        scratch_shapes=[
            pltpu.VMEM((req_dev, pages, page_size, width_two), received.dtype),
            pltpu.VMEM((req_dev * n_rows, pages * page_size), jnp.float32),
            pltpu.VMEM((req_dev * n_rows, pages * page_size), jnp.bfloat16),
            pltpu.VMEM((n_rows, req_dev, head_dim), jnp.float32),
            pltpu.SemaphoreType.DMA((req_dev,)),
            pltpu.SemaphoreType.DMA,
        ],
        compiler_params=pltpu.CompilerParams(vmem_limit_bytes=20 * MIB),
        input_output_aliases={5: 2},
        name="intake",
    )(pick, received, fresh, query, pltpu.with_memory_space_constraint(up_rows, pltpu.HBM), up_begun)


NT = (((1,), (1,)), ((), ()))


def scale_rows(x_ref, gain_ref, scaled):
    blocks, _, cols = x_ref.shape
    squares = 0.0
    for i in range(blocks):
        wide = x_ref[i].astype(jnp.float32)
        square = wide * wide
        squares += sum(square[:, k * 128 : (k + 1) * 128] for k in range(cols // 128))
        scaled[:, i * cols : (i + 1) * cols] = (
            wide * gain_ref[:, i * cols : (i + 1) * cols]
        ).astype(scaled.dtype)
    mean = jnp.sum(squares, axis=1, keepdims=True) * (1.0 / (blocks * cols))
    return lax.rsqrt(mean + 1e-05)


def activate(gate, upper):
    return (gate / (1.0 + jnp.exp(-gate)) * upper).astype(jnp.bfloat16)


def down_to(out_ref, act, down_ref):
    chips, n_tensor, rows_dev, cols_out = out_ref.shape
    for t in range(n_tensor):
        out = jnp.dot(
            act,
            down_ref[:, t * cols_out : (t + 1) * cols_out],
            preferred_element_type=jnp.float32,
        )
        out_ref[:, t] = out.astype(out_ref.dtype).reshape(chips, rows_dev, cols_out)


def expand_own(hidden, gate_rows, up_rows, gain_row, place, rows_dev):
    _, rows, cols = hidden.shape
    units, width = up_rows.shape

    def kernel(place_ref, x_ref, gate_ref, up_ref, gain_ref, act_ref, part_ref, scaled):
        mine = pl.ds(pl.multiple_of(place_ref[2] * rows_dev, rows_dev), rows_dev)
        part_ref[...] = x_ref[place_ref[1], mine, :]
        inverse = scale_rows(x_ref, gain_ref, scaled)
        gate = lax.dot_general(scaled[...], gate_ref[...], NT, preferred_element_type=jnp.float32)
        upper = lax.dot_general(scaled[...], up_ref[...], NT, preferred_element_type=jnp.float32)
        act_ref[...] = activate(gate * inverse, upper * inverse)

    return pl.pallas_call(
        kernel,
        in_specs=[SMEM, VMEM, VMEM, VMEM, VMEM],
        out_specs=[VMEM] * 2,
        out_shape=[
            pltpu.VMEM((rows, units), jnp.bfloat16),
            jax.ShapeDtypeStruct((rows_dev, cols), hidden.dtype),
        ],
        scratch_shapes=[pltpu.VMEM((rows, width), jnp.bfloat16)],
        compiler_params=pltpu.CompilerParams(vmem_limit_bytes=24 * MIB),
        name="expand_own",
    )(place, hidden, gate_rows, up_rows, gain_row)


def feed_forward(hidden, gate_rows, up_rows, gain_row, w_down, n_tensor, rows_dev):
    _, rows, _ = hidden.shape
    units, width = w_down.shape

    def kernel(x_ref, gate_ref, up_ref, gain_ref, down_hbm, out_ref, down_ref, scaled, sem):
        down_copy = pltpu.make_async_copy(down_hbm, down_ref, sem)
        down_copy.start()
        inverse = scale_rows(x_ref, gain_ref, scaled)
        gate = lax.dot_general(scaled[...], gate_ref[...], NT, preferred_element_type=jnp.float32)
        upper = lax.dot_general(scaled[...], up_ref[...], NT, preferred_element_type=jnp.float32)
        act = activate(gate * inverse, upper * inverse)
        down_copy.wait()
        down_to(out_ref, act, down_ref)

    return pl.pallas_call(
        kernel,
        in_specs=[VMEM, VMEM, VMEM, VMEM, HBM],
        out_specs=[VMEM] * 2,
        out_shape=[
            jax.ShapeDtypeStruct(
                (rows // rows_dev, n_tensor, rows_dev, width // n_tensor), jnp.bfloat16
            ),
            pltpu.VMEM((units, width), jnp.bfloat16),
        ],
        scratch_shapes=[
            pltpu.VMEM((rows, width), jnp.bfloat16),
            pltpu.SemaphoreType.DMA,
        ],
        compiler_params=pltpu.CompilerParams(vmem_limit_bytes=28 * MIB),
        name="feed_forward",
    )(hidden, gate_rows, up_rows, gain_row, pltpu.with_memory_space_constraint(w_down, pltpu.HBM))


def shrink_own(act, w_down, n_tensor, rows_dev):
    def kernel(act_ref, down_ref, out_ref):
        down_to(out_ref, act_ref[...], down_ref)

    return pl.pallas_call(
        kernel,
        in_specs=[VMEM, VMEM],
        out_specs=VMEM,
        out_shape=jax.ShapeDtypeStruct(
            (act.shape[0] // rows_dev, n_tensor, rows_dev, w_down.shape[1] // n_tensor),
            jnp.bfloat16,
        ),
        compiler_params=pltpu.CompilerParams(vmem_limit_bytes=16 * MIB),
        name="shrink_own",
    )(act, w_down)


def add_pieces(pieces, hidden, n_steps):
    count, rows, cols = pieces.shape

    def kernel(pieces_ref, hidden_ref, out_ref):
        total = hidden_ref[...].astype(jnp.float32)
        for i in range(count):
            total += pieces_ref[i].astype(jnp.float32)
        out_ref[...] = total.reshape(n_steps, rows // n_steps, cols).astype(out_ref.dtype)

    return pl.pallas_call(
        kernel,
        in_specs=[VMEM, VMEM],
        out_specs=VMEM,
        out_shape=jax.ShapeDtypeStruct((n_steps, rows // n_steps, cols), pieces.dtype),
        compiler_params=pltpu.CompilerParams(vmem_limit_bytes=10 * MIB),
        name="add_pieces",
    )(pieces, hidden)


def exact_dot(left, right, contract):
    return lax.dot_general(
        left.astype(jnp.bfloat16),
        right.astype(jnp.bfloat16),
        (contract, ((), ())),
        preferred_element_type=jnp.float32,
    )


def pack_pages(place, page_loc, lengths, placement, pool, up_rows, n_dp):
    pslots, page_size, width_two = pool.shape
    _, max_pages, n_req = page_loc.shape
    req_dev = n_req // n_dp
    capacity = pslots // n_dp
    low = 32

    def kernel(place_ref, loc_hbm, len_hbm, placement_hbm, pool_hbm, up_hbm, out_buf, pick_ref, up_ref, loc, len_ref, placement_ref, pool_buf, rows_vec, rows, loc_sem, len_sem, placement_sem, pool_sem, rows_sem, up_sem):
        me = place_ref[0]
        len_copy = pltpu.make_async_copy(len_hbm, len_ref, len_sem)
        placement_copy = pltpu.make_async_copy(placement_hbm, placement_ref, placement_sem)
        pool_copy = pltpu.make_async_copy(pool_hbm, pool_buf, pool_sem)
        loc_copy = pltpu.make_async_copy(loc_hbm.at[place_ref[1]], loc, loc_sem)
        loc_copy.start()
        len_copy.start()
        placement_copy.start()
        pool_copy.start()
        shape = (n_req, n_req)
        down = lax.broadcasted_iota(jnp.int32, shape, 0)
        across = lax.broadcasted_iota(jnp.int32, shape, 1)
        placement_copy.wait()
        slot_hot = jnp.where(placement_ref[...] == down, 1.0, 0.0)
        len_copy.wait()
        lens = jnp.broadcast_to(len_ref[...], (8, n_req))
        loc_copy.wait()
        at = loc[...]
        pieces = jnp.concatenate(
            [at // pslots, at % pslots // low, at % low, lens // low, lens % low], axis=0
        )
        by_slot = exact_dot(pieces.astype(jnp.float32), slot_hot, ((1,), (1,)))
        source = by_slot[:max_pages]
        row = by_slot[max_pages : 2 * max_pages] * low + by_slot[2 * max_pages : 3 * max_pages]
        len_row = by_slot[3 * max_pages : 3 * max_pages + 1] * low + by_slot[3 * max_pages + 8 : 3 * max_pages + 9]
        page_at = lax.broadcasted_iota(jnp.int32, (max_pages, n_req), 0).astype(jnp.float32)
        source = jnp.where(page_at * page_size < len_row, source, float(n_dp))
        mine = source == me.astype(jnp.float32)
        ones = jnp.where(mine, 1.0, 0.0)
        earlier = jnp.where(
            lax.broadcasted_iota(jnp.int32, (max_pages, max_pages), 1)
            < lax.broadcasted_iota(jnp.int32, (max_pages, max_pages), 0),
            1.0,
            0.0,
        )
        in_group = jnp.where((down // req_dev == across // req_dev) & (down < across), 1.0, 0.0)
        count = jnp.broadcast_to(jnp.sum(ones, axis=0, keepdims=True), (8, n_req))
        rank = exact_dot(earlier, ones, ((1,), (0,))) + exact_dot(count, in_group, ((1,), (0,)))[:1]
        rank = jnp.where(mine, rank, -1.0)
        found = jnp.concatenate(
            [
                jnp.sum(jnp.where(rank == float(k), row, 0.0), axis=0, keepdims=True)
                for k in range(capacity)
            ],
            axis=0,
        ).astype(jnp.int32)
        group = jnp.where(down // req_dev == across, 1.0, 0.0)
        high_part = exact_dot((found // low).astype(jnp.float32), group, ((1,), (0,)))
        low_part = exact_dot((found % low).astype(jnp.float32), group, ((1,), (0,)))
        rows_vec[...] = (high_part * low + low_part).astype(jnp.int32)
        rows_copy = pltpu.make_async_copy(rows_vec, rows, rows_sem)
        rows_copy.start()
        own = jnp.where(down == me * req_dev + across % req_dev, 1.0, 0.0)
        ahead = jnp.concatenate([source, jnp.floor(len_row * (1.0 / low)), len_row - jnp.floor(len_row * (1.0 / low)) * low], axis=0)
        ahead = jnp.concatenate([ahead, jnp.zeros((6, n_req), jnp.float32)], axis=0)
        own_cols = exact_dot(ahead, own, ((1,), (0,)))
        lane = lax.broadcasted_iota(jnp.int32, (max_pages, n_req), 1)
        hit = own_cols[:max_pages] == (lane // req_dev).astype(jnp.float32)
        ones = jnp.where(hit, 1.0, 0.0)
        count = jnp.broadcast_to(jnp.sum(ones, axis=0, keepdims=True), (8, n_req))
        rank = exact_dot(earlier, ones, ((1,), (0,))) + exact_dot(count, in_group, ((1,), (0,)))[:1]
        spot = jnp.where(hit, rank + 1.0, 0.0)
        requests = jnp.where(down % req_dev == across, 1.0, 0.0)
        base = jnp.where(hit, (lane // req_dev).astype(jnp.float32), 0.0)
        pick = exact_dot(base, requests, ((1,), (0,))) * capacity
        pick += exact_dot(spot, requests, ((1,), (0,))) - 1.0
        own_len = own_cols[max_pages : max_pages + 1] * low + own_cols[max_pages + 1 : max_pages + 2]
        pick_ref[:max_pages] = jnp.maximum(pick, 0.0).astype(jnp.int32)
        pick_ref[max_pages:] = jnp.broadcast_to(own_len, (8, n_req)).astype(jnp.int32)
        rows_copy.wait()
        pool_copy.wait()
        first = pl.ds(0, up_hbm.shape[0] // 2)
        up_copy = pltpu.make_async_copy(up_hbm.at[first], up_ref.at[first], up_sem)
        up_copy.start()

        for d in range(n_dp):

            def move(k, carry):
                out_buf[d * capacity + k] = pool_buf[rows[k, d]]
                return carry

            lax.fori_loop(0, capacity, move, 0, unroll=16)
        up_copy.wait()

    return pl.pallas_call(
        kernel,
        in_specs=[SMEM, HBM, HBM, HBM, HBM, HBM],
        out_specs=[VMEM, VMEM, VMEM],
        out_shape=[
            jax.ShapeDtypeStruct(pool.shape, pool.dtype),
            jax.ShapeDtypeStruct((max_pages + 8, n_req), jnp.int32),
            pltpu.VMEM(up_rows.shape, up_rows.dtype),
        ],
        scratch_shapes=[
            pltpu.VMEM((max_pages, n_req), jnp.int32),
            pltpu.VMEM((1, n_req), jnp.int32),
            pltpu.VMEM((1, n_req), jnp.int32),
            pltpu.VMEM(pool.shape, pool.dtype),
            pltpu.VMEM((capacity, n_req), jnp.int32),
            pltpu.SMEM((capacity, n_req), jnp.int32),
            pltpu.SemaphoreType.DMA,
            pltpu.SemaphoreType.DMA,
            pltpu.SemaphoreType.DMA,
            pltpu.SemaphoreType.DMA,
            pltpu.SemaphoreType.DMA,
            pltpu.SemaphoreType.DMA,
        ],
        compiler_params=pltpu.CompilerParams(vmem_limit_bytes=20 * MIB),
        name="pack_pages",
    )(
        place,
        *[
            pltpu.with_memory_space_constraint(array, pltpu.HBM)
            for array in (page_loc, lengths, placement, pool, up_rows)
        ],
    )


def settle(parts, resid_own, resid_other, place, n_copies):
    n_parts, rows, cols = parts.shape
    n_steps, _, cols_dev = resid_own.shape
    req_dev = rows // n_steps

    def kernel(place_ref, parts_ref, own_ref, other_ref, out_ref):
        core = place_ref[3]
        both_rows = pl.ds(pl.multiple_of(place_ref[1] * 2 * req_dev, 2 * req_dev), 2 * req_dev)
        total = parts_ref[0].astype(jnp.float32)
        for i in range(1, n_parts):
            total += parts_ref[i].astype(jnp.float32)
        resid = []
        for ref in (own_ref, other_ref):
            steps = []
            for s in range(n_steps):
                wide = ref[s, both_rows, :].astype(jnp.float32)
                steps.append(jnp.where(core == 0, wide[:req_dev], wide[req_dev:]))
            resid.append(jnp.concatenate(steps, axis=0))
        left = jnp.where(core == 0, resid[0], resid[1])
        right = jnp.where(core == 0, resid[1], resid[0])
        hidden = (total + jnp.concatenate([left, right], axis=1)).astype(out_ref.dtype)
        for i in range(n_copies):
            out_ref[i] = hidden

    return pl.pallas_call(
        kernel,
        in_specs=[SMEM, VMEM, VMEM, VMEM],
        out_specs=VMEM,
        out_shape=jax.ShapeDtypeStruct((n_copies, rows, cols), parts.dtype),
        compiler_params=pltpu.CompilerParams(vmem_limit_bytes=10 * MIB),
        name="settle",
    )(place, parts, resid_own, resid_other)


def add_cores(ours, from_core):
    def kernel(a_ref, b_ref, out_ref):
        for i in range(ours.shape[0]):
            out_ref[i] = (a_ref[i].astype(jnp.float32) + b_ref[i].astype(jnp.float32)).astype(
                out_ref.dtype
            )

    return pl.pallas_call(
        kernel,
        in_specs=[VMEM, VMEM],
        out_specs=VMEM,
        out_shape=jax.ShapeDtypeStruct(ours.shape, ours.dtype),
        compiler_params=pltpu.CompilerParams(vmem_limit_bytes=12 * MIB),
        name="add_cores",
    )(ours, from_core)


def per_device(
    kv_pool,
    page_loc,
    lengths,
    placement,
    queries,
    new_kv,
    resid_in,
    w_out,
    ffn_gain,
    w_gate,
    w_up,
    w_down,
):
    n_dp = lax.axis_size(DP)
    n_tensor = lax.axis_size(TENSOR)
    dev_dp = lax.axis_index(DP)
    dev_chip = lax.axis_index(CHIP_DP)
    dev_tensor = lax.axis_index(TENSOR)
    core = lax.axis_index("c")
    pslots, _, page_size, width_two = kv_pool.shape
    head_dim = width_two // 2
    n_req = lengths.shape[0]
    req_dev = n_req // n_dp
    max_pages = page_loc.shape[2]
    max_len = max_pages * page_size
    cache_len = max_len + page_size
    n_steps = queries.shape[0]
    hq_dev = queries.shape[2]
    width = ffn_gain.shape[0]
    rows_dev = n_steps * req_dev
    chips_dp = n_dp // 2
    rows_core = n_steps * n_req // 2
    capacity = pslots // n_dp

    place = jnp.stack([dev_dp, dev_tensor, dev_chip, core]).astype(jnp.int32)
    up_rows = jnp.swapaxes(w_up, 0, 1)
    outgoing, pick, up_begun = pack_pages(
        place,
        jnp.swapaxes(page_loc, 1, 2),
        lengths.reshape(1, n_req),
        placement.reshape(1, n_req),
        kv_pool.reshape(pslots, page_size, width_two),
        up_rows,
        n_dp,
    )
    query = jnp.transpose(queries, (1, 0, 2, 3)).reshape(req_dev, n_steps * hq_dev, head_dim)
    fresh = new_kv.reshape(n_steps, req_dev, width_two)

    cols_dev = width // n_dp
    cols_chip = 2 * cols_dev
    swap = [(0, 1), (1, 0)]

    resid_other = lax.ppermute(resid_in, "c", swap)
    w_other = lax.ppermute(w_out, "c", swap)
    outgoing, pick, query, resid_other, w_other, place, first_core = lax.optimization_barrier(
        (outgoing, pick, query, resid_other, w_other, place, core == 0)
    )
    received = lax.all_to_all(
        outgoing.reshape(n_dp, capacity, page_size, width_two), DP, 0, 0, tiled=True
    )
    cache, mixed_copies, up_near = intake(
        pick,
        received.reshape(pslots, page_size, width_two),
        fresh,
        query,
        up_rows,
        up_begun,
        chips_dp,
    )

    w_both = jnp.where(
        first_core,
        jnp.concatenate([w_out, w_other], axis=-1),
        jnp.concatenate([w_other, w_out], axis=-1),
    )
    mixed_rows = lax.all_to_all(mixed_copies, CHIP_DP, 0, 0, tiled=True).reshape(
        rows_core, hq_dev * head_dim
    )
    partial_out = jnp.dot(mixed_rows, w_both, preferred_element_type=jnp.float32).astype(
        jnp.bfloat16
    )
    rows_blk = rows_core // n_tensor
    parts = lax.all_to_all(
        partial_out.reshape(n_tensor, rows_blk, cols_chip), TENSOR, 0, 0, tiled=True
    )
    hidden_copies = settle(parts, resid_in, resid_other, place, chips_dp * n_tensor)
    own_rows = lax.all_to_all(hidden_copies, CHIPS, 0, 0, tiled=True).reshape(
        chips_dp, rows_core, cols_chip
    )
    other_rows = lax.ppermute(own_rows, "c", swap)
    gate_rows = jnp.swapaxes(w_gate, 0, 1)
    gain_row = ffn_gain.reshape(1, width)
    width_out = width // n_tensor

    act_own, own_hidden = expand_own(own_rows, gate_rows, up_near, gain_row, place, rows_dev)
    other_rows, act_own = lax.optimization_barrier((other_rows, act_own))
    theirs, down_near = feed_forward(
        other_rows, gate_rows, up_near, gain_row, w_down, n_tensor, rows_dev
    )
    from_core = lax.ppermute(theirs, "c", swap)
    ours = shrink_own(act_own, down_near, n_tensor, rows_dev)
    chip_sum = add_cores(ours, from_core).reshape(chips_dp * n_tensor, rows_dev, width_out)
    pieces = lax.all_to_all(chip_sum, CHIPS, 0, 0, tiled=True)
    block_out = add_pieces(pieces, own_hidden, n_steps)
    return (block_out, cache.reshape(1, req_dev, cache_len, width_two))


def solution(mesh):
    fine = Mesh(mesh.devices.reshape(2, 4, 2, 4, 2), ("yh", "x", "c", "z", "yl"))
    placed = (
        P(DP, TENSOR, None, None),
        P(),
        P(),
        P(),
        P(None, DP, TENSOR, None),
        P(None, DP, TENSOR, None),
        P(None, None, DP),
        P(TENSOR, DP),
        P(),
        P(None, DP + TENSOR),
        P(None, DP + TENSOR),
        P(DP + TENSOR, None),
    )
    return jax.shard_map(
        per_device,
        mesh=fine,
        in_specs=placed,
        out_specs=(P(None, DP, TENSOR), P(TENSOR, DP, None, None)),
        check_vma=False,
    )
```

```python
import math

import jax
import jax.numpy as jnp
from jax import lax
from jax.experimental import pallas as pl
from jax.experimental.pallas import tpu as pltpu
from jax.sharding import Mesh, PartitionSpec as P

DP = ("yh", "x", "c")
CHIP_DP = ("yh", "x")
TENSOR = ("z", "yl")
CHIPS = ("yh", "x", "z", "yl")
MIB = 1024 * 1024
SMEM = pl.BlockSpec(memory_space=pltpu.SMEM)
VMEM = pl.BlockSpec(memory_space=pltpu.VMEM)
HBM = pl.BlockSpec(memory_space=pltpu.HBM)


def intake(pick, received, fresh, query, up_rows, up_begun, n_copies):
    req_dev, n_rows, head_dim = query.shape
    n_steps = fresh.shape[0]
    _, page_size, width_two = received.shape
    max_pages = pick.shape[0] - 8
    pages = max_pages + 1
    group = n_rows // n_steps
    scale = 1.0 / math.sqrt(head_dim)

    def kernel(pick_ref, recv_ref, fresh_ref, q_ref, up_hbm, up_in, cache_ref, mixed_ref, up_ref, buf, scores, probs, heads, out_sems, up_sem):
        def copy_out(r):
            return pltpu.make_async_copy(buf.at[r], cache_ref.at[r], out_sems.at[r])

        rest = pl.ds(up_hbm.shape[0] // 2, up_hbm.shape[0] // 2)
        up_copy = pltpu.make_async_copy(up_hbm.at[rest], up_ref.at[rest], up_sem)
        up_copy.start()
        row_at = lax.broadcasted_iota(jnp.int32, (page_size, width_two), 0)
        tokens_new = [fresh_ref[s].astype(jnp.float32) for s in range(n_steps)]
        for r in range(req_dev):

            def move(p, carry):
                buf[r, p] = recv_ref[pick_ref[p, r]]
                return carry

            lax.fori_loop(0, max_pages, move, 0, unroll=16)
            length = pick_ref[max_pages, r]
            full = length // page_size

            def clear(p, carry):
                buf[r, p] = jnp.zeros((page_size, width_two), buf.dtype)
                return carry

            lax.fori_loop(full + 1, pages, clear, 0)
            edge = buf[r, full].astype(jnp.float32)
            buf[r, full] = jnp.where(row_at < length % page_size, edge, 0.0).astype(buf.dtype)
            for s in range(n_steps):
                at = length + s
                page = buf[r, at // page_size].astype(jnp.float32)
                token = tokens_new[s][r : r + 1]
                buf[r, at // page_size] = jnp.where(
                    row_at == at % page_size, token, page
                ).astype(buf.dtype)
            copy_out(r).start()
        for r in range(req_dev):
            keys = buf[r, :, :, :head_dim].reshape(pages * page_size, head_dim)
            part = scale * lax.dot_general(
                q_ref[r], keys, (((1,), (1,)), ((), ())), preferred_element_type=jnp.float32
            )
            last = pick_ref[max_pages, r] + lax.broadcasted_iota(jnp.int32, part.shape, 0) // group
            scores[r * n_rows : (r + 1) * n_rows] = jnp.where(
                lax.broadcasted_iota(jnp.int32, part.shape, 1) <= last, part, -jnp.inf
            )
        expo = jnp.exp(scores[...] - jnp.max(scores[...], axis=1, keepdims=True))
        probs[...] = (expo / jnp.sum(expo, axis=1, keepdims=True)).astype(probs.dtype)
        for r in range(req_dev):
            values = buf[r, :, :, head_dim:].reshape(pages * page_size, head_dim)
            head_out = jnp.dot(
                probs[r * n_rows : (r + 1) * n_rows], values, preferred_element_type=jnp.float32
            )
            for i in range(n_rows):
                heads[i, r : r + 1, :] = head_out[i : i + 1, :]
        for g in range(group):
            block = jnp.concatenate([heads[s * group + g] for s in range(n_steps)], axis=0)
            block = block.astype(mixed_ref.dtype)
            for k in range(n_copies):
                mixed_ref[k, :, g * head_dim : (g + 1) * head_dim] = block
        for r in range(req_dev):
            copy_out(r).wait()
        up_copy.wait()

    return pl.pallas_call(
        kernel,
        in_specs=[SMEM, VMEM, VMEM, VMEM, HBM, VMEM],
        out_specs=[HBM, VMEM, VMEM],
        out_shape=[
            jax.ShapeDtypeStruct((req_dev, pages, page_size, width_two), received.dtype),
            jax.ShapeDtypeStruct(
                (n_copies, n_steps * req_dev, group * head_dim), received.dtype
            ),
            pltpu.VMEM(up_rows.shape, up_rows.dtype),
        ],
        scratch_shapes=[
            pltpu.VMEM((req_dev, pages, page_size, width_two), received.dtype),
            pltpu.VMEM((req_dev * n_rows, pages * page_size), jnp.float32),
            pltpu.VMEM((req_dev * n_rows, pages * page_size), jnp.bfloat16),
            pltpu.VMEM((n_rows, req_dev, head_dim), jnp.float32),
            pltpu.SemaphoreType.DMA((req_dev,)),
            pltpu.SemaphoreType.DMA,
        ],
        compiler_params=pltpu.CompilerParams(vmem_limit_bytes=20 * MIB),
        input_output_aliases={5: 2},
        name="intake",
    )(pick, received, fresh, query, pltpu.with_memory_space_constraint(up_rows, pltpu.HBM), up_begun)


NT = (((1,), (1,)), ((), ()))


def scale_rows(x_ref, gain_ref, scaled):
    blocks, _, cols = x_ref.shape
    squares = 0.0
    for i in range(blocks):
        wide = x_ref[i].astype(jnp.float32)
        square = wide * wide
        squares += sum(square[:, k * 128 : (k + 1) * 128] for k in range(cols // 128))
        scaled[:, i * cols : (i + 1) * cols] = (
            wide * gain_ref[:, i * cols : (i + 1) * cols]
        ).astype(scaled.dtype)
    mean = jnp.sum(squares, axis=1, keepdims=True) * (1.0 / (blocks * cols))
    return lax.rsqrt(mean + 1e-05)


def activate(gate, upper):
    return (gate / (1.0 + jnp.exp(-gate)) * upper).astype(jnp.bfloat16)


def down_to(out_ref, act, down_ref):
    n_tensor, chips, rows_dev, cols_out = out_ref.shape
    for t in range(n_tensor):
        out = jnp.dot(
            act,
            down_ref[:, t * cols_out : (t + 1) * cols_out],
            preferred_element_type=jnp.float32,
        )
        out_ref[t] = out.astype(out_ref.dtype).reshape(chips, rows_dev, cols_out)


def expand_own(hidden, gate_rows, up_rows, gain_row, place, rows_dev):
    _, rows, cols = hidden.shape
    units, width = up_rows.shape

    def kernel(place_ref, x_ref, gate_ref, up_ref, gain_ref, act_ref, part_ref, scaled):
        mine = pl.ds(pl.multiple_of(place_ref[2] * rows_dev, rows_dev), rows_dev)
        part_ref[...] = x_ref[place_ref[1], mine, :]
        inverse = scale_rows(x_ref, gain_ref, scaled)
        gate = lax.dot_general(scaled[...], gate_ref[...], NT, preferred_element_type=jnp.float32)
        upper = lax.dot_general(scaled[...], up_ref[...], NT, preferred_element_type=jnp.float32)
        act_ref[...] = activate(gate * inverse, upper * inverse)

    return pl.pallas_call(
        kernel,
        in_specs=[SMEM, VMEM, VMEM, VMEM, VMEM],
        out_specs=[VMEM] * 2,
        out_shape=[
            pltpu.VMEM((rows, units), jnp.bfloat16),
            jax.ShapeDtypeStruct((rows_dev, cols), hidden.dtype),
        ],
        scratch_shapes=[pltpu.VMEM((rows, width), jnp.bfloat16)],
        compiler_params=pltpu.CompilerParams(vmem_limit_bytes=24 * MIB),
        name="expand_own",
    )(place, hidden, gate_rows, up_rows, gain_row)


def feed_forward(hidden, gate_rows, up_rows, gain_row, w_down, n_tensor, rows_dev):
    _, rows, _ = hidden.shape
    units, width = w_down.shape

    def kernel(x_ref, gate_ref, up_ref, gain_ref, down_hbm, out_ref, down_ref, scaled, sem):
        down_copy = pltpu.make_async_copy(down_hbm, down_ref, sem)
        down_copy.start()
        inverse = scale_rows(x_ref, gain_ref, scaled)
        gate = lax.dot_general(scaled[...], gate_ref[...], NT, preferred_element_type=jnp.float32)
        upper = lax.dot_general(scaled[...], up_ref[...], NT, preferred_element_type=jnp.float32)
        act = activate(gate * inverse, upper * inverse)
        down_copy.wait()
        down_to(out_ref, act, down_ref)

    return pl.pallas_call(
        kernel,
        in_specs=[VMEM, VMEM, VMEM, VMEM, HBM],
        out_specs=[VMEM] * 2,
        out_shape=[
            jax.ShapeDtypeStruct(
                (n_tensor, rows // rows_dev, rows_dev, width // n_tensor), jnp.bfloat16
            ),
            pltpu.VMEM((units, width), jnp.bfloat16),
        ],
        scratch_shapes=[
            pltpu.VMEM((rows, width), jnp.bfloat16),
            pltpu.SemaphoreType.DMA,
        ],
        compiler_params=pltpu.CompilerParams(vmem_limit_bytes=28 * MIB),
        name="feed_forward",
    )(hidden, gate_rows, up_rows, gain_row, pltpu.with_memory_space_constraint(w_down, pltpu.HBM))


def shrink_own(act, w_down, n_tensor, rows_dev):
    def kernel(act_ref, down_ref, out_ref):
        down_to(out_ref, act_ref[...], down_ref)

    return pl.pallas_call(
        kernel,
        in_specs=[VMEM, VMEM],
        out_specs=VMEM,
        out_shape=jax.ShapeDtypeStruct(
            (n_tensor, act.shape[0] // rows_dev, rows_dev, w_down.shape[1] // n_tensor),
            jnp.bfloat16,
        ),
        compiler_params=pltpu.CompilerParams(vmem_limit_bytes=16 * MIB),
        name="shrink_own",
    )(act, w_down)


def add_pieces(pieces, hidden, n_steps):
    count, rows, cols = pieces.shape

    def kernel(pieces_ref, hidden_ref, out_ref):
        total = hidden_ref[...].astype(jnp.float32)
        for i in range(count):
            total += pieces_ref[i].astype(jnp.float32)
        out_ref[...] = total.reshape(n_steps, rows // n_steps, cols).astype(out_ref.dtype)

    return pl.pallas_call(
        kernel,
        in_specs=[VMEM, VMEM],
        out_specs=VMEM,
        out_shape=jax.ShapeDtypeStruct((n_steps, rows // n_steps, cols), pieces.dtype),
        compiler_params=pltpu.CompilerParams(vmem_limit_bytes=10 * MIB),
        name="add_pieces",
    )(pieces, hidden)


def exact_dot(left, right, contract):
    return lax.dot_general(
        left.astype(jnp.bfloat16),
        right.astype(jnp.bfloat16),
        (contract, ((), ())),
        preferred_element_type=jnp.float32,
    )


def pack_pages(place, page_loc, lengths, placement, pool, up_rows, n_dp):
    pslots, page_size, width_two = pool.shape
    _, max_pages, n_req = page_loc.shape
    req_dev = n_req // n_dp
    capacity = pslots // n_dp
    low = 32

    def kernel(place_ref, loc_hbm, len_hbm, placement_hbm, pool_hbm, up_hbm, out_buf, pick_ref, up_ref, loc, len_ref, placement_ref, pool_buf, rows_vec, rows, loc_sem, len_sem, placement_sem, pool_sem, rows_sem, up_sem):
        me = place_ref[0]
        len_copy = pltpu.make_async_copy(len_hbm, len_ref, len_sem)
        placement_copy = pltpu.make_async_copy(placement_hbm, placement_ref, placement_sem)
        pool_copy = pltpu.make_async_copy(pool_hbm, pool_buf, pool_sem)
        loc_copy = pltpu.make_async_copy(loc_hbm.at[place_ref[1]], loc, loc_sem)
        loc_copy.start()
        len_copy.start()
        placement_copy.start()
        pool_copy.start()
        shape = (n_req, n_req)
        down = lax.broadcasted_iota(jnp.int32, shape, 0)
        across = lax.broadcasted_iota(jnp.int32, shape, 1)
        placement_copy.wait()
        slot_hot = jnp.where(placement_ref[...] == down, 1.0, 0.0)
        len_copy.wait()
        lens = jnp.broadcast_to(len_ref[...], (8, n_req))
        loc_copy.wait()
        at = loc[...]
        pieces = jnp.concatenate(
            [at // pslots, at % pslots // low, at % low, lens // low, lens % low], axis=0
        )
        by_slot = exact_dot(pieces.astype(jnp.float32), slot_hot, ((1,), (1,)))
        source = by_slot[:max_pages]
        row = by_slot[max_pages : 2 * max_pages] * low + by_slot[2 * max_pages : 3 * max_pages]
        len_row = by_slot[3 * max_pages : 3 * max_pages + 1] * low + by_slot[3 * max_pages + 8 : 3 * max_pages + 9]
        page_at = lax.broadcasted_iota(jnp.int32, (max_pages, n_req), 0).astype(jnp.float32)
        source = jnp.where(page_at * page_size < len_row, source, float(n_dp))
        mine = source == me.astype(jnp.float32)
        ones = jnp.where(mine, 1.0, 0.0)
        earlier = jnp.where(
            lax.broadcasted_iota(jnp.int32, (max_pages, max_pages), 1)
            < lax.broadcasted_iota(jnp.int32, (max_pages, max_pages), 0),
            1.0,
            0.0,
        )
        in_group = jnp.where((down // req_dev == across // req_dev) & (down < across), 1.0, 0.0)
        count = jnp.broadcast_to(jnp.sum(ones, axis=0, keepdims=True), (8, n_req))
        rank = exact_dot(earlier, ones, ((1,), (0,))) + exact_dot(count, in_group, ((1,), (0,)))[:1]
        rank = jnp.where(mine, rank, -1.0)
        found = jnp.concatenate(
            [
                jnp.sum(jnp.where(rank == float(k), row, 0.0), axis=0, keepdims=True)
                for k in range(capacity)
            ],
            axis=0,
        ).astype(jnp.int32)
        group = jnp.where(down // req_dev == across, 1.0, 0.0)
        high_part = exact_dot((found // low).astype(jnp.float32), group, ((1,), (0,)))
        low_part = exact_dot((found % low).astype(jnp.float32), group, ((1,), (0,)))
        rows_vec[...] = (high_part * low + low_part).astype(jnp.int32)
        rows_copy = pltpu.make_async_copy(rows_vec, rows, rows_sem)
        rows_copy.start()
        own = jnp.where(down == me * req_dev + across % req_dev, 1.0, 0.0)
        ahead = jnp.concatenate([source, jnp.floor(len_row * (1.0 / low)), len_row - jnp.floor(len_row * (1.0 / low)) * low], axis=0)
        ahead = jnp.concatenate([ahead, jnp.zeros((6, n_req), jnp.float32)], axis=0)
        own_cols = exact_dot(ahead, own, ((1,), (0,)))
        lane = lax.broadcasted_iota(jnp.int32, (max_pages, n_req), 1)
        hit = own_cols[:max_pages] == (lane // req_dev).astype(jnp.float32)
        ones = jnp.where(hit, 1.0, 0.0)
        count = jnp.broadcast_to(jnp.sum(ones, axis=0, keepdims=True), (8, n_req))
        rank = exact_dot(earlier, ones, ((1,), (0,))) + exact_dot(count, in_group, ((1,), (0,)))[:1]
        spot = jnp.where(hit, rank + 1.0, 0.0)
        requests = jnp.where(down % req_dev == across, 1.0, 0.0)
        base = jnp.where(hit, (lane // req_dev).astype(jnp.float32), 0.0)
        pick = exact_dot(base, requests, ((1,), (0,))) * capacity
        pick += exact_dot(spot, requests, ((1,), (0,))) - 1.0
        own_len = own_cols[max_pages : max_pages + 1] * low + own_cols[max_pages + 1 : max_pages + 2]
        pick_ref[:max_pages] = jnp.maximum(pick, 0.0).astype(jnp.int32)
        pick_ref[max_pages:] = jnp.broadcast_to(own_len, (8, n_req)).astype(jnp.int32)
        rows_copy.wait()
        pool_copy.wait()
        first = pl.ds(0, up_hbm.shape[0] // 2)
        up_copy = pltpu.make_async_copy(up_hbm.at[first], up_ref.at[first], up_sem)
        up_copy.start()

        for d in range(n_dp):

            def move(k, carry):
                out_buf[d * capacity + k] = pool_buf[rows[k, d]]
                return carry

            lax.fori_loop(0, capacity, move, 0, unroll=16)
        up_copy.wait()

    return pl.pallas_call(
        kernel,
        in_specs=[SMEM, HBM, HBM, HBM, HBM, HBM],
        out_specs=[VMEM, VMEM, VMEM],
        out_shape=[
            jax.ShapeDtypeStruct(pool.shape, pool.dtype),
            jax.ShapeDtypeStruct((max_pages + 8, n_req), jnp.int32),
            pltpu.VMEM(up_rows.shape, up_rows.dtype),
        ],
        scratch_shapes=[
            pltpu.VMEM((max_pages, n_req), jnp.int32),
            pltpu.VMEM((1, n_req), jnp.int32),
            pltpu.VMEM((1, n_req), jnp.int32),
            pltpu.VMEM(pool.shape, pool.dtype),
            pltpu.VMEM((capacity, n_req), jnp.int32),
            pltpu.SMEM((capacity, n_req), jnp.int32),
            pltpu.SemaphoreType.DMA,
            pltpu.SemaphoreType.DMA,
            pltpu.SemaphoreType.DMA,
            pltpu.SemaphoreType.DMA,
            pltpu.SemaphoreType.DMA,
            pltpu.SemaphoreType.DMA,
        ],
        compiler_params=pltpu.CompilerParams(vmem_limit_bytes=20 * MIB),
        name="pack_pages",
    )(
        place,
        *[
            pltpu.with_memory_space_constraint(array, pltpu.HBM)
            for array in (page_loc, lengths, placement, pool, up_rows)
        ],
    )


def settle(parts, resid_own, resid_other, place, n_copies):
    n_parts, rows, cols = parts.shape
    n_steps, _, cols_dev = resid_own.shape
    req_dev = rows // n_steps

    def kernel(place_ref, parts_ref, own_ref, other_ref, out_ref):
        core = place_ref[3]
        both_rows = pl.ds(pl.multiple_of(place_ref[1] * 2 * req_dev, 2 * req_dev), 2 * req_dev)
        total = parts_ref[0].astype(jnp.float32)
        for i in range(1, n_parts):
            total += parts_ref[i].astype(jnp.float32)
        resid = []
        for ref in (own_ref, other_ref):
            steps = []
            for s in range(n_steps):
                wide = ref[s, both_rows, :].astype(jnp.float32)
                steps.append(jnp.where(core == 0, wide[:req_dev], wide[req_dev:]))
            resid.append(jnp.concatenate(steps, axis=0))
        left = jnp.where(core == 0, resid[0], resid[1])
        right = jnp.where(core == 0, resid[1], resid[0])
        hidden = (total + jnp.concatenate([left, right], axis=1)).astype(out_ref.dtype)
        for i in range(n_copies):
            out_ref[i] = hidden

    return pl.pallas_call(
        kernel,
        in_specs=[SMEM, VMEM, VMEM, VMEM],
        out_specs=VMEM,
        out_shape=jax.ShapeDtypeStruct((n_copies, rows, cols), parts.dtype),
        compiler_params=pltpu.CompilerParams(vmem_limit_bytes=10 * MIB),
        name="settle",
    )(place, parts, resid_own, resid_other)


def add_cores(ours, from_core):
    def kernel(a_ref, b_ref, out_ref):
        for i in range(ours.shape[0]):
            out_ref[i] = (a_ref[i].astype(jnp.float32) + b_ref[i].astype(jnp.float32)).astype(
                out_ref.dtype
            )

    return pl.pallas_call(
        kernel,
        in_specs=[VMEM, VMEM],
        out_specs=VMEM,
        out_shape=jax.ShapeDtypeStruct(ours.shape, ours.dtype),
        compiler_params=pltpu.CompilerParams(vmem_limit_bytes=12 * MIB),
        name="add_cores",
    )(ours, from_core)


def per_device(
    kv_pool,
    page_loc,
    lengths,
    placement,
    queries,
    new_kv,
    resid_in,
    w_out,
    ffn_gain,
    w_gate,
    w_up,
    w_down,
):
    n_dp = lax.axis_size(DP)
    n_tensor = lax.axis_size(TENSOR)
    dev_dp = lax.axis_index(DP)
    dev_chip = lax.axis_index(CHIP_DP)
    dev_tensor = lax.axis_index(TENSOR)
    core = lax.axis_index("c")
    pslots, _, page_size, width_two = kv_pool.shape
    head_dim = width_two // 2
    n_req = lengths.shape[0]
    req_dev = n_req // n_dp
    max_pages = page_loc.shape[2]
    max_len = max_pages * page_size
    cache_len = max_len + page_size
    n_steps = queries.shape[0]
    hq_dev = queries.shape[2]
    width = ffn_gain.shape[0]
    rows_dev = n_steps * req_dev
    chips_dp = n_dp // 2
    rows_core = n_steps * n_req // 2
    capacity = pslots // n_dp

    place = jnp.stack([dev_dp, dev_tensor, dev_chip, core]).astype(jnp.int32)
    up_rows = jnp.swapaxes(w_up, 0, 1)
    outgoing, pick, up_begun = pack_pages(
        place,
        jnp.swapaxes(page_loc, 1, 2),
        lengths.reshape(1, n_req),
        placement.reshape(1, n_req),
        kv_pool.reshape(pslots, page_size, width_two),
        up_rows,
        n_dp,
    )
    query = jnp.transpose(queries, (1, 0, 2, 3)).reshape(req_dev, n_steps * hq_dev, head_dim)
    fresh = new_kv.reshape(n_steps, req_dev, width_two)

    cols_dev = width // n_dp
    cols_chip = 2 * cols_dev
    swap = [(0, 1), (1, 0)]

    resid_other = lax.ppermute(resid_in, "c", swap)
    w_other = lax.ppermute(w_out, "c", swap)
    outgoing, pick, query, resid_other, w_other, place, first_core = lax.optimization_barrier(
        (outgoing, pick, query, resid_other, w_other, place, core == 0)
    )
    received = lax.all_to_all(
        outgoing.reshape(n_dp, capacity, page_size, width_two), DP, 0, 0, tiled=True
    )
    cache, mixed_copies, up_near = intake(
        pick,
        received.reshape(pslots, page_size, width_two),
        fresh,
        query,
        up_rows,
        up_begun,
        chips_dp,
    )

    w_both = jnp.where(
        first_core,
        jnp.concatenate([w_out, w_other], axis=-1),
        jnp.concatenate([w_other, w_out], axis=-1),
    )
    mixed_rows = lax.all_to_all(mixed_copies, CHIP_DP, 0, 0, tiled=True).reshape(
        rows_core, hq_dev * head_dim
    )
    partial_out = jnp.dot(mixed_rows, w_both, preferred_element_type=jnp.float32).astype(
        jnp.bfloat16
    )
    rows_blk = rows_core // n_tensor
    parts = lax.all_to_all(
        partial_out.reshape(n_tensor, rows_blk, cols_chip), TENSOR, 0, 0, tiled=True
    )
    hidden_copies = settle(parts, resid_in, resid_other, place, chips_dp * n_tensor)
    own_rows = lax.all_to_all(hidden_copies, CHIPS, 0, 0, tiled=True).reshape(
        chips_dp, rows_core, cols_chip
    )
    other_rows = lax.ppermute(own_rows, "c", swap)
    gate_rows = jnp.swapaxes(w_gate, 0, 1)
    gain_row = ffn_gain.reshape(1, width)
    width_out = width // n_tensor

    act_own, own_hidden = expand_own(own_rows, gate_rows, up_near, gain_row, place, rows_dev)
    other_rows, act_own = lax.optimization_barrier((other_rows, act_own))
    theirs, down_near = feed_forward(
        other_rows, gate_rows, up_near, gain_row, w_down, n_tensor, rows_dev
    )
    from_core = lax.ppermute(theirs, "c", swap)
    ours = shrink_own(act_own, down_near, n_tensor, rows_dev)
    chip_sum = add_cores(ours, from_core).reshape(chips_dp * n_tensor, rows_dev, width_out)
    pieces = lax.all_to_all(chip_sum, TENSOR + CHIP_DP, 0, 0, tiled=True)
    block_out = add_pieces(pieces, own_hidden, n_steps)
    return (block_out, cache.reshape(1, req_dev, cache_len, width_two))


def solution(mesh):
    fine = Mesh(mesh.devices.reshape(2, 4, 2, 4, 2), ("yh", "x", "c", "z", "yl"))
    placed = (
        P(DP, TENSOR, None, None),
        P(),
        P(),
        P(),
        P(None, DP, TENSOR, None),
        P(None, DP, TENSOR, None),
        P(None, None, DP),
        P(TENSOR, DP),
        P(),
        P(None, DP + TENSOR),
        P(None, DP + TENSOR),
        P(DP + TENSOR, None),
    )
    return jax.shard_map(
        per_device,
        mesh=fine,
        in_specs=placed,
        out_specs=(P(None, DP, TENSOR), P(TENSOR, DP, None, None)),
        check_vma=False,
    )
```

```python
import math

import jax
import jax.numpy as jnp
from jax import lax
from jax.experimental import pallas as pl
from jax.experimental.pallas import tpu as pltpu
from jax.sharding import Mesh, PartitionSpec as P

DP = ("yh", "x", "c")
CHIP_DP = ("yh", "x")
TENSOR = ("z", "yl")
CHIPS = ("yh", "x", "z", "yl")
MIB = 1024 * 1024
SMEM = pl.BlockSpec(memory_space=pltpu.SMEM)
VMEM = pl.BlockSpec(memory_space=pltpu.VMEM)
HBM = pl.BlockSpec(memory_space=pltpu.HBM)


def intake(pick, received, fresh, query, up_rows, n_copies):
    req_dev, n_rows, head_dim = query.shape
    n_steps = fresh.shape[0]
    _, page_size, width_two = received.shape
    max_pages = pick.shape[0] - 8
    pages = max_pages + 1
    group = n_rows // n_steps
    scale = 1.0 / math.sqrt(head_dim)

    def kernel(pick_ref, recv_ref, fresh_ref, q_ref, up_hbm, cache_ref, mixed_ref, up_ref, buf, scores, probs, heads, out_sems, up_sem):
        def copy_out(r):
            return pltpu.make_async_copy(buf.at[r], cache_ref.at[r], out_sems.at[r])

        up_copy = pltpu.make_async_copy(up_hbm, up_ref, up_sem)
        up_copy.start()
        row_at = lax.broadcasted_iota(jnp.int32, (page_size, width_two), 0)
        tokens_new = [fresh_ref[s].astype(jnp.float32) for s in range(n_steps)]
        for r in range(req_dev):

            def move(p, carry):
                buf[r, p] = recv_ref[pick_ref[p, r]]
                return carry

            lax.fori_loop(0, max_pages, move, 0, unroll=16)
            length = pick_ref[max_pages, r]
            full = length // page_size

            def clear(p, carry):
                buf[r, p] = jnp.zeros((page_size, width_two), buf.dtype)
                return carry

            lax.fori_loop(full + 1, pages, clear, 0)
            edge = buf[r, full].astype(jnp.float32)
            buf[r, full] = jnp.where(row_at < length % page_size, edge, 0.0).astype(buf.dtype)
            for s in range(n_steps):
                at = length + s
                page = buf[r, at // page_size].astype(jnp.float32)
                token = tokens_new[s][r : r + 1]
                buf[r, at // page_size] = jnp.where(
                    row_at == at % page_size, token, page
                ).astype(buf.dtype)
            copy_out(r).start()
        for r in range(req_dev):
            keys = buf[r, :, :, :head_dim].reshape(pages * page_size, head_dim)
            part = scale * lax.dot_general(
                q_ref[r], keys, (((1,), (1,)), ((), ())), preferred_element_type=jnp.float32
            )
            last = pick_ref[max_pages, r] + lax.broadcasted_iota(jnp.int32, part.shape, 0) // group
            scores[r * n_rows : (r + 1) * n_rows] = jnp.where(
                lax.broadcasted_iota(jnp.int32, part.shape, 1) <= last, part, -jnp.inf
            )
        expo = jnp.exp(scores[...] - jnp.max(scores[...], axis=1, keepdims=True))
        probs[...] = (expo / jnp.sum(expo, axis=1, keepdims=True)).astype(probs.dtype)
        for r in range(req_dev):
            values = buf[r, :, :, head_dim:].reshape(pages * page_size, head_dim)
            head_out = jnp.dot(
                probs[r * n_rows : (r + 1) * n_rows], values, preferred_element_type=jnp.float32
            )
            for i in range(n_rows):
                heads[i, r : r + 1, :] = head_out[i : i + 1, :]
        for g in range(group):
            block = jnp.concatenate([heads[s * group + g] for s in range(n_steps)], axis=0)
            block = block.astype(mixed_ref.dtype)
            for k in range(n_copies):
                mixed_ref[k, :, g * head_dim : (g + 1) * head_dim] = block
        for r in range(req_dev):
            copy_out(r).wait()
        up_copy.wait()

    return pl.pallas_call(
        kernel,
        in_specs=[SMEM, VMEM, VMEM, VMEM, HBM],
        out_specs=[HBM, VMEM, VMEM],
        out_shape=[
            jax.ShapeDtypeStruct((req_dev, pages, page_size, width_two), received.dtype),
            jax.ShapeDtypeStruct(
                (n_copies, n_steps * req_dev, group * head_dim), received.dtype
            ),
            pltpu.VMEM(up_rows.shape, up_rows.dtype),
        ],
        scratch_shapes=[
            pltpu.VMEM((req_dev, pages, page_size, width_two), received.dtype),
            pltpu.VMEM((req_dev * n_rows, pages * page_size), jnp.float32),
            pltpu.VMEM((req_dev * n_rows, pages * page_size), jnp.bfloat16),
            pltpu.VMEM((n_rows, req_dev, head_dim), jnp.float32),
            pltpu.SemaphoreType.DMA((req_dev,)),
            pltpu.SemaphoreType.DMA,
        ],
        compiler_params=pltpu.CompilerParams(vmem_limit_bytes=20 * MIB),
        name="intake",
    )(pick, received, fresh, query, pltpu.with_memory_space_constraint(up_rows, pltpu.HBM))


NT = (((1,), (1,)), ((), ()))


def scale_rows(x_ref, gain_ref, scaled):
    blocks, _, cols = x_ref.shape
    squares = 0.0
    for i in range(blocks):
        wide = x_ref[i].astype(jnp.float32)
        square = wide * wide
        squares += sum(square[:, k * 128 : (k + 1) * 128] for k in range(cols // 128))
        scaled[:, i * cols : (i + 1) * cols] = (
            wide * gain_ref[:, i * cols : (i + 1) * cols]
        ).astype(scaled.dtype)
    mean = jnp.sum(squares, axis=1, keepdims=True) * (1.0 / (blocks * cols))
    return lax.rsqrt(mean + 1e-05)


def activate(gate, upper):
    return (gate / (1.0 + jnp.exp(-gate)) * upper).astype(jnp.bfloat16)


def down_to(out_ref, act, down_ref):
    chips, n_tensor, rows_dev, cols_out = out_ref.shape
    for t in range(n_tensor):
        out = jnp.dot(
            act,
            down_ref[:, t * cols_out : (t + 1) * cols_out],
            preferred_element_type=jnp.float32,
        )
        out_ref[:, t] = out.astype(out_ref.dtype).reshape(chips, rows_dev, cols_out)


def expand_own(hidden, gate_rows, up_rows, gain_row, place, rows_dev):
    _, rows, cols = hidden.shape
    units, width = up_rows.shape

    def kernel(place_ref, x_ref, gate_ref, up_ref, gain_ref, act_ref, part_ref, scaled):
        mine = pl.ds(pl.multiple_of(place_ref[2] * rows_dev, rows_dev), rows_dev)
        part_ref[...] = x_ref[place_ref[1], mine, :]
        inverse = scale_rows(x_ref, gain_ref, scaled)
        gate = lax.dot_general(scaled[...], gate_ref[...], NT, preferred_element_type=jnp.float32)
        upper = lax.dot_general(scaled[...], up_ref[...], NT, preferred_element_type=jnp.float32)
        act_ref[...] = activate(gate * inverse, upper * inverse)

    return pl.pallas_call(
        kernel,
        in_specs=[SMEM, VMEM, VMEM, VMEM, VMEM],
        out_specs=[VMEM] * 2,
        out_shape=[
            pltpu.VMEM((rows, units), jnp.bfloat16),
            jax.ShapeDtypeStruct((rows_dev, cols), hidden.dtype),
        ],
        scratch_shapes=[pltpu.VMEM((rows, width), jnp.bfloat16)],
        compiler_params=pltpu.CompilerParams(vmem_limit_bytes=24 * MIB),
        name="expand_own",
    )(place, hidden, gate_rows, up_rows, gain_row)


def feed_forward(hidden, gate_rows, up_rows, gain_row, w_down, n_tensor, rows_dev):
    _, rows, _ = hidden.shape
    units, width = w_down.shape

    def kernel(x_ref, gate_ref, up_ref, gain_ref, down_hbm, out_ref, down_ref, scaled, sem):
        down_copy = pltpu.make_async_copy(down_hbm, down_ref, sem)
        down_copy.start()
        inverse = scale_rows(x_ref, gain_ref, scaled)
        gate = lax.dot_general(scaled[...], gate_ref[...], NT, preferred_element_type=jnp.float32)
        upper = lax.dot_general(scaled[...], up_ref[...], NT, preferred_element_type=jnp.float32)
        act = activate(gate * inverse, upper * inverse)
        down_copy.wait()
        down_to(out_ref, act, down_ref)

    return pl.pallas_call(
        kernel,
        in_specs=[VMEM, VMEM, VMEM, VMEM, HBM],
        out_specs=[VMEM] * 2,
        out_shape=[
            jax.ShapeDtypeStruct(
                (rows // rows_dev, n_tensor, rows_dev, width // n_tensor), jnp.bfloat16
            ),
            pltpu.VMEM((units, width), jnp.bfloat16),
        ],
        scratch_shapes=[
            pltpu.VMEM((rows, width), jnp.bfloat16),
            pltpu.SemaphoreType.DMA,
        ],
        compiler_params=pltpu.CompilerParams(vmem_limit_bytes=28 * MIB),
        name="feed_forward",
    )(hidden, gate_rows, up_rows, gain_row, pltpu.with_memory_space_constraint(w_down, pltpu.HBM))


def shrink_own(act, w_down, n_tensor, rows_dev):
    def kernel(act_ref, down_ref, out_ref):
        down_to(out_ref, act_ref[...], down_ref)

    return pl.pallas_call(
        kernel,
        in_specs=[VMEM, VMEM],
        out_specs=VMEM,
        out_shape=jax.ShapeDtypeStruct(
            (act.shape[0] // rows_dev, n_tensor, rows_dev, w_down.shape[1] // n_tensor),
            jnp.bfloat16,
        ),
        compiler_params=pltpu.CompilerParams(vmem_limit_bytes=16 * MIB),
        name="shrink_own",
    )(act, w_down)


def add_pieces(pieces, hidden, n_steps):
    count, rows, cols = pieces.shape

    def kernel(pieces_ref, hidden_ref, out_ref):
        total = hidden_ref[...].astype(jnp.float32)
        for i in range(count):
            total += pieces_ref[i].astype(jnp.float32)
        out_ref[...] = total.reshape(n_steps, rows // n_steps, cols).astype(out_ref.dtype)

    return pl.pallas_call(
        kernel,
        in_specs=[VMEM, VMEM],
        out_specs=VMEM,
        out_shape=jax.ShapeDtypeStruct((n_steps, rows // n_steps, cols), pieces.dtype),
        compiler_params=pltpu.CompilerParams(vmem_limit_bytes=10 * MIB),
        name="add_pieces",
    )(pieces, hidden)


def exact_dot(left, right, contract):
    return lax.dot_general(
        left.astype(jnp.bfloat16),
        right.astype(jnp.bfloat16),
        (contract, ((), ())),
        preferred_element_type=jnp.float32,
    )


def pack_pages(place, page_loc, lengths, placement, pool, n_dp):
    pslots, page_size, width_two = pool.shape
    _, max_pages, n_req = page_loc.shape
    req_dev = n_req // n_dp
    capacity = pslots // n_dp
    low = 32

    def kernel(place_ref, loc_hbm, len_hbm, placement_hbm, pool_hbm, out_buf, pick_ref, loc, len_ref, placement_ref, pool_buf, rows_vec, rows, loc_sem, len_sem, placement_sem, pool_sem, rows_sem):
        me = place_ref[0]
        len_copy = pltpu.make_async_copy(len_hbm, len_ref, len_sem)
        placement_copy = pltpu.make_async_copy(placement_hbm, placement_ref, placement_sem)
        pool_copy = pltpu.make_async_copy(pool_hbm, pool_buf, pool_sem)
        loc_copy = pltpu.make_async_copy(loc_hbm.at[place_ref[1]], loc, loc_sem)
        loc_copy.start()
        len_copy.start()
        placement_copy.start()
        pool_copy.start()
        shape = (n_req, n_req)
        down = lax.broadcasted_iota(jnp.int32, shape, 0)
        across = lax.broadcasted_iota(jnp.int32, shape, 1)
        placement_copy.wait()
        slot_hot = jnp.where(placement_ref[...] == down, 1.0, 0.0)
        len_copy.wait()
        lens = jnp.broadcast_to(len_ref[...], (8, n_req))
        loc_copy.wait()
        at = loc[...]
        pieces = jnp.concatenate(
            [at // pslots, at % pslots // low, at % low, lens // low, lens % low], axis=0
        )
        by_slot = exact_dot(pieces.astype(jnp.float32), slot_hot, ((1,), (1,)))
        source = by_slot[:max_pages]
        row = by_slot[max_pages : 2 * max_pages] * low + by_slot[2 * max_pages : 3 * max_pages]
        len_row = by_slot[3 * max_pages : 3 * max_pages + 1] * low + by_slot[3 * max_pages + 8 : 3 * max_pages + 9]
        page_at = lax.broadcasted_iota(jnp.int32, (max_pages, n_req), 0).astype(jnp.float32)
        source = jnp.where(page_at * page_size < len_row, source, float(n_dp))
        mine = source == me.astype(jnp.float32)
        ones = jnp.where(mine, 1.0, 0.0)
        earlier = jnp.where(
            lax.broadcasted_iota(jnp.int32, (max_pages, max_pages), 1)
            < lax.broadcasted_iota(jnp.int32, (max_pages, max_pages), 0),
            1.0,
            0.0,
        )
        in_group = jnp.where((down // req_dev == across // req_dev) & (down < across), 1.0, 0.0)
        count = jnp.broadcast_to(jnp.sum(ones, axis=0, keepdims=True), (8, n_req))
        rank = exact_dot(earlier, ones, ((1,), (0,))) + exact_dot(count, in_group, ((1,), (0,)))[:1]
        rank = jnp.where(mine, rank, -1.0)
        found = jnp.concatenate(
            [
                jnp.sum(jnp.where(rank == float(k), row, 0.0), axis=0, keepdims=True)
                for k in range(capacity)
            ],
            axis=0,
        ).astype(jnp.int32)
        group = jnp.where(down // req_dev == across, 1.0, 0.0)
        high_part = exact_dot((found // low).astype(jnp.float32), group, ((1,), (0,)))
        low_part = exact_dot((found % low).astype(jnp.float32), group, ((1,), (0,)))
        rows_vec[...] = (high_part * low + low_part).astype(jnp.int32)
        rows_copy = pltpu.make_async_copy(rows_vec, rows, rows_sem)
        rows_copy.start()
        own = jnp.where(down == me * req_dev + across % req_dev, 1.0, 0.0)
        ahead = jnp.concatenate([source, jnp.floor(len_row * (1.0 / low)), len_row - jnp.floor(len_row * (1.0 / low)) * low], axis=0)
        ahead = jnp.concatenate([ahead, jnp.zeros((6, n_req), jnp.float32)], axis=0)
        own_cols = exact_dot(ahead, own, ((1,), (0,)))
        lane = lax.broadcasted_iota(jnp.int32, (max_pages, n_req), 1)
        hit = own_cols[:max_pages] == (lane // req_dev).astype(jnp.float32)
        ones = jnp.where(hit, 1.0, 0.0)
        count = jnp.broadcast_to(jnp.sum(ones, axis=0, keepdims=True), (8, n_req))
        rank = exact_dot(earlier, ones, ((1,), (0,))) + exact_dot(count, in_group, ((1,), (0,)))[:1]
        spot = jnp.where(hit, rank + 1.0, 0.0)
        requests = jnp.where(down % req_dev == across, 1.0, 0.0)
        base = jnp.where(hit, (lane // req_dev).astype(jnp.float32), 0.0)
        pick = exact_dot(base, requests, ((1,), (0,))) * capacity
        pick += exact_dot(spot, requests, ((1,), (0,))) - 1.0
        own_len = own_cols[max_pages : max_pages + 1] * low + own_cols[max_pages + 1 : max_pages + 2]
        pick_ref[:max_pages] = jnp.maximum(pick, 0.0).astype(jnp.int32)
        pick_ref[max_pages:] = jnp.broadcast_to(own_len, (8, n_req)).astype(jnp.int32)
        rows_copy.wait()
        pool_copy.wait()

        for d in range(n_dp):

            def move(k, carry):
                out_buf[d * capacity + k] = pool_buf[rows[k, d]]
                return carry

            lax.fori_loop(0, capacity, move, 0, unroll=16)

    return pl.pallas_call(
        kernel,
        in_specs=[SMEM, HBM, HBM, HBM, HBM],
        out_specs=[VMEM, VMEM],
        out_shape=[
            jax.ShapeDtypeStruct(pool.shape, pool.dtype),
            jax.ShapeDtypeStruct((max_pages + 8, n_req), jnp.int32),
        ],
        scratch_shapes=[
            pltpu.VMEM((max_pages, n_req), jnp.int32),
            pltpu.VMEM((1, n_req), jnp.int32),
            pltpu.VMEM((1, n_req), jnp.int32),
            pltpu.VMEM(pool.shape, pool.dtype),
            pltpu.VMEM((capacity, n_req), jnp.int32),
            pltpu.SMEM((capacity, n_req), jnp.int32),
            pltpu.SemaphoreType.DMA,
            pltpu.SemaphoreType.DMA,
            pltpu.SemaphoreType.DMA,
            pltpu.SemaphoreType.DMA,
            pltpu.SemaphoreType.DMA,
        ],
        compiler_params=pltpu.CompilerParams(vmem_limit_bytes=20 * MIB),
        name="pack_pages",
    )(
        place,
        *[
            pltpu.with_memory_space_constraint(array, pltpu.HBM)
            for array in (page_loc, lengths, placement, pool)
        ],
    )


def settle(parts, resid_own, resid_other, place, n_copies):
    n_parts, rows, cols = parts.shape
    n_steps, _, cols_dev = resid_own.shape
    req_dev = rows // n_steps

    def kernel(place_ref, parts_ref, own_ref, other_ref, out_ref):
        core = place_ref[3]
        both_rows = pl.ds(pl.multiple_of(place_ref[1] * 2 * req_dev, 2 * req_dev), 2 * req_dev)
        total = parts_ref[0].astype(jnp.float32)
        for i in range(1, n_parts):
            total += parts_ref[i].astype(jnp.float32)
        resid = []
        for ref in (own_ref, other_ref):
            steps = []
            for s in range(n_steps):
                wide = ref[s, both_rows, :].astype(jnp.float32)
                steps.append(jnp.where(core == 0, wide[:req_dev], wide[req_dev:]))
            resid.append(jnp.concatenate(steps, axis=0))
        left = jnp.where(core == 0, resid[0], resid[1])
        right = jnp.where(core == 0, resid[1], resid[0])
        hidden = (total + jnp.concatenate([left, right], axis=1)).astype(out_ref.dtype)
        for i in range(n_copies):
            out_ref[i] = hidden

    return pl.pallas_call(
        kernel,
        in_specs=[SMEM, VMEM, VMEM, VMEM],
        out_specs=VMEM,
        out_shape=jax.ShapeDtypeStruct((n_copies, rows, cols), parts.dtype),
        compiler_params=pltpu.CompilerParams(vmem_limit_bytes=10 * MIB),
        name="settle",
    )(place, parts, resid_own, resid_other)


def add_cores(ours, from_core):
    def kernel(a_ref, b_ref, out_ref):
        for i in range(ours.shape[0]):
            out_ref[i] = (a_ref[i].astype(jnp.float32) + b_ref[i].astype(jnp.float32)).astype(
                out_ref.dtype
            )

    return pl.pallas_call(
        kernel,
        in_specs=[VMEM, VMEM],
        out_specs=VMEM,
        out_shape=jax.ShapeDtypeStruct(ours.shape, ours.dtype),
        compiler_params=pltpu.CompilerParams(vmem_limit_bytes=12 * MIB),
        name="add_cores",
    )(ours, from_core)


def per_device(
    kv_pool,
    page_loc,
    lengths,
    placement,
    queries,
    new_kv,
    resid_in,
    w_out,
    ffn_gain,
    w_gate,
    w_up,
    w_down,
):
    n_dp = lax.axis_size(DP)
    n_tensor = lax.axis_size(TENSOR)
    dev_dp = lax.axis_index(DP)
    dev_chip = lax.axis_index(CHIP_DP)
    dev_tensor = lax.axis_index(TENSOR)
    core = lax.axis_index("c")
    pslots, _, page_size, width_two = kv_pool.shape
    head_dim = width_two // 2
    n_req = lengths.shape[0]
    req_dev = n_req // n_dp
    max_pages = page_loc.shape[2]
    max_len = max_pages * page_size
    cache_len = max_len + page_size
    n_steps = queries.shape[0]
    hq_dev = queries.shape[2]
    width = ffn_gain.shape[0]
    rows_dev = n_steps * req_dev
    chips_dp = n_dp // 2
    rows_core = n_steps * n_req // 2
    capacity = pslots // n_dp

    place = jnp.stack([dev_dp, dev_tensor, dev_chip, core]).astype(jnp.int32)
    outgoing, pick = pack_pages(
        place,
        jnp.swapaxes(page_loc, 1, 2),
        lengths.reshape(1, n_req),
        placement.reshape(1, n_req),
        kv_pool.reshape(pslots, page_size, width_two),
        n_dp,
    )
    query = jnp.transpose(queries, (1, 0, 2, 3)).reshape(req_dev, n_steps * hq_dev, head_dim)
    fresh = new_kv.reshape(n_steps, req_dev, width_two)

    cols_dev = width // n_dp
    cols_chip = 2 * cols_dev
    swap = [(0, 1), (1, 0)]

    resid_other = lax.ppermute(resid_in, "c", swap)
    w_other = lax.ppermute(w_out, "c", swap)
    outgoing, pick, query, resid_other, w_other, place, first_core = lax.optimization_barrier(
        (outgoing, pick, query, resid_other, w_other, place, core == 0)
    )
    received = lax.all_to_all(
        outgoing.reshape(n_dp, capacity, page_size, width_two), DP, 0, 0, tiled=True
    )
    cache, mixed_copies, up_near = intake(
        pick,
        received.reshape(pslots, page_size, width_two),
        fresh,
        query,
        jnp.swapaxes(w_up, 0, 1),
        chips_dp,
    )

    w_both = jnp.where(
        first_core,
        jnp.concatenate([w_out, w_other], axis=-1),
        jnp.concatenate([w_other, w_out], axis=-1),
    )
    mixed_rows = lax.all_to_all(mixed_copies, CHIP_DP, 0, 0, tiled=True).reshape(
        rows_core, hq_dev * head_dim
    )
    partial_out = jnp.dot(mixed_rows, w_both, preferred_element_type=jnp.float32).astype(
        jnp.bfloat16
    )
    rows_blk = rows_core // n_tensor
    parts = lax.all_to_all(
        partial_out.reshape(n_tensor, rows_blk, cols_chip), TENSOR, 0, 0, tiled=True
    )
    hidden_copies = settle(parts, resid_in, resid_other, place, chips_dp * n_tensor)
    own_rows = lax.all_to_all(hidden_copies, CHIPS, 0, 0, tiled=True).reshape(
        chips_dp, rows_core, cols_chip
    )
    other_rows = lax.ppermute(own_rows, "c", swap)
    gate_rows = jnp.swapaxes(w_gate, 0, 1)
    gain_row = ffn_gain.reshape(1, width)
    width_out = width // n_tensor

    act_own, own_hidden = expand_own(own_rows, gate_rows, up_near, gain_row, place, rows_dev)
    other_rows, act_own = lax.optimization_barrier((other_rows, act_own))
    theirs, down_near = feed_forward(
        other_rows, gate_rows, up_near, gain_row, w_down, n_tensor, rows_dev
    )
    from_core = lax.ppermute(theirs, "c", swap)
    ours = shrink_own(act_own, down_near, n_tensor, rows_dev)
    chip_sum = add_cores(ours, from_core).reshape(chips_dp * n_tensor, rows_dev, width_out)
    pieces = lax.all_to_all(chip_sum, CHIPS, 0, 0, tiled=True)
    block_out = add_pieces(pieces, own_hidden, n_steps)
    return (block_out, cache.reshape(1, req_dev, cache_len, width_two))


def solution(mesh):
    fine = Mesh(mesh.devices.reshape(2, 4, 2, 4, 2), ("yh", "x", "c", "z", "yl"))
    placed = (
        P(DP, TENSOR, None, None),
        P(),
        P(),
        P(),
        P(None, DP, TENSOR, None),
        P(None, DP, TENSOR, None),
        P(None, None, DP),
        P(TENSOR, DP),
        P(),
        P(None, DP + TENSOR),
        P(None, DP + TENSOR),
        P(DP + TENSOR, None),
    )
    return jax.shard_map(
        per_device,
        mesh=fine,
        in_specs=placed,
        out_specs=(P(None, DP, TENSOR), P(TENSOR, DP, None, None)),
        check_vma=False,
    )
```
